32 devices in a mesh: ctx: 8 (over y, x, core), exp: 4 (over z).
Axes of the slice: x: 2, y: 2, z: 4, core: 2. Of those that a mesh axis runs over, the one named last changes fastest.
Arguments:
- tokens: bfloat16 [4, 4096, 1024], P(None, ('ctx', 'exp')), may hold values from -6 to 6
- doc_lengths: int32 [4, 8], replicated, may hold values from 0 to 4096, as said below
- routes: int32 [4, 4096, 2], P(None, ('ctx', 'exp')), may hold values from 0 to 3, all different within a row
- priority: int32 [4, 4096], P(None, ('ctx', 'exp')), may hold values from 0 to 511, as said below
- norm1_gain: bfloat16 [1024], replicated, may hold values from 0.099609375 to 1.8984375
- w_query: bfloat16 [1024, 1024], replicated, may hold values from -0.1875 to 0.1875
- w_key: bfloat16 [1024, 1024], replicated, may hold values from -0.1875 to 0.1875
- w_value: bfloat16 [1024, 1024], replicated, may hold values from -0.1875 to 0.1875
- w_out: bfloat16 [1024, 1024], replicated, may hold values from -1.5 to 1.5
- bias_table: bfloat16 [512], replicated, may hold values from -4 to 4
- norm2_gain: bfloat16 [1024], replicated, may hold values from 0.099609375 to 1.8984375
- w_router: bfloat16 [1024, 4], replicated, may hold values from -0.125 to 0.125
- w_gate: bfloat16 [4, 1024, 2816], P('exp'), may hold values from -0.1875 to 0.1875
- w_up: bfloat16 [4, 1024, 2816], P('exp'), may hold values from -0.1875 to 0.1875
- w_down: bfloat16 [4, 2816, 1024], P('exp'), may hold values from -0.3125 to 0.3125
- cotangent: bfloat16 [4, 4096, 1024], P(None, ('ctx', 'exp')), may hold values from -6 to 6
Outputs:
- mixed: bfloat16 [4, 4096, 1024], P(None, ('ctx', 'exp'))
- grad_tokens: bfloat16 [4, 4096, 1024], P(None, ('ctx', 'exp'))
- grad_norm1: float32 [1024], P(('ctx', 'exp'))
- grad_query: float32 [1024, 1024], P(('ctx', 'exp'))
- grad_key: float32 [1024, 1024], P(('ctx', 'exp'))
- grad_value: float32 [1024, 1024], P(('ctx', 'exp'))
- grad_out: float32 [1024, 1024], P(('ctx', 'exp'))
- grad_table: float32 [512], P(('ctx', 'exp'))
- grad_norm2: float32 [1024], P(('ctx', 'exp'))
- grad_router: float32 [1024, 4], P(('ctx', 'exp'))
- grad_gate: float32 [4, 1024, 2816], P('exp', 'ctx')
- grad_up: float32 [4, 1024, 2816], P('exp', 'ctx')
- grad_down: float32 [4, 2816, 1024], P('exp', 'ctx')
The draws below stay inside these ranges and needn't reach their ends.
Inputs may be any that keep to these rules, and one draw needn't show every extreme that they name: `doc_lengths`: the lengths of each sequence sum to 4096; trailing lengths may be zero; one sequence, chosen by the seed, is a single document. `priority`: within each group of positions g * 128 to (g + 1) * 128 - 1 of all sequences, every value appears exactly once. `routes`: the two experts of a position differ.
All inputs are finite; a program needn't handle non-finite values.
Results may differ from the reference program's by a relative error of at most 0.02.
Values may be sent and summed in bfloat16 or wider, within the bound.
No kernel may reach another device: no remote copies, remote signals or barrier semaphores. Data moves between devices by JAX's collectives and lax.ppermute only.
A program may use at most 320 MiB of HBM per device.

```python
from functools import partial
import jax
import jax.numpy as jnp
import numpy as np
from jax import lax

D = 1024
HEADS = 16
HEAD_DIM = 64
FF = 2816
BUCKETS = 32
WINDOW = 1024
PIECE = 128
DOCS = 8
SEQS = 4
LENGTH = 4096
EXPERTS = 4
SLOT = 320
N_EXP = 4


def draw_doc_lengths(key, part):
    key = jax.random.fold_in(key, 11)
    cut_key, which_key = jax.random.split(key, 2)
    cuts = jnp.sort(jax.random.randint(cut_key, (SEQS, DOCS - 1), 1, LENGTH), axis=1).astype(jnp.int32)
    edges = jnp.concatenate([jnp.zeros((SEQS, 1), jnp.int32), cuts, jnp.full((SEQS, 1), LENGTH, jnp.int32)], axis=1)
    lengths = edges[:, 1:] - edges[:, :-1]
    chosen = jax.random.randint(which_key, (), 0, SEQS)
    single = jnp.zeros((DOCS,), jnp.int32).at[0].set(LENGTH)
    rows_index = jnp.arange(SEQS)[:, None]
    return jnp.where(rows_index == chosen, single[None, :], lengths).astype(jnp.int32)


def draw_priority(key, part):
    key = jax.random.fold_in(key, 23)
    groups = LENGTH // PIECE
    keys = jax.random.split(key, groups)
    orders = jax.vmap(lambda one_key: jax.random.permutation(one_key, SEQS * PIECE))(keys)
    orders = orders.reshape(groups, SEQS, PIECE).transpose(1, 0, 2).reshape(SEQS, LENGTH)
    return orders.astype(jnp.int32)


def level_of(rng, shape, pieces, low, largest):
    loudness = 1.0
    for position, blocks in pieces:
        heights = jax.random.uniform(jax.random.fold_in(jax.random.fold_in(rng, 6), position), (blocks,), jnp.float32, low / len(pieces), largest / len(pieces))
        loudness = loudness * jnp.repeat(jnp.exp(heights), shape[position] // blocks).reshape((-1,) + (1,) * (len(shape) - 1 - position))
    return loudness


def picks_of(key, rows, amount, top, lift):
    sequence = jax.random.permutation(jax.random.fold_in(key, 1), amount)
    pull = sequence
    for power in range(3):
        pull = pull * pull // amount
    pull = pull * lift // amount
    chance = jax.random.randint(jax.random.fold_in(key, 2), (rows, amount), 0, 4096) + pull
    sure = jax.random.permutation(jax.random.fold_in(key, 3), rows)[jnp.arange(amount) % rows]
    chance = jnp.where(jnp.arange(rows)[:, None] == sure[None, :], 1 << 14, chance)
    merit = chance * amount + jnp.arange(amount)
    return lax.top_k(merit.astype(jnp.int32), top)[1].astype(jnp.int32)


def bell_draw(own_key, dims, deviation, reach, cuts=(), held_as=jnp.bfloat16):
    drawn = jax.random.normal(own_key, dims, jnp.float32) * deviation
    if len(cuts) > 0:
        drawn = level_of(own_key, dims, cuts, -0.22, 0.18) * drawn
    return jnp.clip(drawn, min=-reach, max=reach).astype(held_as)


def setup_inputs(seed: int = 0) -> dict:
    streams_of = jax.random.split(jax.random.key(seed), 17)
    return {
        "tokens": bell_draw(streams_of[0], (SEQS, LENGTH, D), 1.0, 6.0, ((1, 32),)),
        "doc_lengths": draw_doc_lengths(jax.random.fold_in(streams_of[16], 71), 0),
        "routes": picks_of(streams_of[2], SEQS * LENGTH, EXPERTS, 2, 8192).reshape((SEQS, LENGTH, 2)),
        "priority": draw_priority(jax.random.fold_in(streams_of[16], 71), 0),
        "norm1_gain": jnp.clip(1.0 + 0.18 * jax.random.normal(streams_of[4], (D,), jnp.float32), 0.099609375, 1.8984375).astype(jnp.bfloat16),
        "w_query": bell_draw(streams_of[5], (D, D), D ** -0.5, 0.1875),
        "w_key": bell_draw(streams_of[6], (D, D), D ** -0.5, 0.1875),
        "w_value": bell_draw(streams_of[7], (D, D), D ** -0.5, 0.1875),
        "w_out": bell_draw(streams_of[8], (D, D), (D // 64) ** -0.5, 1.5),
        "bias_table": bell_draw(streams_of[9], (HEADS * BUCKETS,), 1.0, 4.0),
        "norm2_gain": jnp.clip(1.0 + 0.18 * jax.random.normal(streams_of[10], (D,), jnp.float32), 0.099609375, 1.8984375).astype(jnp.bfloat16),
        "w_router": bell_draw(streams_of[11], (D, EXPERTS), (2 * D) ** -0.5, 0.125),
        "w_gate": bell_draw(streams_of[12], (EXPERTS, D, FF), D ** -0.5, 0.1875, ((0, 4),)),
        "w_up": bell_draw(streams_of[13], (EXPERTS, D, FF), D ** -0.5, 0.1875, ((0, 4),)),
        "w_down": bell_draw(streams_of[14], (EXPERTS, FF, D), (FF // 8) ** -0.5, 0.3125, ((0, 4),)),
        "cotangent": bell_draw(streams_of[15], (SEQS, LENGTH, D), 1.0, 6.0, ((1, 32),)),
    }


epsilon = 1e-06

@jax.custom_vjp
def low(v):
    return lax.optimization_barrier(v.astype(jnp.bfloat16)).astype(jnp.float32)

@jax.custom_vjp
def low_back(v):
    return v

def low_keep(v):
    return (low(v), None)

def low_pass(kept, grad):
    return (grad,)

def back_keep(v):
    return (v, None)

def back_low(kept, grad):
    return (low(grad),)
low.defvjp(low_keep, low_pass)
low_back.defvjp(back_keep, back_low)

def matmul(left, right):
    return jnp.dot(left, right, precision=lax.Precision.HIGHEST, preferred_element_type=jnp.float32)

def bucket_of(distance):
    limits = np.ceil(16.0 * 8.0 ** (np.arange(1, 16) / 16.0)).astype(np.int32)
    above = lax.optimization_barrier(jnp.sum((distance[..., None] >= jnp.asarray(limits)).astype(jnp.int32), axis=-1))
    return jnp.where(distance < 16, distance, 16 + above).astype(jnp.int32)

def norm_rows(values, gain):
    return values * lax.rsqrt(lax.optimization_barrier(jnp.mean(values * values, axis=-1, keepdims=True)) + epsilon) * gain

def group_places(route_rows, priority_rows, experts):
    count = priority_rows.shape[0]
    inverse = jnp.zeros((count,), jnp.int32).at[priority_rows].set(jnp.arange(count, dtype=jnp.int32))
    ordered = jnp.concatenate([route_rows[inverse, 0], route_rows[inverse, 1]])
    onehot = (ordered[:, None] == jnp.arange(experts, dtype=jnp.int32)[None, :]).astype(jnp.int32)
    earlier = jnp.cumsum(onehot, axis=0) - onehot
    ranked = lax.optimization_barrier(jnp.sum(earlier * onehot, axis=1)).astype(jnp.int32)
    return jnp.stack([ranked[priority_rows], ranked[count + priority_rows]], axis=1)

@jax.checkpoint
def attend(query, key_pad, value_pad, bias, doc_ids, doc_keys, index):
    block = PIECE * N_EXP
    blocks = LENGTH // block
    seq = (index // blocks).astype(jnp.int32)
    start = (index % blocks * block).astype(jnp.int32)
    zero = jnp.zeros((), jnp.int32)
    q_blk = lax.dynamic_slice(query, (seq, start, zero, zero), (1, block, HEADS, HEAD_DIM))[0]
    k_blk = lax.dynamic_slice(key_pad, (seq, start, zero, zero), (1, 3 * block, HEADS, HEAD_DIM))[0]
    v_blk = lax.dynamic_slice(value_pad, (seq, start, zero, zero), (1, 3 * block, HEADS, HEAD_DIM))[0]
    q_doc = lax.dynamic_slice(doc_ids, (seq, start), (1, block))[0]
    k_doc = lax.dynamic_slice(doc_keys, (seq, start), (1, 3 * block))[0]
    distance = jnp.arange(block, dtype=jnp.int32)[:, None] + 2 * block - jnp.arange(3 * block, dtype=jnp.int32)[None, :]
    allowed = (distance >= 0) & (distance < WINDOW) & (q_doc[:, None] == k_doc[None, :])
    scores = jnp.einsum('qhd,khd->hqk', q_blk, k_blk, precision=lax.Precision.HIGHEST) * HEAD_DIM ** (-0.5) + bias
    scores = low_back(scores)
    scores = jnp.where(allowed[None], scores, -1e+30)
    probs = low(jax.nn.softmax(scores, axis=-1))
    return jnp.einsum('hqk,khd->qhd', probs, v_blk, precision=lax.Precision.HIGHEST)

@jax.checkpoint
def expert_apply(parts):
    inputs, gate_weight, up_weight, down_weight = parts
    gate_pre = low_back(matmul(inputs, gate_weight))
    up_pre = low_back(matmul(inputs, up_weight))
    activation = low(jax.nn.gelu(gate_pre) * up_pre)
    return low(low_back(matmul(activation, down_weight)))

def reference(tokens, doc_lengths, routes, priority, norm1_gain, w_query, w_key, w_value, w_out, bias_table, norm2_gain, w_router, w_gate, w_up, w_down, cotangent):
    block = PIECE * N_EXP
    blocks = LENGTH // block
    groups = LENGTH // PIECE
    group_size = SEQS * PIECE
    positions = jnp.arange(LENGTH, dtype=jnp.int32)
    ends = jnp.cumsum(doc_lengths, axis=1).astype(jnp.int32)
    doc_ids = lax.optimization_barrier(jnp.sum((positions[None, :, None] >= ends[:, None, :]).astype(jnp.int32), axis=2)).astype(jnp.int32)
    doc_keys = jnp.concatenate([jnp.full((SEQS, 2 * block), -1, jnp.int32), doc_ids], axis=1)
    distance = jnp.arange(block, dtype=jnp.int32)[:, None] + 2 * block - jnp.arange(3 * block, dtype=jnp.int32)[None, :]
    onehot = (bucket_of(distance)[..., None] == jnp.arange(BUCKETS, dtype=jnp.int32)).astype(jnp.float32)
    route_groups = routes.reshape(SEQS, groups, PIECE, 2).transpose(1, 0, 2, 3).reshape(groups, group_size, 2)
    prio_groups = priority.reshape(SEQS, groups, PIECE).transpose(1, 0, 2).reshape(groups, group_size)
    places = jax.vmap(lambda rows, order: group_places(rows, order, EXPERTS))(route_groups, prio_groups)
    kept = places < SLOT
    target = jnp.where(kept, route_groups * SLOT + places, EXPERTS * SLOT).astype(jnp.int32)
    fill_value = jnp.arange(2 * group_size, dtype=jnp.int32)
    assign = jax.vmap(lambda spot: jnp.full((EXPERTS * SLOT,), 2 * group_size, jnp.int32).at[spot.reshape(-1)].set(fill_value, mode='drop'))(target)
    slot_token = jnp.where(assign < 2 * group_size, assign // 2, group_size).astype(jnp.int32)
    pick = jnp.where(kept, target, 0).astype(jnp.int32)
    keep_weight = kept.astype(jnp.float32)
    route_hot = (route_groups[..., None] == jnp.arange(EXPERTS, dtype=jnp.int32)).astype(jnp.float32)

    def forward(x_in, gain1, wq, wk, wv, wo, table, gain2, wr, wg, wu, wd):
        normed = low(norm_rows(x_in, gain1)).reshape(-1, D)
        query = low(low_back(matmul(normed, wq))).reshape(SEQS, LENGTH, HEADS, HEAD_DIM)
        key = low(low_back(matmul(normed, wk))).reshape(SEQS, LENGTH, HEADS, HEAD_DIM)
        value = low(low_back(matmul(normed, wv))).reshape(SEQS, LENGTH, HEADS, HEAD_DIM)
        bias = jnp.einsum('qkb,hb->hqk', onehot, table.reshape(HEADS, BUCKETS), precision=lax.Precision.HIGHEST)
        front = jnp.zeros((SEQS, 2 * block, HEADS, HEAD_DIM), jnp.float32)
        key_pad = jnp.concatenate([front, key], axis=1)
        value_pad = jnp.concatenate([front, value], axis=1)
        context = lax.map(partial(attend, query, key_pad, value_pad, bias, doc_ids, doc_keys), jnp.arange(SEQS * blocks, dtype=jnp.int32))
        context = low(low_back(context.reshape(SEQS * LENGTH, D)))
        attn = low_back(matmul(context, wo)).reshape(SEQS, LENGTH, D)
        hidden = x_in + attn
        moe_in = low(norm_rows(hidden, gain2))
        router_probs = jax.nn.softmax(matmul(moe_in.reshape(-1, D), wr), axis=-1)
        probs_groups = router_probs.reshape(SEQS, groups, PIECE, EXPERTS).transpose(1, 0, 2, 3).reshape(groups, group_size, EXPERTS)
        gates = lax.optimization_barrier(jnp.sum(probs_groups[:, :, None, :] * route_hot, axis=-1))
        moe_groups = moe_in.reshape(SEQS, groups, PIECE, D).transpose(1, 0, 2, 3).reshape(groups, group_size, D)
        padded = jnp.concatenate([moe_groups, jnp.zeros((groups, 1, D), jnp.float32)], axis=1)
        inputs = jax.vmap(lambda rows, spot: rows[spot])(padded, slot_token)
        inputs = inputs.reshape(groups, EXPERTS, SLOT, D).transpose(1, 0, 2, 3).reshape(EXPERTS, groups * SLOT, D)
        inputs = low_back(inputs)
        outputs = lax.map(expert_apply, (inputs, wg, wu, wd))
        out_groups = outputs.reshape(EXPERTS, groups, SLOT, D).transpose(1, 0, 2, 3).reshape(groups, EXPERTS * SLOT, D)
        chosen = jax.vmap(lambda rows, spot: rows[spot])(out_groups, pick.reshape(groups, 2 * group_size)).reshape(groups, group_size, 2, D)
        mix = lax.optimization_barrier(jnp.sum((gates * keep_weight)[..., None] * chosen, axis=2))
        mix = mix.reshape(groups, SEQS, PIECE, D).transpose(1, 0, 2, 3).reshape(SEQS, LENGTH, D)
        return hidden + mix
    primals = (tokens, norm1_gain, w_query, w_key, w_value, w_out, bias_table, norm2_gain, w_router, w_gate, w_up, w_down)
    primals = tuple((item.astype(jnp.float32) for item in primals))
    mixed, pullback = jax.vjp(forward, *primals)
    grads = pullback(cotangent.astype(jnp.float32))
    return (mixed.astype(jnp.bfloat16), grads[0].astype(jnp.bfloat16), grads[1], grads[2], grads[3], grads[4], grads[5], grads[6], grads[7], grads[8], grads[9], grads[10], grads[11])
```

```python
import functools

import jax
import jax.numpy as jnp
import numpy as np
from jax import lax
from jax.experimental import pallas as pl
from jax.experimental.pallas import tpu as pltpu
from jax.sharding import PartitionSpec as P

WINDOW = 1024
TILE = 128
TILES_SEEN = WINDOW // TILE + 1
epsilon = 1e-06
bucket_total = 32
NEG = -1e30
f32 = jnp.float32
bf16 = jnp.bfloat16
VMEM = 56 * 1024 * 1024


def dot(left, right):
    return jnp.dot(left, right, preferred_element_type=f32)


def dot_nt(left, right):
    return lax.dot_general(left, right, (((1,), (1,)), ((), ())), preferred_element_type=f32)


def dot_tn(left, right):
    return lax.dot_general(left, right, (((0,), (0,)), ((), ())), preferred_element_type=f32)


def exact_dot(left, right):
    return jnp.dot(left, right, precision=lax.Precision.HIGHEST, preferred_element_type=f32)


def bucket_of(distance):
    limits = np.ceil(16.0 * 8.0 ** (np.arange(1, 16) / 16.0)).astype(np.int32)
    above = np.sum(distance[..., None] >= limits, axis=-1)
    return np.where(distance < 16, distance, 16 + above)


def bias_kernel(vec_ref, out_ref):
    for a in range(TILES_SEEN):
        first = (TILES_SEEN - 1 - a) * TILE
        for h in range(2):
            row = vec_ref[0, h : h + 1, first : first + 2 * TILE]
            wide = jnp.broadcast_to(row, (TILE, 2 * TILE))
            rolled = pltpu.roll(wide, TILE, 1, stride=1, stride_axis=0)
            out_ref[0, a, :, h * TILE : (h + 1) * TILE] = rolled[:, :TILE].astype(bf16)


def split_heads(x):
    lane = lax.broadcasted_iota(jnp.int32, x.shape, 1)
    zero = jnp.zeros_like(x)
    return jnp.concatenate([jnp.where(lane < 64, x, zero), jnp.where(lane < 64, zero, x)], axis=0)


def merge_heads(xt):
    return jnp.concatenate([xt[:64, :TILE], xt[64:, TILE:]], axis=0).T


def attend_kernel(tiles, lo_ref, q_ref, k_ref, v_ref, b_ref, out_ref, lse_ref, s_ref, p_ref):
    vt = v_ref[...].T
    row = lax.broadcasted_iota(jnp.int32, (TILE, 2 * TILE), 0)
    for t in range(tiles):
        q2 = split_heads(q_ref[t * TILE : (t + 1) * TILE, :])
        lo = lo_ref[:, t * 2 * TILE : (t + 1) * 2 * TILE]
        top = jnp.full((8, 2 * TILE), NEG, f32)
        for a in range(TILES_SEEN):
            kb = t + a
            s = dot_nt(k_ref[kb * TILE : (kb + 1) * TILE, :], q2) + b_ref[0, a].astype(f32)
            s = jnp.where(row >= lo - kb * TILE, s, NEG)
            s_ref[a] = s
            top = jnp.maximum(top, jnp.max(s.reshape(TILE // 8, 8, 2 * TILE), axis=0))
        top = jnp.max(top, axis=0, keepdims=True)
        total = jnp.zeros((8, 2 * TILE), f32)
        for a in range(TILES_SEEN):
            p = jnp.exp(s_ref[a] - top)
            total = total + jnp.sum(p.reshape(TILE // 8, 8, 2 * TILE), axis=0)
            p_ref[a * TILE : (a + 1) * TILE, :] = p.astype(bf16)
        total = jnp.sum(total, axis=0, keepdims=True)
        ct = dot(vt[:, t * TILE : (t + TILES_SEEN) * TILE], p_ref[...]) / total
        out_ref[t * TILE : (t + 1) * TILE, :] = merge_heads(ct).astype(bf16)
        lse_ref[0, :, t * 2 * TILE : (t + 1) * 2 * TILE] = top + jnp.log(total)


def attend_back_kernel(
    tiles, lo_ref, lse_ref, q_ref, k_ref, v_ref, o_ref, do_ref, b_ref,
    dq_ref, dk_ref, dv_ref, tab_ref, q2_ref, do2_ref, ds_ref, p_ref, acc_ref, delta_ref,
):
    row = lax.broadcasted_iota(jnp.int32, (TILE, 2 * TILE), 0)
    for t in range(tiles):
        rows = slice(t * TILE, (t + 1) * TILE)
        both = slice(t * 2 * TILE, (t + 1) * 2 * TILE)
        q2_ref[both, :] = split_heads(q_ref[rows, :])
        do2_ref[both, :] = split_heads(do_ref[rows, :])
        prod = (do_ref[rows, :].astype(f32) * o_ref[rows, :].astype(f32)).T
        delta_ref[:, t * 2 * TILE : t * 2 * TILE + TILE] = jnp.sum(prod[:64], axis=0, keepdims=True)
        delta_ref[:, t * 2 * TILE + TILE : (t + 1) * 2 * TILE] = jnp.sum(prod[64:], axis=0, keepdims=True)
    acc_ref[...] = jnp.zeros_like(acc_ref)
    keys = tiles + TILES_SEEN - 1
    for kb in range(keys):
        first, last = max(0, kb - TILES_SEEN + 1), min(tiles - 1, kb)
        krows = slice(kb * TILE, (kb + 1) * TILE)
        cols = slice(first * 2 * TILE, (last + 1) * 2 * TILE)
        key, value = k_ref[krows, :], v_ref[krows, :]
        for t in range(first, last + 1):
            both = slice(t * 2 * TILE, (t + 1) * 2 * TILE)
            a = kb - t
            s = dot_nt(key, q2_ref[both, :]) + b_ref[0, a].astype(f32)
            s = jnp.where(row >= lo_ref[:, both] - kb * TILE, s, NEG)
            p = jnp.exp(s - lse_ref[0, :, both])
            dp = dot_nt(value, do2_ref[both, :])
            ds = p * (dp - delta_ref[:, both])
            acc_ref[a] += ds
            p_ref[:, both] = p.astype(bf16)
            ds_ref[krows, both] = ds.astype(bf16)
        dk_ref[krows, :] = dot(ds_ref[krows, cols], q2_ref[cols, :]).astype(bf16)
        dv_ref[krows, :] = dot(p_ref[:, cols], do2_ref[cols, :]).astype(bf16)
    kt = k_ref[...].T
    for t in range(tiles):
        both = slice(t * 2 * TILE, (t + 1) * 2 * TILE)
        span = slice(t * TILE, (t + TILES_SEEN) * TILE)
        dqt = dot(kt[:, span], ds_ref[span, both]) * 0.125
        dq_ref[t * TILE : (t + 1) * TILE, :] = merge_heads(dqt).astype(bf16)
    for a in range(TILES_SEEN):
        for h in range(2):
            part = acc_ref[a, :, h * TILE : (h + 1) * TILE]
            part = jnp.concatenate([part, jnp.zeros_like(part)], axis=1)
            half = TILE // 2
            while half >= 1:
                part = part[:half] + pltpu.roll(part[half:], 2 * TILE - half, 1)
                half //= 2
            tab_ref[0, h, a : a + 1, :] = pltpu.roll(part, TILE, 1)


def bias_tiles(vec):
    pairs = vec.shape[0]
    return pl.pallas_call(
        bias_kernel,
        grid=(pairs,),
        in_specs=[pl.BlockSpec((1, 2, vec.shape[2]), lambda g: (g, 0, 0))],
        out_specs=pl.BlockSpec((1, TILES_SEEN, TILE, 2 * TILE), lambda g: (g, 0, 0, 0)),
        out_shape=jax.ShapeDtypeStruct((pairs, TILES_SEEN, TILE, 2 * TILE), bf16),
        compiler_params=pltpu.CompilerParams(vmem_limit_bytes=VMEM),
        name="bias_tiles",
    )(vec)


def attend(lo, q, k, v, bias):
    rows, width = q.shape
    keys = k.shape[0]
    pairs, tiles = width // TILE, rows // TILE
    half = lambda n: pl.BlockSpec((n, TILE), lambda g: (0, g))
    return pl.pallas_call(
        functools.partial(attend_kernel, tiles),
        grid=(pairs,),
        in_specs=[
            pl.BlockSpec((1, 2 * rows), lambda g: (0, 0)),
            half(rows), half(keys), half(keys),
            pl.BlockSpec((1, TILES_SEEN, TILE, 2 * TILE), lambda g: (g, 0, 0, 0)),
        ],
        out_specs=[half(rows), pl.BlockSpec((1, 1, 2 * rows), lambda g: (g, 0, 0))],
        out_shape=[
            jax.ShapeDtypeStruct((rows, width), bf16),
            jax.ShapeDtypeStruct((pairs, 1, 2 * rows), f32),
        ],
        scratch_shapes=[
            pltpu.VMEM((TILES_SEEN, TILE, 2 * TILE), f32),
            pltpu.VMEM((TILES_SEEN * TILE, 2 * TILE), bf16),
        ],
        compiler_params=pltpu.CompilerParams(vmem_limit_bytes=VMEM),
        cost_estimate=pl.CostEstimate(flops=20_000_000_000, bytes_accessed=16_000_000, transcendentals=9_400_000),
        name="attend",
    )(lo, q, k, v, bias)


def attend_back(lo, lse, q, k, v, o, do, bias):
    rows, width = q.shape
    keys = k.shape[0]
    pairs, tiles = width // TILE, rows // TILE
    half = lambda n: pl.BlockSpec((n, TILE), lambda g: (0, g))
    return pl.pallas_call(
        functools.partial(attend_back_kernel, tiles),
        grid=(pairs,),
        in_specs=[
            pl.BlockSpec((1, 2 * rows), lambda g: (0, 0)),
            pl.BlockSpec((1, 1, 2 * rows), lambda g: (g, 0, 0)),
            half(rows), half(keys), half(keys), half(rows), half(rows),
            pl.BlockSpec((1, TILES_SEEN, TILE, 2 * TILE), lambda g: (g, 0, 0, 0)),
        ],
        out_specs=[
            half(rows), half(keys), half(keys),
            pl.BlockSpec((1, 2, TILES_SEEN, 2 * TILE), lambda g: (g, 0, 0, 0)),
        ],
        out_shape=[
            jax.ShapeDtypeStruct((rows, width), bf16),
            jax.ShapeDtypeStruct((keys, width), bf16),
            jax.ShapeDtypeStruct((keys, width), bf16),
            jax.ShapeDtypeStruct((pairs, 2, TILES_SEEN, 2 * TILE), f32),
        ],
        scratch_shapes=[
            pltpu.VMEM((2 * rows, TILE), bf16),
            pltpu.VMEM((2 * rows, TILE), bf16),
            pltpu.VMEM((keys, 2 * rows), bf16),
            pltpu.VMEM((TILE, 2 * rows), bf16),
            pltpu.VMEM((TILES_SEEN, TILE, 2 * TILE), f32),
            pltpu.VMEM((1, 2 * rows), f32),
        ],
        compiler_params=pltpu.CompilerParams(vmem_limit_bytes=VMEM),
        cost_estimate=pl.CostEstimate(flops=50_000_000_000, bytes_accessed=24_000_000, transcendentals=9_400_000),
        name="attend_back",
    )(lo, lse, q, k, v, o, do, bias)


def shift(x, by):
    count = lax.axis_size("ctx")
    return lax.ppermute(x, "ctx", [(i, i + by) for i in range(count) if 0 <= i + by < count])


def core_swap(x):
    return lax.ppermute(x, "ctx", [(i, i ^ 1) for i in range(lax.axis_size("ctx"))])


def over_exp(x):
    return lax.all_to_all(x, "exp", split_axis=0, concat_axis=0, tiled=True)


def sum_over_ctx(partial):
    count = lax.axis_size("ctx")
    rows, width = partial.shape
    side = lax.axis_index("ctx") % 2
    parts = partial.reshape(count // 2, 2, rows // count, width)
    other = core_swap(lax.dynamic_index_in_dim(parts, 1 - side, 1, keepdims=False))
    mine = lax.dynamic_index_in_dim(parts, side, 1, keepdims=False)
    pair = (mine.astype(f32) + other.astype(f32)).astype(bf16)
    groups = [list(range(core, count, 2)) for core in range(2)]
    got = lax.all_to_all(pair, "ctx", split_axis=0, concat_axis=0, tiled=True, axis_index_groups=groups)
    return jnp.sum(got.astype(f32), axis=0)


def sum_over_all(partial):
    rows_sum = sum_over_ctx(partial).astype(bf16)
    count = lax.axis_size("exp")
    got = over_exp(rows_sum.reshape(count, -1, rows_sum.shape[-1]))
    return jnp.sum(got.astype(f32), axis=0)


def norm_rows(values, gain):
    return values * lax.rsqrt(jnp.mean(values * values, axis=-1, keepdims=True) + epsilon) * gain


def norm_back(values, gain, grad):
    r = lax.rsqrt(jnp.mean(values * values, axis=-1, keepdims=True) + epsilon)
    u = grad * gain
    inner = jnp.mean(values * u, axis=-1, keepdims=True)
    return r * u - values * (r * r * r) * inner, jnp.sum(grad * values * r, axis=0)


def gelu_parts(v):
    c = np.float32(np.sqrt(2.0 / np.pi))
    t = jnp.tanh(c * (v + 0.044715 * v * v * v))
    half = 0.5 * (1.0 + t)
    return v * half, half + 0.5 * v * (1.0 - t * t) * (c * (1.0 + 3.0 * 0.044715 * v * v))


def on_device(
    tokens, doc_lengths, routes, priority, norm1_gain, w_query, w_key, w_value, w_out, bias_table,
    norm2_gain, w_router, w_gate, w_up, w_down, cotangent,
):
    seqs, piece_len, width = tokens.shape
    exp_count = lax.axis_size("exp")
    ctx_count = lax.axis_size("ctx")
    device_count = exp_count * ctx_count
    block_len = piece_len * exp_count
    rows = seqs * piece_len
    heads = bias_table.shape[0] // bucket_total
    experts = w_router.shape[1]
    slot = 5 * rows // (2 * experts)
    slots = experts * slot
    ctx = lax.axis_index("ctx")
    exp = lax.axis_index("exp")
    side = ctx % 2

    x_own = over_exp(tokens).reshape(block_len, width)
    x_two = shift(x_own, 2)
    x_one = core_swap(jnp.where(side == 0, x_own, x_two))

    route_rows = routes.reshape(rows, 2)
    order = priority.reshape(rows)
    earlier = order[None, :] < order[:, None]
    r0, r1 = route_rows[:, 0], route_rows[:, 1]
    place0 = jnp.sum((earlier & (r0[None, :] == r0[:, None])).astype(jnp.int32), axis=1)
    place1 = jnp.sum((earlier & (r1[None, :] == r1[:, None])).astype(jnp.int32), axis=1) + jnp.sum(
        (r0[None, :] == r1[:, None]).astype(jnp.int32), axis=1
    )
    target0 = jnp.where(place0 < slot, r0 * slot + place0, -1)
    target1 = jnp.where(place1 < slot, r1 * slot + place1, -1)
    slot_index = jnp.arange(slots, dtype=jnp.int32)[:, None]
    spread = ((slot_index == target0[None, :]) | (slot_index == target1[None, :])).astype(bf16)

    def dispatch(values):
        return over_exp(dot(spread, values).astype(bf16).reshape(experts, slot, width)).reshape(slots, width)

    def collect(values):
        return dot_tn(spread, over_exp(values.reshape(experts, slot, width)).reshape(slots, width))

    cot_rows = cotangent.reshape(rows, width)
    cot_slots = dispatch(cot_rows)

    distance = np.arange(-TILE, WINDOW + TILE)
    seen = (distance >= 0) & (distance < WINDOW)
    hot = (bucket_of(np.clip(distance, 0, None))[None, :] == np.arange(bucket_total)[:, None]) & seen[None, :]
    vec = exact_dot(bias_table.astype(f32).reshape(heads, bucket_total), jnp.asarray(hot, f32))
    vec = jnp.where(jnp.asarray(seen)[None, :], vec, NEG).reshape(heads // 2, 2, -1)
    bias = bias_tiles(vec)

    ends = jnp.cumsum(lax.dynamic_index_in_dim(doc_lengths, exp, 0, keepdims=False))
    q_pos = ctx * block_len + jnp.arange(block_len, dtype=jnp.int32)
    start = jnp.max(jnp.where(ends[None, :] <= q_pos[:, None], ends[None, :], 0), axis=1)
    lo = start - (ctx - 2) * block_len
    lo = jnp.broadcast_to(lo.reshape(-1, 1, TILE), (block_len // TILE, 2, TILE)).reshape(1, -1)

    gain_one = norm1_gain.astype(f32)
    x_window = jnp.concatenate([x_two, x_one, x_own], axis=0)
    normed = norm_rows(x_window.astype(f32), gain_one).astype(bf16)
    normed_own = normed[2 * block_len :]
    q = (dot(normed_own, w_query).astype(bf16) * 0.125).astype(bf16)
    k = dot(normed, w_key).astype(bf16)
    v = dot(normed, w_value).astype(bf16)
    context, lse = attend(lo, q, k, v, bias)

    context_rows = over_exp(context.reshape(exp_count, piece_len, width)).reshape(rows, width)
    hidden = tokens.reshape(rows, width).astype(f32) + dot(context_rows, w_out)
    gain_two = norm2_gain.astype(f32)
    moe_in = norm_rows(hidden, gain_two).astype(bf16)

    wg, wu, wd = w_gate[0], w_up[0], w_down[0]
    grad_raw = dot_nt(cot_slots, wd)
    inputs = dispatch(moe_in)
    router_probs = jax.nn.softmax(dot(inputs, w_router), axis=-1)
    own_expert = (jnp.arange(experts) == exp).astype(f32)[None, :]
    gate = jnp.sum(router_probs * own_expert, axis=-1, keepdims=True)
    gate_pre = dot(inputs, wg)
    up_pre = dot(inputs, wu)
    gelu, gelu_slope = gelu_parts(gate_pre)
    activation = gelu * up_pre
    act_low = activation.astype(bf16)
    grad_gates = jnp.sum(activation * grad_raw, axis=-1, keepdims=True)
    grad_act = grad_raw * gate
    grad_gate_pre = (grad_act * up_pre * gelu_slope).astype(bf16)
    grad_up_pre = (grad_act * gelu).astype(bf16)
    grad_logits = grad_gates * router_probs * (own_expert - gate)
    grad_inputs = (
        dot_nt(grad_gate_pre, wg)
        + dot_nt(grad_up_pre, wu)
        + exact_dot(grad_logits, w_router.astype(f32).T)
    ).astype(bf16)
    grad_moe = collect(grad_inputs)
    grad_router_part = lax.dot_general(
        inputs.astype(f32), grad_logits, (((0,), (0,)), ((), ())),
        precision=lax.Precision.HIGHEST, preferred_element_type=f32,
    )
    produced = (dot(act_low, wd) * gate).astype(bf16)
    mixed = (hidden + collect(produced)).astype(bf16).reshape(seqs, piece_len, width)
    grad_out_slots = (gate * cot_slots.astype(f32)).astype(bf16)
    grad_gate = sum_over_ctx(dot_tn(inputs, grad_gate_pre).astype(bf16))
    grad_up = sum_over_ctx(dot_tn(inputs, grad_up_pre).astype(bf16))
    grad_down = sum_over_ctx(dot_tn(act_low, grad_out_slots).astype(bf16))

    grad_norm, grad_gain_two = norm_back(hidden, gain_two, grad_moe)
    grad_hidden = cot_rows.astype(f32) + grad_norm
    grad_attn = grad_hidden.astype(bf16)
    grad_out = sum_over_all(dot_tn(context_rows, grad_attn).astype(bf16))
    grad_context = dot_nt(grad_attn, w_out).astype(bf16)
    grad_context = over_exp(grad_context.reshape(seqs, piece_len, width)).reshape(block_len, width)

    dq, dk, dv, diagonals = attend_back(lo, lse, q, k, v, context, grad_context, bias)
    grad_window = dot_nt(dk, w_key) + dot_nt(dv, w_value)
    part_two = grad_window[:block_len].astype(bf16)
    part_one = grad_window[block_len : 2 * block_len].astype(bf16)
    swapped = core_swap(part_one).astype(f32)
    own_sum = grad_window[2 * block_len :] + dot_nt(dq, w_query)
    own_sum = own_sum + jnp.where(side == 0, swapped, 0.0)
    leave = jnp.where(side == 0, part_two.astype(f32), part_two.astype(f32) + swapped).astype(bf16)
    grad_normed = own_sum + shift(leave, -2).astype(f32)
    grad_query = sum_over_all(dot_tn(normed_own, dq).astype(bf16))
    grad_key = sum_over_all(dot_tn(normed, dk).astype(bf16))
    grad_value = sum_over_all(dot_tn(normed, dv).astype(bf16))
    grad_x, grad_gain_one = norm_back(x_own.astype(f32), gain_one, grad_normed)
    grad_x = over_exp(grad_x.astype(bf16).reshape(exp_count, piece_len, width)).reshape(rows, width)
    grad_tokens = (grad_hidden + grad_x.astype(f32)).astype(bf16).reshape(seqs, piece_len, width)

    places = np.arange((TILES_SEEN) * 2 * TILE).reshape(TILES_SEEN, 2 * TILE)
    block, lane = places // (2 * TILE), places % (2 * TILE)
    where_dist = lane - TILE + (TILES_SEEN - 1 - block) * TILE
    ok = (where_dist >= 0) & (where_dist < WINDOW)
    to_bucket = (bucket_of(np.clip(where_dist, 0, None))[..., None] == np.arange(bucket_total)) & ok[..., None]
    table_part = exact_dot(diagonals.reshape(heads, -1), jnp.asarray(to_bucket.reshape(-1, bucket_total), f32))
    small = [
        grad_gain_one.reshape(device_count, -1),
        grad_gain_two.reshape(device_count, -1),
        table_part.reshape(device_count, -1),
        grad_router_part.reshape(device_count, -1),
    ]
    sizes = [s.shape[1] for s in small]
    packed = jnp.concatenate(small, axis=1)
    packed = jnp.pad(packed, ((0, 0), (0, -packed.shape[1] % 128)))
    packed = lax.all_to_all(packed, ("ctx", "exp"), split_axis=0, concat_axis=0, tiled=True)
    packed = jnp.sum(packed, axis=0)
    cuts = np.cumsum([0] + sizes)
    norm1_out, norm2_out, table_out, router_out = [packed[cuts[i] : cuts[i + 1]] for i in range(4)]
    return (
        mixed, grad_tokens, norm1_out, grad_query, grad_key, grad_value, grad_out, table_out, norm2_out,
        router_out.reshape(-1, experts), grad_gate[None], grad_up[None], grad_down[None],
    )


def solution(mesh):
    rows = P(None, ("ctx", "exp"), None)
    flat = P(("ctx", "exp"))
    in_specs = (
        rows, P(), rows, P(None, ("ctx", "exp")), P(), P(), P(), P(), P(), P(), P(), P(),
        P("exp", None, None), P("exp", None, None), P("exp", None, None), rows,
    )
    out_specs = (
        rows, rows, flat, P(("ctx", "exp"), None), P(("ctx", "exp"), None), P(("ctx", "exp"), None),
        P(("ctx", "exp"), None), flat, flat, P(("ctx", "exp"), None),
        P("exp", "ctx", None), P("exp", "ctx", None), P("exp", "ctx", None),
    )
    return jax.shard_map(on_device, mesh=mesh, in_specs=in_specs, out_specs=out_specs, check_vma=False)
```

```python
import functools

import jax
import jax.numpy as jnp
import numpy as np
from jax import lax
from jax.experimental import pallas as pl
from jax.experimental.pallas import tpu as pltpu
from jax.sharding import PartitionSpec as P

WINDOW = 1024
TILE = 128
TILES_SEEN = WINDOW // TILE + 1
epsilon = 1e-06
bucket_total = 32
NEG = -1e30
f32 = jnp.float32
bf16 = jnp.bfloat16
VMEM = 56 * 1024 * 1024


def cost(us):
    return pl.CostEstimate(flops=int(us * 1.15e9), bytes_accessed=0, transcendentals=0)


def behind(kernel, inputs, others):
    return lambda *refs: kernel(*refs[:inputs], *refs[inputs + len(others) :])


def anywhere(others):
    return [pl.BlockSpec(memory_space=pl.ANY)] * len(others)


def dot(left, right):
    return jnp.dot(left, right, preferred_element_type=f32)


def dot_nt(left, right):
    return lax.dot_general(left, right, (((1,), (1,)), ((), ())), preferred_element_type=f32)


def dot_tn(left, right):
    return lax.dot_general(left, right, (((0,), (0,)), ((), ())), preferred_element_type=f32)


def exact_dot(left, right):
    return jnp.dot(left, right, precision=lax.Precision.HIGHEST, preferred_element_type=f32)


def bucket_of(distance):
    limits = np.ceil(16.0 * 8.0 ** (np.arange(1, 16) / 16.0)).astype(np.int32)
    above = np.sum(distance[..., None] >= limits, axis=-1)
    return np.where(distance < 16, distance, 16 + above)


def bias_kernel(vec_ref, out_ref):
    for a in range(TILES_SEEN):
        first = (TILES_SEEN - 1 - a) * TILE
        for h in range(2):
            row = vec_ref[0, h : h + 1, first : first + 2 * TILE]
            wide = jnp.broadcast_to(row, (TILE, 2 * TILE))
            rolled = pltpu.roll(wide, TILE, 1, stride=1, stride_axis=0)
            out_ref[0, a, :, h * TILE : (h + 1) * TILE] = rolled[:, :TILE].astype(bf16)


def split_heads(x):
    lane = lax.broadcasted_iota(jnp.int32, x.shape, 1)
    zero = jnp.zeros_like(x)
    return jnp.concatenate([jnp.where(lane < 64, x, zero), jnp.where(lane < 64, zero, x)], axis=0)


def merge_heads(xt):
    return jnp.concatenate([xt[:64, :TILE], xt[64:, TILE:]], axis=0).T


def key_block(kb, z):
    return (kb // 4) * 4 + ((kb % 4) ^ z)


def attend_kernel(ks, z_ref, lo_ref, q_ref, k_ref, v_ref, b_ref, *refs):
    outs, (lse_ref, s_ref, p_ref, v_s) = refs[: len(ks)], refs[len(ks) :]
    z = z_ref[0]
    row = lax.broadcasted_iota(jnp.int32, (TILE, 2 * TILE), 0)
    for n, k in enumerate(ks):
        t = z ^ k
        q2 = split_heads(q_ref[n])
        lo = lo_ref[n] - t * TILE
        top = jnp.full((8, 2 * TILE), NEG, f32)
        for a in range(TILES_SEEN):
            at = key_block(t + a, z)
            v_s[a * TILE : (a + 1) * TILE, :] = v_ref[at]
            s = dot_nt(k_ref[at], q2) + b_ref[0, a].astype(f32)
            s = jnp.where(row >= lo - a * TILE, s, NEG)
            s_ref[a] = s
            top = jnp.maximum(top, jnp.max(s.reshape(TILE // 8, 8, 2 * TILE), axis=0))
        top = jnp.max(top, axis=0, keepdims=True)
        total = jnp.zeros((8, 2 * TILE), f32)
        for a in range(TILES_SEEN):
            p = jnp.exp(s_ref[a] - top)
            total = total + jnp.sum(p.reshape(TILE // 8, 8, 2 * TILE), axis=0)
            p_ref[a * TILE : (a + 1) * TILE, :] = p.astype(bf16)
        total = jnp.sum(total, axis=0, keepdims=True)
        ct = dot(v_s[...].T, p_ref[...]) / total
        outs[n][...] = merge_heads(ct).astype(bf16)
        lse_ref[0, n] = top + jnp.log(total)


def attend_back_kernel(pieces, z_ref, lo_ref, lse_a, lse_b, q_ref, k_ref, v_ref, b_ref, *refs):
    o_refs, do_refs = refs[:pieces], refs[pieces : 2 * pieces]
    dq_ref, dk_ref, dv_ref, tab_ref, q2_ref, do2_ref, ds_ref, p_ref, acc_ref, row_ref, k_s = refs[2 * pieces :]
    z = z_ref[0]
    row = lax.broadcasted_iota(jnp.int32, (TILE, 2 * TILE), 0)
    for k in range(pieces):
        both = pl.ds(pl.multiple_of((z ^ k) * 2 * TILE, 2 * TILE), 2 * TILE)
        out, grad = o_refs[k][...], do_refs[k][...]
        q2_ref[both, :] = split_heads(q_ref[k])
        do2_ref[both, :] = split_heads(grad)
        prod = (grad.astype(f32) * out.astype(f32)).T
        lse_ref = lse_a if k < pieces // 2 else lse_b
        row_ref[0:1, both] = lse_ref[0, k % (pieces // 2)]
        row_ref[1:2, both] = jnp.concatenate(
            [jnp.sum(prod[:64], axis=0, keepdims=True), jnp.sum(prod[64:], axis=0, keepdims=True)], axis=1
        )
    acc_ref[...] = jnp.zeros_like(acc_ref)
    keys = pieces + TILES_SEEN - 1
    for kb in range(keys):
        first, last = max(0, kb - TILES_SEEN + 1), min(pieces - 1, kb)
        krows = slice(kb * TILE, (kb + 1) * TILE)
        cols = slice(first * 2 * TILE, (last + 1) * 2 * TILE)
        at = key_block(kb, z)
        key, value = k_ref[at], v_ref[at]
        k_s[krows, :] = key
        for t in range(first, last + 1):
            both = slice(t * 2 * TILE, (t + 1) * 2 * TILE)
            a = kb - t
            s = dot_nt(key, q2_ref[both, :]) + b_ref[0, a].astype(f32)
            s = jnp.where(row >= lo_ref[z ^ t] - kb * TILE, s, NEG)
            p = jnp.exp(s - row_ref[0:1, both])
            dp = dot_nt(value, do2_ref[both, :])
            ds = p * (dp - row_ref[1:2, both])
            acc_ref[a] += ds
            p_ref[:, both] = p.astype(bf16)
            ds_ref[krows, both] = ds.astype(bf16)
        dk_ref[at] = dot(ds_ref[krows, cols], q2_ref[cols, :]).astype(bf16)
        dv_ref[at] = dot(p_ref[:, cols], do2_ref[cols, :]).astype(bf16)
    kt = k_s[...].T
    for t in range(pieces):
        both = slice(t * 2 * TILE, (t + 1) * 2 * TILE)
        span = slice(t * TILE, (t + TILES_SEEN) * TILE)
        dqt = dot(kt[:, span], ds_ref[span, both]) * 0.125
        dq_ref[z ^ t] = merge_heads(dqt).astype(bf16)
    for a in range(TILES_SEEN):
        for h in range(2):
            part = acc_ref[a, :, h * TILE : (h + 1) * TILE]
            part = jnp.concatenate([part, jnp.zeros_like(part)], axis=1)
            half = TILE // 2
            while half >= 1:
                part = part[:half] + pltpu.roll(part[half:], 2 * TILE - half, 1)
                half //= 2
            tab_ref[0, h, a : a + 1, :] = pltpu.roll(part, TILE, 1)


def bias_tiles(vec):
    pairs = vec.shape[0]
    return pl.pallas_call(
        bias_kernel,
        grid=(pairs,),
        in_specs=[pl.BlockSpec((1, 2, vec.shape[2]), lambda g: (g, 0, 0))],
        out_specs=pl.BlockSpec((1, TILES_SEEN, TILE, 2 * TILE), lambda g: (g, 0, 0, 0)),
        out_shape=jax.ShapeDtypeStruct((pairs, TILES_SEEN, TILE, 2 * TILE), bf16),
        compiler_params=pltpu.CompilerParams(vmem_limit_bytes=VMEM),
        cost_estimate=cost(6),
        name="bias_tiles",
    )(vec)


SMEM = pl.BlockSpec(memory_space=pltpu.SMEM)


def attend(ks, z, lo, q, k, v, bias, others=()):
    count, _, width = q.shape
    blocks, pairs = k.shape[0], width // TILE
    part = lambda n: pl.BlockSpec((n, TILE, TILE), lambda g: (0, 0, g))
    return pl.pallas_call(
        behind(functools.partial(attend_kernel, ks), 6, others),
        grid=(pairs,),
        in_specs=[
            SMEM,
            pl.BlockSpec((count, 1, 2 * TILE), lambda g: (0, 0, 0)),
            part(count), part(blocks), part(blocks),
            pl.BlockSpec((1, TILES_SEEN, TILE, 2 * TILE), lambda g: (g, 0, 0, 0)),
        ] + anywhere(others),
        out_specs=[pl.BlockSpec((TILE, TILE), lambda g: (0, g))] * count
        + [pl.BlockSpec((1, count, 1, 2 * TILE), lambda g: (g, 0, 0, 0))],
        out_shape=[jax.ShapeDtypeStruct((TILE, width), bf16)] * count
        + [
            jax.ShapeDtypeStruct((pairs, count, 1, 2 * TILE), f32),
        ],
        scratch_shapes=[
            pltpu.VMEM((TILES_SEEN, TILE, 2 * TILE), f32),
            pltpu.VMEM((TILES_SEEN * TILE, 2 * TILE), bf16),
            pltpu.VMEM((TILES_SEEN * TILE, TILE), bf16),
        ],
        compiler_params=pltpu.CompilerParams(vmem_limit_bytes=VMEM),
        cost_estimate=cost(7.4 * count),
        name="attend",
    )(z, lo, q, k, v, bias, *others)


def attend_back(part_index, part_count, z, lo, lses, q, k, v, bias, o, do, others=()):
    pieces, _, width = q.shape
    blocks, pairs = k.shape[0], width // TILE // part_count
    base = part_index * pairs
    part = lambda n: pl.BlockSpec((n, TILE, TILE), lambda g: (0, 0, base + g))
    alone = lambda n: pl.BlockSpec((n, TILE, TILE), lambda g: (0, 0, g))
    columns = pieces * 2 * TILE
    return pl.pallas_call(
        behind(functools.partial(attend_back_kernel, pieces), 8 + 2 * pieces, others),
        grid=(pairs,),
        in_specs=[
            SMEM,
            pl.BlockSpec((pieces, 1, 2 * TILE), lambda g: (0, 0, 0)),
            pl.BlockSpec((1, pieces // 2, 1, 2 * TILE), lambda g: (base + g, 0, 0, 0)),
            pl.BlockSpec((1, pieces // 2, 1, 2 * TILE), lambda g: (base + g, 0, 0, 0)),
            part(pieces), part(blocks), part(blocks),
            pl.BlockSpec((1, TILES_SEEN, TILE, 2 * TILE), lambda g: (base + g, 0, 0, 0)),
        ]
        + [pl.BlockSpec((TILE, TILE), lambda g: (0, base + g))] * pieces
        + [pl.BlockSpec((TILE, TILE), lambda g: (0, g))] * pieces
        + anywhere(others),
        out_specs=[
            alone(pieces), alone(blocks), alone(blocks),
            pl.BlockSpec((1, 2, TILES_SEEN, 2 * TILE), lambda g: (g, 0, 0, 0)),
        ],
        out_shape=[
            jax.ShapeDtypeStruct((pieces, TILE, width // part_count), bf16),
            jax.ShapeDtypeStruct((blocks, TILE, width // part_count), bf16),
            jax.ShapeDtypeStruct((blocks, TILE, width // part_count), bf16),
            jax.ShapeDtypeStruct((pairs, 2, TILES_SEEN, 2 * TILE), f32),
        ],
        scratch_shapes=[
            pltpu.VMEM((columns, TILE), bf16),
            pltpu.VMEM((columns, TILE), bf16),
            pltpu.VMEM((blocks * TILE, columns), bf16),
            pltpu.VMEM((TILE, columns), bf16),
            pltpu.VMEM((TILES_SEEN, TILE, 2 * TILE), f32),
            pltpu.VMEM((8, columns), f32),
            pltpu.VMEM((blocks * TILE, TILE), bf16),
        ],
        compiler_params=pltpu.CompilerParams(vmem_limit_bytes=VMEM),
        cost_estimate=cost(42 / part_count),
        name="attend_back",
    )(z, lo, *lses, q, k, v, bias, *o, *do, *others)


def gelu_parts(v):
    c = np.float32(np.sqrt(2.0 / np.pi))
    t = jnp.tanh(c * (v + 0.044715 * v * v * v))
    half = 0.5 * (1.0 + t)
    return v * half, half + 0.5 * v * (1.0 - t * t) * (c * (1.0 + 3.0 * 0.044715 * v * v))


def expert_kernel(
    experts, held, z_ref, x_ref, c_ref, wg_ref, wu_ref, wd_ref, wr_ref, *refs,
):
    gin_ref, kept_ref, act_ref, dgp_ref, dup_ref, gcot_ref, gate_out, glog_ref, acc_ref, gg_ref, rp_ref, gate_ref = refs[held:]
    step = pl.program_id(0)
    lane = lax.broadcasted_iota(jnp.int32, (x_ref.shape[0], TILE), 1)
    x, c = x_ref[...], c_ref[...]

    @pl.when(step == 0)
    def _():
        logits = jnp.where(lane < experts, dot(x, wr_ref[...]), NEG)
        e = jnp.exp(logits - jnp.max(logits, axis=1, keepdims=True))
        probs = e / jnp.sum(e, axis=1, keepdims=True)
        rp_ref[...] = probs
        gate = jnp.sum(jnp.where(lane == z_ref[0], probs, 0.0), axis=1, keepdims=True)
        gate_ref[...] = jnp.broadcast_to(gate, gate_ref.shape)
        gate_out[...] = gate_ref[...]
        kept_ref[...] = x
        gcot_ref[...] = (gate * c.astype(f32)).astype(bf16)
        acc_ref[...] = jnp.zeros_like(acc_ref)
        gg_ref[...] = jnp.zeros_like(gg_ref)

    raw = dot_nt(c, wd_ref[0])
    gate_pre = dot(x, wg_ref[0])
    up_pre = dot(x, wu_ref[0])
    gelu, slope = gelu_parts(gate_pre)
    act = gelu * up_pre
    act_ref[...] = act.astype(bf16)
    prod = act * raw
    gg_ref[...] += prod[:, :TILE] + prod[:, TILE:]
    scaled = raw * gate_ref[:, :1]
    dgp = (scaled * up_pre * slope).astype(bf16)
    dup = (scaled * gelu).astype(bf16)
    dgp_ref[...] = dgp
    dup_ref[...] = dup
    acc_ref[...] += dot_nt(dgp, wg_ref[0]) + dot_nt(dup, wu_ref[0])

    @pl.when(step == pl.num_programs(0) - 1)
    def _():
        gg = jnp.sum(gg_ref[...], axis=1, keepdims=True)
        own = jnp.where(lane == z_ref[0], 1.0, 0.0)
        glog = gg * rp_ref[...] * (own - gate_ref[...])
        glog_ref[...] = glog
        high = glog.astype(bf16)
        low = (glog - high.astype(f32)).astype(bf16)
        gin_ref[...] = (acc_ref[...] + dot_nt(high, wr_ref[...]) + dot_nt(low, wr_ref[...])).astype(bf16)


def expert(chunk, chunks, held, z, x, c, wg, wu, wd, wr, experts, others=()):
    rows, width = x.shape
    hidden = wg.shape[2]
    wide = 2 * TILE
    whole = pl.BlockSpec((rows, width), lambda f: (0, 0))
    kept = pl.BlockSpec((rows, width), lambda f: (chunk, 0))
    thin = pl.BlockSpec((rows, TILE), lambda f: (chunk, 0))
    tile = pl.BlockSpec((rows, wide), lambda f: (chunk, f))
    full = lambda n, t: jax.ShapeDtypeStruct((chunks * rows, n), t)
    held = [] if held is None else list(held)
    return pl.pallas_call(
        functools.partial(expert_kernel, experts, len(held) + len(others)),
        grid=(hidden // wide,),
        in_specs=[
            SMEM, whole, whole,
            pl.BlockSpec((1, width, wide), lambda f: (0, 0, f)),
            pl.BlockSpec((1, width, wide), lambda f: (0, 0, f)),
            pl.BlockSpec((1, wide, width), lambda f: (0, f, 0)),
            pl.BlockSpec((width, TILE), lambda f: (0, 0)),
        ] + anywhere(held) + anywhere(others),
        out_specs=[whole, kept, tile, tile, tile, kept, thin, thin],
        out_shape=[
            jax.ShapeDtypeStruct((rows, width), bf16),
            full(width, bf16), full(hidden, bf16), full(hidden, bf16), full(hidden, bf16), full(width, bf16),
            full(TILE, f32), full(TILE, f32),
        ],
        input_output_aliases={7 + i: 1 + i for i in range(len(held))},
        scratch_shapes=[
            pltpu.VMEM((rows, width), f32), pltpu.VMEM((rows, TILE), f32), pltpu.VMEM((rows, TILE), f32),
            pltpu.VMEM((rows, TILE), f32),
        ],
        compiler_params=pltpu.CompilerParams(vmem_limit_bytes=VMEM),
        cost_estimate=cost(23),
        name="expert",
    )(z, x, c, wg, wu, wd, wr, *held, *others)


def gate_up_kernel(x_ref, dgp_ref, dup_ref, gate_ref, up_ref, xt_ref):
    @pl.when(pl.program_id(0) == 0)
    def _():
        xt_ref[...] = x_ref[...].T

    gate_ref[...] = dot(xt_ref[...], dgp_ref[...]).astype(bf16)
    up_ref[...] = dot(xt_ref[...], dup_ref[...]).astype(bf16)


def gate_up_grads(x, dgp, dup, others=()):
    rows, width = x.shape
    hidden, wide = dgp.shape[1], 2 * TILE
    tile = pl.BlockSpec((rows, wide), lambda f: (0, f))
    out = pl.BlockSpec((width, wide), lambda f: (0, f))
    return pl.pallas_call(
        behind(gate_up_kernel, 3, others),
        grid=(hidden // wide,),
        in_specs=[pl.BlockSpec((rows, width), lambda f: (0, 0)), tile, tile] + anywhere(others),
        out_specs=[out, out],
        out_shape=[jax.ShapeDtypeStruct((width, hidden), bf16)] * 2,
        scratch_shapes=[pltpu.VMEM((width, rows), bf16)],
        compiler_params=pltpu.CompilerParams(vmem_limit_bytes=VMEM),
        cost_estimate=cost(26),
        name="gate_up_grads",
    )(x, dgp, dup, *others)


def down_kernel(act_ref, gcot_ref, wd_ref, gate_ref, down_ref, *refs):
    outs, acc_ref = refs[:-1], refs[-1]
    step = pl.program_id(0)
    act = act_ref[...]
    down_ref[...] = dot(act.T, gcot_ref[...]).astype(bf16)
    more = dot(act, wd_ref[0])

    @pl.when(step == 0)
    def _():
        acc_ref[...] = more

    @pl.when(step > 0)
    def _():
        acc_ref[...] += more

    @pl.when(step == pl.num_programs(0) - 1)
    def _():
        rows = outs[0].shape[0]
        for n, out in enumerate(outs):
            part = slice(n * rows, (n + 1) * rows)
            out[...] = (acc_ref[part, :] * gate_ref[part, :1]).astype(bf16)


def down_and_out(act, gcot, wd, gate, chunks, others=()):
    rows, hidden = act.shape
    width, wide = gcot.shape[1], 2 * TILE
    fixed = lambda r, c: pl.BlockSpec((r, c), lambda f: (0, 0))
    return pl.pallas_call(
        behind(down_kernel, 4, others),
        grid=(hidden // wide,),
        in_specs=[
            pl.BlockSpec((rows, wide), lambda f: (0, f)), fixed(rows, width),
            pl.BlockSpec((1, wide, width), lambda f: (0, f, 0)), fixed(rows, TILE),
        ] + anywhere(others),
        out_specs=[pl.BlockSpec((wide, width), lambda f: (f, 0))] + [fixed(rows // chunks, width)] * chunks,
        out_shape=[jax.ShapeDtypeStruct((hidden, width), bf16)]
        + [jax.ShapeDtypeStruct((rows // chunks, width), bf16)] * chunks,
        scratch_shapes=[pltpu.VMEM((rows, width), f32)],
        compiler_params=pltpu.CompilerParams(vmem_limit_bytes=VMEM),
        cost_estimate=cost(26),
        name="down_and_out",
    )(act, gcot, wd, gate, *others)


def norm_kernel(per_block, two_ref, one_ref, own_ref, gain_ref, out_ref, turned_ref):
    step = pl.program_id(0)

    def put(ref):
        x = ref[0].astype(f32)
        r = lax.rsqrt(jnp.mean(x * x, axis=-1, keepdims=True) + epsilon)
        normed = (x * r * gain_ref[...]).astype(bf16)
        out_ref[0] = normed
        turned_ref[...] = normed.T.reshape(turned_ref.shape)

    for n, ref in enumerate((two_ref, one_ref, own_ref)):
        pl.when(step // per_block == n)(functools.partial(put, ref))


def norm_window(two, one, own, gain, chips):
    pieces, rows, width = own.shape
    at = lambda n: pl.BlockSpec((1, rows, width), lambda f: (jnp.clip(f - n * pieces, 0, pieces - 1), 0, 0))
    return pl.pallas_call(
        functools.partial(norm_kernel, pieces),
        grid=(3 * pieces,),
        in_specs=[at(0), at(1), at(2), pl.BlockSpec((1, width), lambda f: (0, 0))],
        out_specs=[
            pl.BlockSpec((1, rows, width), lambda f: (f, 0, 0)),
            pl.BlockSpec((chips, 2, width // chips // 2, rows), lambda f: (0, 0, 0, f)),
        ],
        out_shape=[
            jax.ShapeDtypeStruct((3 * pieces, rows, width), bf16),
            jax.ShapeDtypeStruct((chips, 2, width // chips // 2, 3 * pieces * rows), bf16),
        ],
        compiler_params=pltpu.CompilerParams(vmem_limit_bytes=VMEM),
        cost_estimate=cost(10),
        name="norm_window",
    )(two, one, own, gain)


def slot_rows(t_ref, k, slot):
    index = lax.broadcasted_iota(jnp.int32, (slot, t_ref.shape[1]), 0) + k * slot
    return ((index == t_ref[0:1, :]) | (index == t_ref[1:2, :])).astype(bf16)


def row_slots(t_ref, k, slot):
    index = lax.broadcasted_iota(jnp.int32, (t_ref.shape[0], slot), 1) + k * slot
    return ((index == t_ref[:, 0:1]) | (index == t_ref[:, 1:2])).astype(bf16)


def collect(t_ref, refs):
    total = None
    for k, ref in enumerate(refs):
        part = dot(row_slots(t_ref, k, ref.shape[0]), ref[...])
        total = part if total is None else total + part
    return total


def turned(ref, z):
    return jnp.concatenate([ref[z ^ k] for k in range(ref.shape[0])], axis=0)


def call(kernel, ins, outs, us, name, others=(), scratch=()):
    specs = [SMEM if a.ndim == 1 else pl.BlockSpec(memory_space=pltpu.VMEM) for a in ins]
    return pl.pallas_call(
        behind(kernel, len(ins), others),
        in_specs=specs + anywhere(others),
        out_specs=[pl.BlockSpec(memory_space=pltpu.VMEM)] * len(outs),
        out_shape=[jax.ShapeDtypeStruct(shape, dtype) for shape, dtype in outs],
        scratch_shapes=list(scratch),
        compiler_params=pltpu.CompilerParams(vmem_limit_bytes=VMEM),
        cost_estimate=cost(us),
        name=name,
    )(*ins, *others)


def cot_kernel(ks, slot, z_ref, t_ref, cot_ref, *outs):
    values = turned(cot_ref, z_ref[0])
    for k, out in zip(ks, outs):
        out[...] = dot(slot_rows(t_ref, k, slot), values).astype(bf16)


def rows_kernel(ks, slot, t_ref, value_ref, *outs):
    for k, out in zip(ks, outs):
        out[...] = dot(slot_rows(t_ref, k, slot), value_ref[...]).astype(bf16)


def hidden_kernel(ks, slot, z_ref, t_ref, tok_ref, w_ref, gain_ref, *refs):
    pieces = tok_ref.shape[0]
    context, hidden_ref, moe_ref, outs = refs[:pieces], refs[pieces], refs[pieces + 1], refs[pieces + 2 :]
    left = jnp.concatenate([ref[...] for ref in context], axis=0)
    hidden = turned(tok_ref, z_ref[0]).astype(f32) + dot(left, w_ref[...])
    hidden_ref[...] = hidden
    moe_in = norm_rows(hidden, gain_ref[...]).astype(bf16)
    moe_ref[...] = moe_in
    for k, out in zip(ks, outs):
        out[...] = dot(slot_rows(t_ref, k, slot), moe_in).astype(bf16)


def middle_kernel(parts, z_ref, t_ref, hidden_ref, cot_ref, w_ref, gain_ref, *refs):
    pieces = cot_ref.shape[0]
    grad_ref, attn_ref, gain_grad_ref, outs = refs[pieces], refs[pieces + 1], refs[pieces + 2], refs[pieces + 3 :]
    grad_moe = collect(t_ref, refs[:pieces])
    grad_norm, gain_grad = norm_back(hidden_ref[...], gain_ref[...], grad_moe)
    gain_grad_ref[...] = gain_grad[None]
    grad = turned(cot_ref, z_ref[0]).astype(f32) + grad_norm
    grad_ref[...] = grad
    low = grad.astype(bf16)
    attn_ref[...] = low
    context = dot_nt(low, w_ref[...]).astype(bf16)
    rows, width = context.shape[0] // pieces, context.shape[1] // parts
    for n in range(parts):
        for k in range(pieces):
            outs[n * pieces + k][...] = context[k * rows : (k + 1) * rows, n * width : (n + 1) * width]


def mix_kernel(z_ref, t_ref, hidden_ref, *refs):
    out_ref = refs[-1]
    rows = out_ref.shape[1]
    mixed = (hidden_ref[...] + collect(t_ref, refs[:-1])).astype(bf16)
    for k in range(out_ref.shape[0]):
        out_ref[z_ref[0] ^ k] = mixed[k * rows : (k + 1) * rows]


def inputs_kernel(last, dq_ref, dk_ref, dv_ref, wq_ref, wk_ref, wv_ref, *refs):
    step = pl.program_id(0)
    flat = lambda ref: ref[...].reshape(-1, ref.shape[-1])
    grad = dot_nt(flat(dk_ref), wk_ref[...]) + dot_nt(flat(dv_ref), wv_ref[...])
    if not last:
        refs[0][...] = grad

        @pl.when(step == 2)
        def _():
            refs[0][...] = grad + dot_nt(flat(dq_ref), wq_ref[...])

        return
    acc_ref, normed_ref, two_ref, one_ref, own_ref, gain_ref = refs
    grad = grad + acc_ref[...]

    def gain(total):
        return jnp.sum(total * flat(normed_ref).astype(f32), axis=0, keepdims=True)

    @pl.when(step == 0)
    def _():
        two_ref[...] = grad.astype(bf16)
        gain_ref[...] = gain(grad)

    @pl.when(step == 1)
    def _():
        one_ref[...] = grad.astype(bf16)
        gain_ref[...] += gain(grad)

    @pl.when(step == 2)
    def _():
        total = grad + dot_nt(flat(dq_ref), wq_ref[...])
        own_ref[...] = total
        gain_ref[...] += gain(total)


def input_grads(part, dq, dk, dv, wq, wk, wv, acc=None, normed=None, others=()):
    pieces, rows, some = dq.shape
    width = wq.shape[0]
    block = pieces * rows
    window = pl.BlockSpec((pieces, rows, some), lambda f: (f, 0, 0))
    weight = pl.BlockSpec((width, some), lambda f: (0, part))
    once = pl.BlockSpec((block, width), lambda f: (0, 0))
    step = pl.BlockSpec((block, width), lambda f: (f, 0))
    specs = [pl.BlockSpec((pieces, rows, some), lambda f: (0, 0, 0)), window, window, weight, weight, weight]
    ins, outs = [dq, dk, dv, wq, wk, wv], [(step, (3 * block, width), f32)]
    if acc is not None:
        specs += [step, pl.BlockSpec((pieces, rows, width), lambda f: (f, 0, 0))]
        ins += [acc, normed]
        outs = [(once, (block, width), bf16)] * 2 + [(once, (block, width), f32)]
        outs += [(pl.BlockSpec((1, width), lambda f: (0, 0)), (1, width), f32)]
    return pl.pallas_call(
        behind(functools.partial(inputs_kernel, acc is not None), len(ins), others),
        grid=(3,),
        in_specs=specs + anywhere(others),
        out_specs=[o[0] for o in outs],
        out_shape=[jax.ShapeDtypeStruct(o[1], o[2]) for o in outs],
        compiler_params=pltpu.CompilerParams(vmem_limit_bytes=VMEM),
        cost_estimate=cost(7),
        name="input_grads",
    )(*ins, *others)


def tail_kernel(x_ref, sum_ref, swapped_ref, gain_ref, *refs):
    count = len(refs) // 2
    rows = x_ref.shape[1]
    for k in range(count):
        part = slice(k * rows, (k + 1) * rows)
        grad = sum_ref[part, :] + swapped_ref[part, :].astype(f32) + refs[k][...].astype(f32)
        refs[count + k][...] = norm_back(x_ref[k].astype(f32), gain_ref[...], grad)[0].astype(bf16)


def end_kernel(z_ref, grad_ref, *refs):
    out_ref = refs[-1]
    rows = out_ref.shape[1]
    for k in range(out_ref.shape[0]):
        out_ref[z_ref[0] ^ k] = (grad_ref[k * rows : (k + 1) * rows, :] + refs[k][...].astype(f32)).astype(bf16)


def projection_kernel(third, small, s_ref, nt_ref, dq_ref, dk_ref, dv_ref, *refs):
    other_ref, mine_ref = refs[-2:]
    step = pl.program_id(0)
    keys = nt_ref.shape[3]
    own = dq_ref.shape[0]

    def put(grad_ref, first):
        for where, ref in ((1 - s_ref[0], other_ref), (s_ref[0], mine_ref)):
            left = nt_ref[:, where, :, first:].reshape(-1, keys - first)
            ref[...] = dot(left, grad_ref[...]).astype(bf16).reshape(ref.shape)

    @pl.when(step < third)
    def _():
        put(dq_ref, keys - own)

    @pl.when((step >= third) & (step < 2 * third))
    def _():
        put(dk_ref, 0)

    @pl.when((step >= 2 * third) & (step < 3 * third))
    def _():
        put(dv_ref, 0)

    if small:

        @pl.when(step == 3 * third)
        def _():
            other_ref[...] = refs[0][:, 1 - s_ref[0]]
            mine_ref[...] = refs[0][:, s_ref[0]]


def projection_grads(side, normed_t, dq, dk, dv, small=(), others=()):
    chips, _, rows, keys = normed_t.shape
    own, width = dq.shape
    wide = 2 * TILE
    third = width // wide
    at = lambda j: (lambda f: (0, jnp.clip(f - j * third, 0, third - 1)))
    out = pl.BlockSpec((chips, rows, wide), lambda f: (0, 0, f))
    shape = jax.ShapeDtypeStruct((chips, rows, 3 * width + wide * len(small)), bf16)
    return pl.pallas_call(
        behind(functools.partial(projection_kernel, third, len(small)), 5 + len(small), others),
        grid=(3 * third + len(small),),
        in_specs=[
            SMEM,
            pl.BlockSpec((chips, 2, rows, keys), lambda f: (0, 0, 0, 0)),
            pl.BlockSpec((own, wide), at(0)),
            pl.BlockSpec((keys, wide), at(1)),
            pl.BlockSpec((keys, wide), at(2)),
        ] + [pl.BlockSpec((chips, 2, rows, wide), lambda f: (0, 0, 0, 0))] * len(small) + anywhere(others),
        out_specs=[out, out],
        out_shape=[shape, shape],
        compiler_params=pltpu.CompilerParams(vmem_limit_bytes=VMEM),
        cost_estimate=cost(9.3),
        name="projection_grads",
    )(side, normed_t, dq, dk, dv, *small, *others)


def shift(x, by):
    count = lax.axis_size("ctx")
    return lax.ppermute(x, "ctx", [(i, i + by) for i in range(count) if 0 <= i + by < count])


def core_swap(x):
    return lax.ppermute(x, "ctx", [(i, i ^ 1) for i in range(lax.axis_size("ctx"))])


def z_swap(x, k):
    if k == 0:
        return x
    return lax.ppermute(x, "exp", [(i, i ^ k) for i in range(lax.axis_size("exp"))])


def sum_over_chips(pair):
    chips = pair.shape[0]
    count = lax.axis_size("ctx")
    if chips > 4 or chips & (chips - 1):
        groups = [list(range(core, count, 2)) for core in range(2)]
        got = lax.all_to_all(pair, "ctx", split_axis=0, concat_axis=0, tiled=True, axis_index_groups=groups)
        return jnp.sum(got.astype(f32), axis=0)
    chip = lax.axis_index("ctx") // 2
    total = None
    for d in range(chips - 1, -1, -1):
        block = lax.dynamic_index_in_dim(pair, chip ^ d, 0, keepdims=False)
        if d:
            block = lax.ppermute(block, "ctx", [(i, i ^ (2 * d)) for i in range(count)])
        total = block.astype(f32) if total is None else total + block.astype(f32)
    return total


def sum_over_ctx(partial):
    count = lax.axis_size("ctx")
    rows, width = partial.shape
    side = lax.axis_index("ctx") % 2
    parts = partial.reshape(count // 2, 2, rows // count, width)
    other = core_swap(lax.dynamic_index_in_dim(parts, 1 - side, 1, keepdims=False))
    mine = lax.dynamic_index_in_dim(parts, side, 1, keepdims=False)
    return sum_over_chips((mine.astype(f32) + other.astype(f32)).astype(bf16))


def sum_over_exp(partial):
    count = lax.axis_size("exp")
    z = lax.axis_index("exp")
    parts = partial.reshape(count, -1, partial.shape[-1])
    total = None
    for k in range(count - 1, -1, -1):
        block = z_swap(lax.dynamic_index_in_dim(parts, z ^ k, 0, keepdims=False), k).astype(f32)
        total = block if total is None else total + block
    return total


def sum_over_all(partial):
    return sum_over_exp(sum_over_ctx(partial).astype(bf16))


def norm_rows(values, gain):
    return values * lax.rsqrt(jnp.mean(values * values, axis=-1, keepdims=True) + epsilon) * gain


def norm_back(values, gain, grad):
    r = lax.rsqrt(jnp.mean(values * values, axis=-1, keepdims=True) + epsilon)
    u = grad * gain
    inner = jnp.mean(values * u, axis=-1, keepdims=True)
    return r * u - values * (r * r * r) * inner, jnp.sum(grad * values * r, axis=0)


def on_device(
    tokens, doc_lengths, routes, priority, norm1_gain, w_query, w_key, w_value, w_out, bias_table,
    norm2_gain, w_router, w_gate, w_up, w_down, cotangent,
):
    seqs, piece_len, width = tokens.shape
    exp_count = lax.axis_size("exp")
    ctx_count = lax.axis_size("ctx")
    device_count = exp_count * ctx_count
    block_len = piece_len * exp_count
    rows = seqs * piece_len
    heads = bias_table.shape[0] // bucket_total
    experts = w_router.shape[1]
    slot = 5 * rows // (2 * experts)
    slots = experts * slot
    ctx = lax.axis_index("ctx")
    exp = lax.axis_index("exp")
    side = ctx % 2

    z = jnp.reshape(exp, (1,))
    far_first = [2, 3, 1]

    turn = jnp.arange(seqs, dtype=jnp.int32) ^ exp
    pick = lambda array, k: lax.dynamic_index_in_dim(array, exp ^ k, 0, keepdims=False)

    x_own = [None] * seqs
    for k in [0, 2, 3, 1]:
        x_own[k] = z_swap(pick(tokens, k), k)
    x_pieces = x_own
    x_two = [shift(piece, 2) for piece in x_own]
    x_own, x_two = jnp.stack(x_own), jnp.stack(x_two)
    x_one = core_swap(jnp.where(side == 0, x_own, x_two))

    route_rows = jnp.take(routes, turn, axis=0).reshape(rows, 2)
    order = jnp.take(priority, turn, axis=0).reshape(rows)
    earlier = order[None, :] < order[:, None]
    r0, r1 = route_rows[:, 0], route_rows[:, 1]
    place0 = jnp.sum((earlier & (r0[None, :] == r0[:, None])).astype(jnp.int32), axis=1)
    place1 = jnp.sum((earlier & (r1[None, :] == r1[:, None])).astype(jnp.int32), axis=1) + jnp.sum(
        (r0[None, :] == r1[:, None]).astype(jnp.int32), axis=1
    )
    target0 = jnp.where(place0 < slot, (r0 ^ exp) * slot + place0, -1)
    target1 = jnp.where(place1 < slot, (r1 ^ exp) * slot + place1, -1)
    targets = jnp.stack([target0, target1])
    targets_t = targets.T
    slot_shape = ((slot, width), bf16)
    sent = call(
        functools.partial(cot_kernel, far_first + [0], slot), [z, targets, cotangent], [slot_shape] * experts, 4, "cot_rows", x_pieces[1:]
    )
    cot_slots = [None] * experts
    for k, rows_k in zip(far_first + [0], sent):
        cot_slots[k] = z_swap(rows_k, k)

    distance = np.arange(-TILE, WINDOW + TILE)
    seen = (distance >= 0) & (distance < WINDOW)
    hot = (bucket_of(np.clip(distance, 0, None))[None, :] == np.arange(bucket_total)[:, None]) & seen[None, :]
    vec = exact_dot(bias_table.astype(f32).reshape(heads, bucket_total), jnp.asarray(hot, f32))
    vec = jnp.where(jnp.asarray(seen)[None, :], vec, NEG).reshape(heads // 2, 2, -1)
    bias = bias_tiles(vec)

    ends = jnp.cumsum(lax.dynamic_index_in_dim(doc_lengths, exp, 0, keepdims=False))
    piece_start = ctx * block_len + turn[:, None] * piece_len
    q_pos = piece_start + jnp.arange(piece_len, dtype=jnp.int32)[None, :]
    start = jnp.max(jnp.where(ends <= q_pos[..., None], ends, 0), axis=2)
    lo = start - (ctx - 2) * block_len
    lo = jnp.broadcast_to(lo[:, None, None, :], (seqs, 1, 2, TILE)).reshape(seqs, 1, 2 * TILE)

    gain_one = norm1_gain.astype(f32)
    normed, normed_t = norm_window(x_two, x_one, x_own, gain_one[None], ctx_count // 2)
    normed = normed.reshape(-1, width)
    normed_own = normed[2 * block_len :]
    q = (dot(normed_own, w_query).astype(bf16) * 0.125).astype(bf16).reshape(seqs, piece_len, width)
    k_win = dot(normed, w_key).astype(bf16).reshape(-1, TILE, width)
    v_win = dot(normed, w_value).astype(bf16).reshape(-1, TILE, width)
    contexts, lses, context_rows = [None] * seqs, [], [None] * seqs
    for first in (2, 0):
        others = [contexts[2], cot_slots[3], cot_slots[1]] if first == 0 else [cot_slots[2]]
        *c, l = attend((first, first + 1), z, lo[first : first + 2], q[first : first + 2], k_win, v_win, bias, others)
        lses.insert(0, l)
        for k in (first, first + 1):
            contexts[k] = c[k - first]
            context_rows[k] = z_swap(contexts[k], k)
    router_wide = jnp.pad(w_router, ((0, 0), (0, TILE - experts)))
    gain_two = norm2_gain.astype(f32)[None]
    hidden, moe_in, *sent = call(
        functools.partial(hidden_kernel, [2, 0], slot),
        [z, targets, tokens, w_out, gain_two] + context_rows,
        [((rows, width), f32), ((rows, width), bf16), slot_shape, slot_shape], 9, "hidden_rows",
    )
    inputs = [sent[1], None, z_swap(sent[0], 2), None]
    held, returned, turns = None, [None] * experts, [0, 2, 1, 3]
    for i, k in enumerate(turns):
        back, *held = expert(k, experts, held, z, inputs[k], cot_slots[k], w_gate, w_up, w_down, router_wide, experts)
        returned[k] = z_swap(back, k)
        if i == 0:
            sent = call(functools.partial(rows_kernel, [3, 1], slot), [targets, moe_in], [slot_shape] * 2, 3, "moe_rows", [back])
            inputs[3], inputs[1] = z_swap(sent[0], 3), z_swap(sent[1], 1)
    all_inputs, act_low, grad_gate_pre, grad_up_pre, grad_out_slots, gate, grad_logits = held
    grad_logits = grad_logits[:, :experts]
    scatter = lambda partial: lax.psum_scatter(partial, "ctx", scatter_dimension=0, tiled=True).astype(f32)
    gate_part, up_part = gate_up_grads(all_inputs, grad_gate_pre, grad_up_pre, [returned[turns[1]], returned[turns[2]]])
    grad_gate, grad_up = scatter(gate_part), scatter(up_part)

    part_count = 2
    part_width = width // part_count
    grad_hidden, grad_attn, grad_gain_two, *sent_back = call(
        functools.partial(middle_kernel, part_count),
        [z, targets_t, hidden, cotangent, w_out, gain_two] + returned,
        [((rows, width), f32), ((rows, width), bf16), ((1, width), f32)] + [((piece_len, part_width), bf16)] * (seqs * part_count),
        12, "middle_rows", [gate_part],
    )
    arrived = [[z_swap(sent_back[n * seqs + k], k) for k in range(seqs)] for n in range(part_count)]
    down_part, *produced = down_and_out(act_low, grad_out_slots, w_down, gate, experts, [sent_back[-1]])
    grad_down = scatter(down_part)
    grad_out = sum_over_ctx(dot_tn(jnp.concatenate(context_rows), grad_attn).astype(bf16)).astype(bf16)
    grad_router_part = lax.dot_general(
        all_inputs.astype(f32), grad_logits, (((0,), (0,)), ((), ())),
        precision=lax.Precision.HIGHEST, preferred_element_type=f32,
    )
    given = [z_swap(produced[k], k) for k in range(experts)]

    side_ref = jnp.reshape(side, (1,))
    weights = (w_query, w_key, w_value)
    flat = lambda grads: [grad.reshape(-1, part_width) for grad in grads]
    back = lambda n, others: attend_back(n, part_count, z, lo, lses, q, k_win, v_win, bias, contexts, arrived[n], others)
    *grads, diagonal = back(0, [down_part] + arrived[1])
    other, mine = projection_grads(side_ref, normed_t, *flat(grads), (), [given[2], given[1]])
    first_pair = (mine.astype(f32) + core_swap(other).astype(f32)).astype(bf16)
    first_sum = sum_over_chips(first_pair).astype(bf16)
    acc = input_grads(0, *grads, *weights, others=[other])[0]
    *grads, more = back(1, [acc, grad_out, first_pair])
    part_two, part_one, own_sum, gain_part = input_grads(1, *grads, *weights, acc, normed.reshape(-1, piece_len, width), [first_sum])
    grad_gain_one = gain_part / gain_one
    diagonals = jnp.concatenate([diagonal, more])
    places = np.arange((TILES_SEEN) * 2 * TILE).reshape(TILES_SEEN, 2 * TILE)
    block, lane = places // (2 * TILE), places % (2 * TILE)
    where_dist = lane - TILE + (TILES_SEEN - 1 - block) * TILE
    ok = (where_dist >= 0) & (where_dist < WINDOW)
    to_bucket = (bucket_of(np.clip(where_dist, 0, None))[..., None] == np.arange(bucket_total)) & ok[..., None]
    table_part = exact_dot(diagonals.reshape(heads, -1), jnp.asarray(to_bucket.reshape(-1, bucket_total), f32))
    small = [
        grad_gain_one.reshape(device_count, -1),
        grad_gain_two.reshape(device_count, -1),
        table_part.reshape(device_count, -1),
        grad_router_part.reshape(device_count, -1),
    ]
    cuts = np.cumsum([0] + [item.shape[1] for item in small])
    packed = jnp.concatenate(small, axis=1)
    share = width // device_count
    packed = jnp.pad(packed, ((0, 0), (0, -packed.shape[1] % share))).reshape(width, -1)
    packed = jnp.pad(packed.astype(bf16), ((0, 0), (0, 2 * TILE - packed.shape[1])))
    packed = packed.reshape(ctx_count // 2, 2, -1, 2 * TILE)
    other, mine = projection_grads(side_ref, normed_t, *flat(grads), [packed])
    pair = (mine.astype(f32) + core_swap(other).astype(f32)).astype(bf16)
    last_sum = sum_over_chips(pair).astype(bf16)
    swapped = core_swap(part_one)
    leave = jnp.where(side == 0, part_two.astype(f32), part_two.astype(f32) + swapped.astype(f32)).astype(bf16)
    swapped = jnp.where(side == 0, swapped, jnp.zeros_like(swapped))
    came = [shift(leave[k * piece_len : (k + 1) * piece_len], -2) for k in range(seqs)]
    mixed = call(
        mix_kernel, [z, targets_t, hidden] + given, [((seqs, piece_len, width), bf16)], 8, "mixed_rows", [leave, pair]
    )[0]
    pieces = call(
        tail_kernel, [x_own, own_sum, swapped, gain_one[None]] + came, [((piece_len, width), bf16)] * seqs, 6, "tail_rows", [mixed, last_sum]
    )
    pieces = [z_swap(piece, k) for k, piece in enumerate(pieces)]
    grad_tokens = call(end_kernel, [z, grad_hidden] + pieces, [((seqs, piece_len, width), bf16)], 4, "end_rows")[0]
    dense = sum_over_exp(jnp.concatenate([grad_out, first_sum, last_sum], axis=1))
    grad_out = dense[:, :width]
    parts = [dense[:, width + i * part_width : width + (i + 1) * part_width] for i in range(3 * part_count)]
    grad_query, grad_key, grad_value = [jnp.concatenate(parts[i::3], axis=1) for i in range(3)]
    packed = dense[:, 4 * width :].reshape(-1, 2 * TILE)[:, : -(-cuts[-1] // share)].reshape(-1)
    norm1_out, norm2_out, table_out, router_out = [packed[cuts[i] : cuts[i + 1]] for i in range(4)]
    return (
        mixed, grad_tokens, norm1_out, grad_query, grad_key, grad_value, grad_out, table_out, norm2_out,
        router_out.reshape(-1, experts), grad_gate[None], grad_up[None], grad_down[None],
    )


def solution(mesh):
    rows = P(None, ("ctx", "exp"), None)
    flat = P(("ctx", "exp"))
    in_specs = (
        rows, P(), rows, P(None, ("ctx", "exp")), P(), P(), P(), P(), P(), P(), P(), P(),
        P("exp", None, None), P("exp", None, None), P("exp", None, None), rows,
    )
    out_specs = (
        rows, rows, flat, P(("ctx", "exp"), None), P(("ctx", "exp"), None), P(("ctx", "exp"), None),
        P(("ctx", "exp"), None), flat, flat, P(("ctx", "exp"), None),
        P("exp", "ctx", None), P("exp", "ctx", None), P("exp", "ctx", None),
    )
    return jax.shard_map(on_device, mesh=mesh, in_specs=in_specs, out_specs=out_specs, check_vma=False)
```

```python
import functools

import jax
import jax.numpy as jnp
import numpy as np
from jax import lax
from jax.experimental import pallas as pl
from jax.experimental.pallas import tpu as pltpu
from jax.sharding import PartitionSpec as P

WINDOW = 1024
TILE = 128
TILES_SEEN = WINDOW // TILE + 1
epsilon = 1e-06
bucket_total = 32
NEG = -1e30
f32 = jnp.float32
bf16 = jnp.bfloat16
VMEM = 56 * 1024 * 1024


def cost(us):
    return pl.CostEstimate(flops=int(us * 1.15e9), bytes_accessed=0, transcendentals=0)


def behind(kernel, inputs, others):
    return lambda *refs: kernel(*refs[:inputs], *refs[inputs + len(others) :])


def anywhere(others):
    return [pl.BlockSpec(memory_space=pl.ANY)] * len(others)


def dot(left, right):
    return jnp.dot(left, right, preferred_element_type=f32)


def dot_nt(left, right):
    return lax.dot_general(left, right, (((1,), (1,)), ((), ())), preferred_element_type=f32)


def dot_tn(left, right):
    return lax.dot_general(left, right, (((0,), (0,)), ((), ())), preferred_element_type=f32)


def exact_dot(left, right):
    return jnp.dot(left, right, precision=lax.Precision.HIGHEST, preferred_element_type=f32)


def bucket_of(distance):
    limits = np.ceil(16.0 * 8.0 ** (np.arange(1, 16) / 16.0)).astype(np.int32)
    above = np.sum(distance[..., None] >= limits, axis=-1)
    return np.where(distance < 16, distance, 16 + above)


def bias_kernel(vec_ref, out_ref):
    for a in range(TILES_SEEN):
        first = (TILES_SEEN - 1 - a) * TILE
        for h in range(2):
            row = vec_ref[0, h : h + 1, first : first + 2 * TILE]
            wide = jnp.broadcast_to(row, (TILE, 2 * TILE))
            rolled = pltpu.roll(wide, TILE, 1, stride=1, stride_axis=0)
            out_ref[0, a, :, h * TILE : (h + 1) * TILE] = rolled[:, :TILE].astype(bf16)


def split_heads(x):
    lane = lax.broadcasted_iota(jnp.int32, x.shape, 1)
    zero = jnp.zeros_like(x)
    return jnp.concatenate([jnp.where(lane < 64, x, zero), jnp.where(lane < 64, zero, x)], axis=0)


def merge_heads(xt):
    return jnp.concatenate([xt[:64, :TILE], xt[64:, TILE:]], axis=0).T


def key_block(kb, z):
    return (kb // 4) * 4 + ((kb % 4) ^ z)


def attend_kernel(ks, z_ref, lo_ref, q_ref, k_ref, v_ref, b_ref, *refs):
    outs, (lse_ref, s_ref, p_ref, v_s) = refs[: len(ks)], refs[len(ks) :]
    z = z_ref[0]
    row = lax.broadcasted_iota(jnp.int32, (TILE, 2 * TILE), 0)
    for n, k in enumerate(ks):
        t = z ^ k
        q2 = split_heads(q_ref[n])
        lo = lo_ref[n] - t * TILE
        top = jnp.full((8, 2 * TILE), NEG, f32)
        for a in range(TILES_SEEN):
            at = key_block(t + a, z)
            v_s[a * TILE : (a + 1) * TILE, :] = v_ref[at]
            s = dot_nt(k_ref[at], q2) + b_ref[0, a].astype(f32)
            s = jnp.where(row >= lo - a * TILE, s, NEG)
            s_ref[a] = s
            top = jnp.maximum(top, jnp.max(s.reshape(TILE // 8, 8, 2 * TILE), axis=0))
        top = jnp.max(top, axis=0, keepdims=True)
        total = jnp.zeros((8, 2 * TILE), f32)
        for a in range(TILES_SEEN):
            p = jnp.exp(s_ref[a] - top)
            total = total + jnp.sum(p.reshape(TILE // 8, 8, 2 * TILE), axis=0)
            p_ref[a * TILE : (a + 1) * TILE, :] = p.astype(bf16)
        total = jnp.sum(total, axis=0, keepdims=True)
        ct = dot(v_s[...].T, p_ref[...]) / total
        outs[n][...] = merge_heads(ct).astype(bf16)
        lse_ref[0, n] = top + jnp.log(total)


def attend_back_kernel(pieces, z_ref, lo_ref, lse_a, lse_b, q_ref, k_ref, v_ref, b_ref, *refs):
    o_refs, do_refs = refs[:pieces], refs[pieces : 2 * pieces]
    dq_ref, dk_ref, dv_ref, tab_ref, q2_ref, do2_ref, ds_ref, p_ref, acc_ref, row_ref, k_s = refs[2 * pieces :]
    z = z_ref[0]
    row = lax.broadcasted_iota(jnp.int32, (TILE, 2 * TILE), 0)
    for k in range(pieces):
        both = pl.ds(pl.multiple_of((z ^ k) * 2 * TILE, 2 * TILE), 2 * TILE)
        out, grad = o_refs[k][...], do_refs[k][...]
        q2_ref[both, :] = split_heads(q_ref[k])
        do2_ref[both, :] = split_heads(grad)
        prod = (grad.astype(f32) * out.astype(f32)).T
        lse_ref = lse_a if k < pieces // 2 else lse_b
        row_ref[0:1, both] = lse_ref[0, k % (pieces // 2)]
        row_ref[1:2, both] = jnp.concatenate(
            [jnp.sum(prod[:64], axis=0, keepdims=True), jnp.sum(prod[64:], axis=0, keepdims=True)], axis=1
        )
    acc_ref[...] = jnp.zeros_like(acc_ref)
    keys = pieces + TILES_SEEN - 1
    for kb in range(keys):
        first, last = max(0, kb - TILES_SEEN + 1), min(pieces - 1, kb)
        krows = slice(kb * TILE, (kb + 1) * TILE)
        cols = slice(first * 2 * TILE, (last + 1) * 2 * TILE)
        at = key_block(kb, z)
        key, value = k_ref[at], v_ref[at]
        k_s[krows, :] = key
        for t in range(first, last + 1):
            both = slice(t * 2 * TILE, (t + 1) * 2 * TILE)
            a = kb - t
            s = dot_nt(key, q2_ref[both, :]) + b_ref[0, a].astype(f32)
            s = jnp.where(row >= lo_ref[z ^ t] - kb * TILE, s, NEG)
            p = jnp.exp(s - row_ref[0:1, both])
            dp = dot_nt(value, do2_ref[both, :])
            ds = p * (dp - row_ref[1:2, both])
            acc_ref[a] += ds
            p_ref[:, both] = p.astype(bf16)
            ds_ref[krows, both] = ds.astype(bf16)
        dk_ref[at] = dot(ds_ref[krows, cols], q2_ref[cols, :]).astype(bf16)
        dv_ref[at] = dot(p_ref[:, cols], do2_ref[cols, :]).astype(bf16)
    kt = k_s[...].T
    for t in range(pieces):
        both = slice(t * 2 * TILE, (t + 1) * 2 * TILE)
        span = slice(t * TILE, (t + TILES_SEEN) * TILE)
        dqt = dot(kt[:, span], ds_ref[span, both]) * 0.125
        dq_ref[z ^ t] = merge_heads(dqt).astype(bf16)
    for a in range(TILES_SEEN):
        for h in range(2):
            part = acc_ref[a, :, h * TILE : (h + 1) * TILE]
            part = jnp.concatenate([part, jnp.zeros_like(part)], axis=1)
            half = TILE // 2
            while half >= 1:
                part = part[:half] + pltpu.roll(part[half:], 2 * TILE - half, 1)
                half //= 2
            tab_ref[0, h, a : a + 1, :] = pltpu.roll(part, TILE, 1)


def bias_tiles(vec, others=()):
    pairs = vec.shape[0]
    return pl.pallas_call(
        behind(bias_kernel, 1, others),
        grid=(pairs,),
        in_specs=[pl.BlockSpec((1, 2, vec.shape[2]), lambda g: (g, 0, 0))] + anywhere(others),
        out_specs=pl.BlockSpec((1, TILES_SEEN, TILE, 2 * TILE), lambda g: (g, 0, 0, 0)),
        out_shape=jax.ShapeDtypeStruct((pairs, TILES_SEEN, TILE, 2 * TILE), bf16),
        compiler_params=pltpu.CompilerParams(vmem_limit_bytes=VMEM),
        cost_estimate=cost(6),
        name="bias_tiles",
    )(vec, *others)


SMEM = pl.BlockSpec(memory_space=pltpu.SMEM)


def attend(ks, z, lo, q, k, v, bias, others=()):
    count, _, width = q.shape
    blocks, pairs = k.shape[0], width // TILE
    part = lambda n: pl.BlockSpec((n, TILE, TILE), lambda g: (0, 0, g))
    return pl.pallas_call(
        behind(functools.partial(attend_kernel, ks), 6, others),
        grid=(pairs,),
        in_specs=[
            SMEM,
            pl.BlockSpec((count, 1, 2 * TILE), lambda g: (0, 0, 0)),
            part(count), part(blocks), part(blocks),
            pl.BlockSpec((1, TILES_SEEN, TILE, 2 * TILE), lambda g: (g, 0, 0, 0)),
        ] + anywhere(others),
        out_specs=[pl.BlockSpec((TILE, TILE), lambda g: (0, g))] * count
        + [pl.BlockSpec((1, count, 1, 2 * TILE), lambda g: (g, 0, 0, 0))],
        out_shape=[jax.ShapeDtypeStruct((TILE, width), bf16)] * count
        + [
            jax.ShapeDtypeStruct((pairs, count, 1, 2 * TILE), f32),
        ],
        scratch_shapes=[
            pltpu.VMEM((TILES_SEEN, TILE, 2 * TILE), f32),
            pltpu.VMEM((TILES_SEEN * TILE, 2 * TILE), bf16),
            pltpu.VMEM((TILES_SEEN * TILE, TILE), bf16),
        ],
        compiler_params=pltpu.CompilerParams(vmem_limit_bytes=VMEM),
        cost_estimate=cost(7.4 * count),
        name="attend",
    )(z, lo, q, k, v, bias, *others)


def attend_back(part_index, part_count, z, lo, lses, q, k, v, bias, o, do, others=()):
    pieces, _, width = q.shape
    blocks, pairs = k.shape[0], width // TILE // part_count
    base = part_index * pairs
    part = lambda n: pl.BlockSpec((n, TILE, TILE), lambda g: (0, 0, base + g))
    alone = lambda n: pl.BlockSpec((n, TILE, TILE), lambda g: (0, 0, g))
    columns = pieces * 2 * TILE
    return pl.pallas_call(
        behind(functools.partial(attend_back_kernel, pieces), 8 + 2 * pieces, others),
        grid=(pairs,),
        in_specs=[
            SMEM,
            pl.BlockSpec((pieces, 1, 2 * TILE), lambda g: (0, 0, 0)),
            pl.BlockSpec((1, pieces // 2, 1, 2 * TILE), lambda g: (base + g, 0, 0, 0)),
            pl.BlockSpec((1, pieces // 2, 1, 2 * TILE), lambda g: (base + g, 0, 0, 0)),
            part(pieces), part(blocks), part(blocks),
            pl.BlockSpec((1, TILES_SEEN, TILE, 2 * TILE), lambda g: (base + g, 0, 0, 0)),
        ]
        + [pl.BlockSpec((TILE, TILE), lambda g: (0, base + g))] * pieces
        + [pl.BlockSpec((TILE, TILE), lambda g: (0, base + g))] * pieces
        + anywhere(others),
        out_specs=[
            alone(pieces), alone(blocks), alone(blocks),
            pl.BlockSpec((1, 2, TILES_SEEN, 2 * TILE), lambda g: (g, 0, 0, 0)),
        ],
        out_shape=[
            jax.ShapeDtypeStruct((pieces, TILE, width // part_count), bf16),
            jax.ShapeDtypeStruct((blocks, TILE, width // part_count), bf16),
            jax.ShapeDtypeStruct((blocks, TILE, width // part_count), bf16),
            jax.ShapeDtypeStruct((pairs, 2, TILES_SEEN, 2 * TILE), f32),
        ],
        scratch_shapes=[
            pltpu.VMEM((columns, TILE), bf16),
            pltpu.VMEM((columns, TILE), bf16),
            pltpu.VMEM((blocks * TILE, columns), bf16),
            pltpu.VMEM((TILE, columns), bf16),
            pltpu.VMEM((TILES_SEEN, TILE, 2 * TILE), f32),
            pltpu.VMEM((8, columns), f32),
            pltpu.VMEM((blocks * TILE, TILE), bf16),
        ],
        compiler_params=pltpu.CompilerParams(vmem_limit_bytes=VMEM),
        cost_estimate=cost(42 / part_count),
        name="attend_back",
    )(z, lo, *lses, q, k, v, bias, *o, *do, *others)


def gelu_parts(v):
    c = np.float32(np.sqrt(2.0 / np.pi))
    t = jnp.tanh(c * (v + 0.044715 * v * v * v))
    half = 0.5 * (1.0 + t)
    return v * half, half + 0.5 * v * (1.0 - t * t) * (c * (1.0 + 3.0 * 0.044715 * v * v))


def expert_kernel(experts, count, held, z_ref, *refs):
    x_refs, c_refs, (wg_ref, wu_ref, wd_ref, wr_ref) = refs[:count], refs[count : 2 * count], refs[2 * count : 2 * count + 4]
    refs = refs[2 * count + 4 + held :]
    gin_refs, refs = refs[:count], refs[count:]
    kept_ref, act_ref, dgp_ref, dup_ref, gcot_ref, gate_out, glog_ref, acc_ref, gg_ref, rp_ref, gate_ref, xs_ref, cs_ref = refs
    step = pl.program_id(0)
    rows = xs_ref.shape[0]
    lane = lax.broadcasted_iota(jnp.int32, (rows, TILE), 1)

    @pl.when(step == 0)
    def _():
        for n in range(count):
            part = slice(n * rows // count, (n + 1) * rows // count)
            xs_ref[part, :] = x_refs[n][...]
            cs_ref[part, :] = c_refs[n][...]
        x = xs_ref[...]
        logits = jnp.where(lane < experts, dot(x, wr_ref[...]), NEG)
        e = jnp.exp(logits - jnp.max(logits, axis=1, keepdims=True))
        probs = e / jnp.sum(e, axis=1, keepdims=True)
        rp_ref[...] = probs
        gate = jnp.sum(jnp.where(lane == z_ref[0], probs, 0.0), axis=1, keepdims=True)
        gate_ref[...] = jnp.broadcast_to(gate, gate_ref.shape)
        gate_out[...] = gate_ref[...]
        kept_ref[...] = x
        gcot_ref[...] = (gate * cs_ref[...].astype(f32)).astype(bf16)
        acc_ref[...] = jnp.zeros_like(acc_ref)
        gg_ref[...] = jnp.zeros_like(gg_ref)

    x, c = xs_ref[...], cs_ref[...]
    raw = dot_nt(c, wd_ref[0])
    gate_pre = dot(x, wg_ref[0])
    up_pre = dot(x, wu_ref[0])
    gelu, slope = gelu_parts(gate_pre)
    act = gelu * up_pre
    act_ref[...] = act.astype(bf16)
    prod = act * raw
    gg_ref[...] += prod[:, :TILE] + prod[:, TILE:]
    scaled = raw * gate_ref[:, :1]
    dgp = (scaled * up_pre * slope).astype(bf16)
    dup = (scaled * gelu).astype(bf16)
    dgp_ref[...] = dgp
    dup_ref[...] = dup
    acc_ref[...] += dot_nt(dgp, wg_ref[0]) + dot_nt(dup, wu_ref[0])

    @pl.when(step == pl.num_programs(0) - 1)
    def _():
        gg = jnp.sum(gg_ref[...], axis=1, keepdims=True)
        own = jnp.where(lane == z_ref[0], 1.0, 0.0)
        glog = gg * rp_ref[...] * (own - gate_ref[...])
        glog_ref[...] = glog
        high = glog.astype(bf16)
        low = (glog - high.astype(f32)).astype(bf16)
        gin = (acc_ref[...] + dot_nt(high, wr_ref[...]) + dot_nt(low, wr_ref[...])).astype(bf16)
        for n in range(count):
            gin_refs[n][...] = gin[n * rows // count : (n + 1) * rows // count]


def expert(index, total, held, z, xs, cs, wg, wu, wd, wr, experts, others=()):
    count, (slot, width) = len(xs), xs[0].shape
    rows = count * slot
    hidden = wg.shape[2]
    wide = 2 * TILE
    whole = pl.BlockSpec((slot, width), lambda f: (0, 0))
    kept = pl.BlockSpec((rows, width), lambda f: (index, 0))
    thin = pl.BlockSpec((rows, TILE), lambda f: (index, 0))
    tile = pl.BlockSpec((rows, wide), lambda f: (index, f))
    full = lambda n, t: jax.ShapeDtypeStruct((total * slot, n), t)
    held = [] if held is None else list(held)
    return pl.pallas_call(
        functools.partial(expert_kernel, experts, count, len(held) + len(others)),
        grid=(hidden // wide,),
        in_specs=[SMEM] + [whole] * (2 * count) + [
            pl.BlockSpec((1, width, wide), lambda f: (0, 0, f)),
            pl.BlockSpec((1, width, wide), lambda f: (0, 0, f)),
            pl.BlockSpec((1, wide, width), lambda f: (0, f, 0)),
            pl.BlockSpec((width, TILE), lambda f: (0, 0)),
        ] + anywhere(held) + anywhere(others),
        out_specs=[whole] * count + [kept, tile, tile, tile, kept, thin, thin],
        out_shape=[jax.ShapeDtypeStruct((slot, width), bf16)] * count + [
            full(width, bf16), full(hidden, bf16), full(hidden, bf16), full(hidden, bf16), full(width, bf16),
            full(TILE, f32), full(TILE, f32),
        ],
        input_output_aliases={2 * count + 5 + i: count + i for i in range(len(held))},
        scratch_shapes=[
            pltpu.VMEM((rows, width), f32), pltpu.VMEM((rows, TILE), f32), pltpu.VMEM((rows, TILE), f32),
            pltpu.VMEM((rows, TILE), f32), pltpu.VMEM((rows, width), bf16), pltpu.VMEM((rows, width), bf16),
        ],
        compiler_params=pltpu.CompilerParams(vmem_limit_bytes=VMEM),
        cost_estimate=cost(10 + 13 * count),
        name="expert",
    )(z, *xs, *cs, wg, wu, wd, wr, *held, *others)


def gate_up_kernel(s_ref, x_ref, dgp_ref, dup_ref, glog_ref, other_ref, mine_ref, router_ref, xt_ref):
    @pl.when(pl.program_id(0) == 0)
    def _():
        xt_ref[...] = x_ref[...].T
        high = glog_ref[...].astype(bf16)
        low = (glog_ref[...] - high.astype(f32)).astype(bf16)
        router_ref[...] = dot(xt_ref[...], high) + dot(xt_ref[...], low)

    first = s_ref[0] == 0
    for n, ref in enumerate((dgp_ref, dup_ref)):
        result = dot(xt_ref[...], ref[...]).astype(bf16).reshape((other_ref.shape[0], 2) + other_ref.shape[2:])
        other_ref[:, n] = jnp.where(first, result[:, 1], result[:, 0])
        mine_ref[:, n] = jnp.where(first, result[:, 0], result[:, 1])


def gate_up_grads(side, chips, x, dgp, dup, glog, others=()):
    rows, width = x.shape
    hidden, wide = dgp.shape[1], 2 * TILE
    part = width // chips // 2
    tile = pl.BlockSpec((rows, wide), lambda f: (0, f))
    out = pl.BlockSpec((chips, 2, part, wide), lambda f: (0, 0, 0, f))
    shape = jax.ShapeDtypeStruct((chips, 2, part, hidden), bf16)
    return pl.pallas_call(
        behind(gate_up_kernel, 5, others),
        grid=(hidden // wide,),
        in_specs=[
            SMEM,
            pl.BlockSpec((rows, width), lambda f: (0, 0)),
            tile,
            tile,
            pl.BlockSpec((rows, TILE), lambda f: (0, 0)),
        ]
        + anywhere(others),
        out_specs=[out, out, pl.BlockSpec((width, TILE), lambda f: (0, 0))],
        out_shape=[shape, shape, jax.ShapeDtypeStruct((width, TILE), f32)],
        scratch_shapes=[pltpu.VMEM((width, rows), bf16)],
        compiler_params=pltpu.CompilerParams(vmem_limit_bytes=VMEM),
        cost_estimate=cost(24),
        name="gate_up_grads",
    )(side, x, dgp, dup, glog, *others)


def down_kernel(s_ref, act_ref, gcot_ref, other_ref, mine_ref, res_ref):
    res_ref[...] = dot(act_ref[...].T, gcot_ref[...]).astype(bf16).reshape(res_ref.shape)
    other_ref[...] = res_ref[:, 1 - s_ref[0]]
    mine_ref[...] = res_ref[:, s_ref[0]]


def down_grads(side, chips, act, gcot, others=()):
    rows, hidden = act.shape
    width, wide = gcot.shape[1], hidden // 2
    part = hidden // chips // 2
    out = pl.BlockSpec((chips // 2, part, width), lambda f: (f, 0, 0))
    shape = jax.ShapeDtypeStruct((chips, part, width), bf16)
    return pl.pallas_call(
        behind(down_kernel, 3, others),
        grid=(2,),
        in_specs=[SMEM, pl.BlockSpec((rows, wide), lambda f: (0, f)), pl.BlockSpec((rows, width), lambda f: (0, 0))]
        + anywhere(others),
        out_specs=[out, out],
        out_shape=[shape, shape],
        scratch_shapes=[pltpu.VMEM((chips // 2, 2, part, width), bf16)],
        compiler_params=pltpu.CompilerParams(vmem_limit_bytes=VMEM),
        cost_estimate=cost(14),
        name="down_grads",
    )(side, act, gcot, *others)


def out_kernel(act_ref, wd_ref, gate_ref, *refs):
    outs, acc_ref = refs[:-1], refs[-1]
    step = pl.program_id(0)
    more = dot(act_ref[...], wd_ref[0])

    @pl.when(step == 0)
    def _():
        acc_ref[...] = more

    @pl.when(step > 0)
    def _():
        acc_ref[...] += more

    @pl.when(step == pl.num_programs(0) - 1)
    def _():
        rows = outs[0].shape[0]
        for n, out in enumerate(outs):
            part = slice(n * rows, (n + 1) * rows)
            out[...] = (acc_ref[part, :] * gate_ref[part, :1]).astype(bf16)


def expert_out(act, wd, gate, chunks, others=()):
    rows, hidden = act.shape
    width, wide = wd.shape[2], hidden // 2
    fixed = lambda r, c: pl.BlockSpec((r, c), lambda f: (0, 0))
    return pl.pallas_call(
        behind(out_kernel, 3, others),
        grid=(hidden // wide,),
        in_specs=[
            pl.BlockSpec((rows, wide), lambda f: (0, f)),
            pl.BlockSpec((1, wide, width), lambda f: (0, f, 0)), fixed(rows, TILE),
        ] + anywhere(others),
        out_specs=[fixed(rows // chunks, width)] * chunks,
        out_shape=[jax.ShapeDtypeStruct((rows // chunks, width), bf16)] * chunks,
        scratch_shapes=[pltpu.VMEM((rows, width), f32)],
        compiler_params=pltpu.CompilerParams(vmem_limit_bytes=VMEM),
        cost_estimate=cost(14),
        name="expert_out",
    )(act, wd, gate, *others)


def norm_kernel(per_block, two_ref, one_ref, own_ref, gain_ref, out_ref, turned_ref):
    step = pl.program_id(0)

    def put(ref):
        x = ref[0].astype(f32)
        r = lax.rsqrt(jnp.mean(x * x, axis=-1, keepdims=True) + epsilon)
        normed = (x * r * gain_ref[...]).astype(bf16)
        out_ref[0] = normed
        turned_ref[...] = normed.T.reshape(turned_ref.shape)

    for n, ref in enumerate((two_ref, one_ref, own_ref)):
        pl.when(step // per_block == n)(functools.partial(put, ref))


def norm_window(two, one, own, gain, chips):
    pieces, rows, width = own.shape
    at = lambda n: pl.BlockSpec((1, rows, width), lambda f: (jnp.clip(f - n * pieces, 0, pieces - 1), 0, 0))
    return pl.pallas_call(
        functools.partial(norm_kernel, pieces),
        grid=(3 * pieces,),
        in_specs=[at(0), at(1), at(2), pl.BlockSpec((1, width), lambda f: (0, 0))],
        out_specs=[
            pl.BlockSpec((1, rows, width), lambda f: (f, 0, 0)),
            pl.BlockSpec((chips, 2, width // chips // 2, rows), lambda f: (0, 0, 0, f)),
        ],
        out_shape=[
            jax.ShapeDtypeStruct((3 * pieces, rows, width), bf16),
            jax.ShapeDtypeStruct((chips, 2, width // chips // 2, 3 * pieces * rows), bf16),
        ],
        compiler_params=pltpu.CompilerParams(vmem_limit_bytes=VMEM),
        cost_estimate=cost(10),
        name="norm_window",
    )(two, one, own, gain)


def slot_rows(t_ref, k, slot):
    index = lax.broadcasted_iota(jnp.int32, (slot, t_ref.shape[1]), 0) + k * slot
    return ((index == t_ref[0:1, :]) | (index == t_ref[1:2, :])).astype(bf16)


def row_slots(t_ref, k, slot):
    index = lax.broadcasted_iota(jnp.int32, (t_ref.shape[0], slot), 1) + k * slot
    return ((index == t_ref[:, 0:1]) | (index == t_ref[:, 1:2])).astype(bf16)


def collect(t_ref, refs):
    total = None
    for k, ref in enumerate(refs):
        part = dot(row_slots(t_ref, k, ref.shape[0]), ref[...])
        total = part if total is None else total + part
    return total


def turned(ref, z):
    return jnp.concatenate([ref[z ^ k] for k in range(ref.shape[0])], axis=0)


def call(kernel, ins, outs, us, name, others=(), scratch=()):
    specs = [SMEM if a.ndim == 1 else pl.BlockSpec(memory_space=pltpu.VMEM) for a in ins]
    return pl.pallas_call(
        behind(kernel, len(ins), others),
        in_specs=specs + anywhere(others),
        out_specs=[pl.BlockSpec(memory_space=pltpu.VMEM)] * len(outs),
        out_shape=[jax.ShapeDtypeStruct(shape, dtype) for shape, dtype in outs],
        scratch_shapes=list(scratch),
        compiler_params=pltpu.CompilerParams(vmem_limit_bytes=VMEM),
        cost_estimate=cost(us),
        name=name,
    )(*ins, *others)


def pair_kernel(mine_ref, other_ref, out_ref):
    out_ref[...] = (mine_ref[...].astype(f32) + other_ref[...].astype(f32)).astype(bf16)


def pair_sum(mine, other, others=()):
    block = pl.BlockSpec((1,) + mine.shape[1:], lambda f: (f,) + (0,) * (mine.ndim - 1))
    return pl.pallas_call(
        behind(pair_kernel, 2, others),
        grid=mine.shape[:1],
        in_specs=[block, block] + anywhere(others),
        out_specs=block,
        out_shape=jax.ShapeDtypeStruct(mine.shape, bf16),
        compiler_params=pltpu.CompilerParams(vmem_limit_bytes=VMEM),
        cost_estimate=cost(6),
        name="pair_sum",
    )(mine, other, *others)


def cot_kernel(ks, slot, z_ref, t_ref, cot_ref, *outs):
    values = turned(cot_ref, z_ref[0])
    for k, out in zip(ks, outs):
        out[...] = dot(slot_rows(t_ref, k, slot), values).astype(bf16)


def rows_kernel(ks, slot, t_ref, value_ref, *outs):
    for k, out in zip(ks, outs):
        out[...] = dot(slot_rows(t_ref, k, slot), value_ref[...]).astype(bf16)


def hidden_kernel(ks, slot, z_ref, t_ref, tok_ref, w_ref, gain_ref, *refs):
    pieces = tok_ref.shape[0]
    context, hidden_ref, moe_ref, outs = refs[:pieces], refs[pieces], refs[pieces + 1], refs[pieces + 2 :]
    left = jnp.concatenate([ref[...] for ref in context], axis=0)
    hidden = turned(tok_ref, z_ref[0]).astype(f32) + dot(left, w_ref[...])
    hidden_ref[...] = hidden
    moe_in = norm_rows(hidden, gain_ref[...]).astype(bf16)
    moe_ref[...] = moe_in
    for k, out in zip(ks, outs):
        out[...] = dot(slot_rows(t_ref, k, slot), moe_in).astype(bf16)


def middle_kernel(z_ref, t_ref, hidden_ref, cot_ref, w_ref, gain_ref, *refs):
    pieces = cot_ref.shape[0]
    grad_ref, attn_ref, gain_grad_ref, outs = refs[pieces], refs[pieces + 1], refs[pieces + 2], refs[pieces + 3 :]
    grad_moe = collect(t_ref, refs[:pieces])
    grad_norm, gain_grad = norm_back(hidden_ref[...], gain_ref[...], grad_moe)
    gain_grad_ref[...] = gain_grad[None]
    grad = turned(cot_ref, z_ref[0]).astype(f32) + grad_norm
    grad_ref[...] = grad
    low = grad.astype(bf16)
    attn_ref[...] = low
    context = dot_nt(low, w_ref[...]).astype(bf16)
    rows = context.shape[0] // pieces
    for k in range(pieces):
        outs[k][...] = context[k * rows : (k + 1) * rows]


def mix_kernel(z_ref, t_ref, hidden_ref, *refs):
    out_ref = refs[-1]
    rows = out_ref.shape[1]
    mixed = (hidden_ref[...] + collect(t_ref, refs[:-1])).astype(bf16)
    for k in range(out_ref.shape[0]):
        out_ref[z_ref[0] ^ k] = mixed[k * rows : (k + 1) * rows]


def inputs_kernel(last, dq_ref, dk_ref, dv_ref, wq_ref, wk_ref, wv_ref, *refs):
    step = pl.program_id(0)
    flat = lambda ref: ref[...].reshape(-1, ref.shape[-1])
    grad = dot_nt(flat(dk_ref), wk_ref[...]) + dot_nt(flat(dv_ref), wv_ref[...])
    if not last:
        refs[0][...] = grad

        @pl.when(step == 2)
        def _():
            refs[0][...] = grad + dot_nt(flat(dq_ref), wq_ref[...])

        return
    acc_ref, two_ref, one_ref, own_ref = refs
    grad = grad + acc_ref[...]

    @pl.when(step == 0)
    def _():
        two_ref[...] = grad.astype(bf16)

    @pl.when(step == 1)
    def _():
        one_ref[...] = grad.astype(bf16)

    @pl.when(step == 2)
    def _():
        own_ref[...] = grad + dot_nt(flat(dq_ref), wq_ref[...])


def input_grads(part, dq, dk, dv, wq, wk, wv, acc=None, others=()):
    pieces, rows, some = dq.shape
    width = wq.shape[0]
    block = pieces * rows
    window = pl.BlockSpec((pieces, rows, some), lambda f: (f, 0, 0))
    weight = pl.BlockSpec((width, some), lambda f: (0, part))
    once = pl.BlockSpec((block, width), lambda f: (0, 0))
    step = pl.BlockSpec((block, width), lambda f: (f, 0))
    specs = [pl.BlockSpec((pieces, rows, some), lambda f: (0, 0, 0)), window, window, weight, weight, weight]
    ins, outs = [dq, dk, dv, wq, wk, wv], [(step, (3 * block, width), f32)]
    if acc is not None:
        specs += [step]
        ins += [acc]
        outs = [(once, (block, width), bf16)] * 2 + [(once, (block, width), f32)]
    return pl.pallas_call(
        behind(functools.partial(inputs_kernel, acc is not None), len(ins), others),
        grid=(3,),
        in_specs=specs + anywhere(others),
        out_specs=[o[0] for o in outs],
        out_shape=[jax.ShapeDtypeStruct(o[1], o[2]) for o in outs],
        compiler_params=pltpu.CompilerParams(vmem_limit_bytes=VMEM),
        cost_estimate=cost(7),
        name="input_grads",
    )(*ins, *others)


def leave_kernel(s_ref, z_ref, two_ref, swapped_ref, parts_ref, leave_ref, keep_ref, *refs):
    outs, total_ref = refs[:-1], refs[-1]
    zero = jnp.zeros_like(swapped_ref)
    swapped = swapped_ref[...]
    add = jnp.where(s_ref[0] == 0, zero, swapped)
    leave_ref[...] = (two_ref[...].astype(f32) + add.astype(f32)).astype(bf16)
    keep_ref[...] = jnp.where(s_ref[0] == 0, swapped, zero)
    total = parts_ref[0].astype(f32)
    for i in range(1, parts_ref.shape[0]):
        total = total + parts_ref[i].astype(f32)
    total_ref[...] = total.astype(bf16).reshape(total_ref.shape)
    for k, out in enumerate(outs):
        out[...] = total_ref[z_ref[0] ^ k]


def tail_kernel(z_ref, x_ref, sum_ref, swapped_ref, gain_ref, came_ref, *refs):
    pieces, rows, width = x_ref.shape
    blocks, outs, total_ref = refs[0], refs[1:-1], refs[-1]
    total = blocks[0].astype(f32)
    for i in range(1, blocks.shape[0]):
        total = total + blocks[i].astype(f32)
    total_ref[...] = total.astype(bf16).reshape(total_ref.shape)
    share, long = total_ref.shape[1:]
    for k in range(pieces):
        part = slice(k * rows, (k + 1) * rows)
        grad = sum_ref[part, :] + swapped_ref[part, :].astype(f32) + came_ref[part, :].astype(f32)
        outs[k][:rows, :] = norm_back(x_ref[k].astype(f32), gain_ref[...], grad)[0].astype(bf16)
        theirs = total_ref[z_ref[0] ^ k]
        outs[k][rows : rows + share, :] = theirs[:, :width]
        outs[k][rows + share :, : long - width] = theirs[:, width:]
        outs[k][rows + share :, long - width :] = jnp.zeros((share, 2 * width - long), bf16)


def end_kernel(z_ref, grad_ref, wq_ref, wk_ref, wv_ref, gain_ref, *refs):
    outs = refs[-7:]
    pieces, rows, width = outs[0].shape
    share, long = refs[pieces].shape
    half = (long - width) // 3
    first = refs[pieces][...].astype(f32)
    for k in range(1, pieces):
        first = first + refs[pieces + k][...].astype(f32)
    outs[6][...] = first[:, 3 * half :]
    total = None
    for k in range(pieces):
        outs[0][z_ref[0] ^ k] = (grad_ref[k * rows : (k + 1) * rows, :] + refs[k][:rows, :].astype(f32)).astype(bf16)
        part = jnp.concatenate([refs[k][rows : rows + share, :], refs[k][rows + share :, :]], axis=1).astype(f32)
        total = part if total is None else total + part
    gain = jnp.zeros((share, 1), f32)
    for i, weight in enumerate((wq_ref, wk_ref, wv_ref)):
        parts = (first[:, i * half : (i + 1) * half], total[:, i * half : (i + 1) * half])
        for n, part in enumerate(parts):
            columns = slice(n * half, (n + 1) * half)
            outs[1 + i][:, columns] = part
            gain = gain + jnp.sum(part * weight[:, columns].astype(f32), axis=1, keepdims=True)
    outs[4][...] = total[:, 3 * half : 3 * half + outs[4].shape[1]]
    outs[5][...] = gain / gain_ref[...]


def projection_kernel(third, small, pieces, s_ref, nt_ref, dq_ref, dk_ref, dv_ref, *refs):
    other_ref, mine_ref = refs[small + pieces + (pieces > 0) :][:2]
    step = pl.program_id(0)
    keys = nt_ref.shape[3]
    own = dq_ref.shape[0]

    def put(grad_ref, first):
        for where, ref in ((1 - s_ref[0], other_ref), (s_ref[0], mine_ref)):
            left = nt_ref[:, where, :, first:].reshape(-1, keys - first)
            ref[...] = dot(left, grad_ref[...]).astype(bf16).reshape(ref.shape)

    @pl.when(step < third)
    def _():
        put(dq_ref, keys - own)

    @pl.when((step >= third) & (step < 2 * third))
    def _():
        put(dk_ref, 0)

    @pl.when((step >= 2 * third) & (step < 3 * third))
    def _():
        put(dv_ref, 0)

    if pieces:
        turned_ref, context, attn_ref = refs[-1], refs[:pieces], refs[pieces]
        count = context[0].shape[0]

        @pl.when(step == 3 * third)
        def _():
            for k in range(pieces):
                turned_ref[:, :, :, k * count : (k + 1) * count] = context[k][...].T.reshape(turned_ref.shape[:3] + (count,))

        @pl.when(step >= 3 * third)
        def _():
            for where, ref in ((1 - s_ref[0], other_ref), (s_ref[0], mine_ref)):
                left = turned_ref[:, where].reshape(-1, pieces * count)
                ref[...] = dot(left, attn_ref[...]).astype(bf16).reshape(ref.shape)

    if small:

        @pl.when(step == 3 * third)
        def _():
            other_ref[...] = refs[0][:, 1 - s_ref[0]]
            mine_ref[...] = refs[0][:, s_ref[0]]


def projection_grads(side, normed_t, dq, dk, dv, small=(), context=(), attn=(), others=()):
    chips, _, rows, keys = normed_t.shape
    own, width = dq.shape
    wide = 2 * TILE
    third = width // wide
    at = lambda j: (lambda f: (0, jnp.clip(f - j * third, 0, third - 1)))
    fixed = lambda array: pl.BlockSpec(array.shape, lambda f: (0,) * array.ndim)
    more = len(small) + sum(array.shape[1] // wide for array in attn)
    out = pl.BlockSpec((chips, rows, wide), lambda f: (0, 0, f))
    shape = jax.ShapeDtypeStruct((chips, rows, 3 * width + wide * more), bf16)
    ins = [side, normed_t, dq, dk, dv, *small, *context, *attn]
    scratch = [pltpu.VMEM((chips, 2, rows, len(context) * array.shape[0]), bf16) for array in context[:1]]
    return pl.pallas_call(
        behind(functools.partial(projection_kernel, third, len(small), len(context)), len(ins), others),
        grid=(3 * third + more,),
        in_specs=[
            SMEM,
            fixed(normed_t),
            pl.BlockSpec((own, wide), at(0)),
            pl.BlockSpec((keys, wide), at(1)),
            pl.BlockSpec((keys, wide), at(2)),
        ]
        + [fixed(array) for array in [*small, *context]]
        + [pl.BlockSpec((array.shape[0], wide), lambda f: (0, jnp.maximum(f - 3 * third, 0))) for array in attn]
        + anywhere(others),
        out_specs=[out, out],
        out_shape=[shape, shape],
        scratch_shapes=scratch,
        compiler_params=pltpu.CompilerParams(vmem_limit_bytes=VMEM),
        cost_estimate=cost(9.3 + more),
        name="projection_grads",
    )(*ins, *others)


def shift(x, by):
    count = lax.axis_size("ctx")
    return lax.ppermute(x, "ctx", [(i, i + by) for i in range(count) if 0 <= i + by < count])


def core_swap(x):
    return lax.ppermute(x, "ctx", [(i, i ^ 1) for i in range(lax.axis_size("ctx"))])


def z_swap(x, k):
    if k == 0:
        return x
    return lax.ppermute(x, "exp", [(i, i ^ k) for i in range(lax.axis_size("exp"))])


def over_chips(pair):
    count = lax.axis_size("ctx")
    groups = [list(range(core, count, 2)) for core in range(2)]
    return lax.all_to_all(pair, "ctx", split_axis=0, concat_axis=0, tiled=True, axis_index_groups=groups)


def summed(parts):
    return jnp.sum(parts.astype(f32), axis=0)


def add_pair(mine, other):
    return (mine.astype(f32) + core_swap(other).astype(f32)).astype(bf16)


def norm_rows(values, gain):
    return values * lax.rsqrt(jnp.mean(values * values, axis=-1, keepdims=True) + epsilon) * gain


def norm_back(values, gain, grad):
    r = lax.rsqrt(jnp.mean(values * values, axis=-1, keepdims=True) + epsilon)
    u = grad * gain
    inner = jnp.mean(values * u, axis=-1, keepdims=True)
    return r * u - values * (r * r * r) * inner, jnp.sum(grad * values * r, axis=0)


def on_device(
    tokens, doc_lengths, routes, priority, norm1_gain, w_query, w_key, w_value, w_out, bias_table,
    norm2_gain, w_router, w_gate, w_up, w_down, cotangent,
):
    seqs, piece_len, width = tokens.shape
    exp_count = lax.axis_size("exp")
    ctx_count = lax.axis_size("ctx")
    device_count = exp_count * ctx_count
    block_len = piece_len * exp_count
    rows = seqs * piece_len
    heads = bias_table.shape[0] // bucket_total
    experts = w_router.shape[1]
    slot = 5 * rows // (2 * experts)
    slots = experts * slot
    ctx = lax.axis_index("ctx")
    exp = lax.axis_index("exp")
    side = ctx % 2

    z = jnp.reshape(exp, (1,))
    far_first = [2, 3, 1]

    turn = jnp.arange(seqs, dtype=jnp.int32) ^ exp
    pick = lambda array, k: lax.dynamic_index_in_dim(array, exp ^ k, 0, keepdims=False)

    x_own = [None] * seqs
    for k in [0, 2, 3, 1]:
        x_own[k] = z_swap(pick(tokens, k), k)
    x_pieces = x_own
    x_two = [shift(piece, 2) for piece in x_own]
    x_own, x_two = jnp.stack(x_own), jnp.stack(x_two)
    x_one = core_swap(jnp.where(side == 0, x_own, x_two))

    route_rows = jnp.take(routes, turn, axis=0).reshape(rows, 2)
    order = jnp.take(priority, turn, axis=0).reshape(rows)
    earlier = order[None, :] < order[:, None]
    r0, r1 = route_rows[:, 0], route_rows[:, 1]
    place0 = jnp.sum((earlier & (r0[None, :] == r0[:, None])).astype(jnp.int32), axis=1)
    place1 = jnp.sum((earlier & (r1[None, :] == r1[:, None])).astype(jnp.int32), axis=1) + jnp.sum(
        (r0[None, :] == r1[:, None]).astype(jnp.int32), axis=1
    )
    target0 = jnp.where(place0 < slot, (r0 ^ exp) * slot + place0, -1)
    target1 = jnp.where(place1 < slot, (r1 ^ exp) * slot + place1, -1)
    targets = jnp.stack([target0, target1])
    targets_t = targets.T
    slot_shape = ((slot, width), bf16)
    sent = call(
        functools.partial(cot_kernel, far_first + [0], slot), [z, targets, cotangent], [slot_shape] * experts, 4, "cot_rows", x_pieces[1:]
    )
    cot_slots = [None] * experts
    for k, rows_k in zip(far_first + [0], sent):
        cot_slots[k] = z_swap(rows_k, k)

    distance = np.arange(-TILE, WINDOW + TILE)
    seen = (distance >= 0) & (distance < WINDOW)
    hot = (bucket_of(np.clip(distance, 0, None))[None, :] == np.arange(bucket_total)[:, None]) & seen[None, :]
    vec = exact_dot(bias_table.astype(f32).reshape(heads, bucket_total), jnp.asarray(hot, f32))
    vec = jnp.where(jnp.asarray(seen)[None, :], vec, NEG).reshape(heads // 2, 2, -1)
    bias = bias_tiles(vec, sent[:1])

    ends = jnp.cumsum(lax.dynamic_index_in_dim(doc_lengths, exp, 0, keepdims=False))
    piece_start = ctx * block_len + turn[:, None] * piece_len
    q_pos = piece_start + jnp.arange(piece_len, dtype=jnp.int32)[None, :]
    start = jnp.max(jnp.where(ends <= q_pos[..., None], ends, 0), axis=2)
    lo = start - (ctx - 2) * block_len
    lo = jnp.broadcast_to(lo[:, None, None, :], (seqs, 1, 2, TILE)).reshape(seqs, 1, 2 * TILE)

    gain_one = norm1_gain.astype(f32)
    normed, normed_t = norm_window(x_two, x_one, x_own, gain_one[None], ctx_count // 2)
    normed = normed.reshape(-1, width)
    normed_own = normed[2 * block_len :]
    q = (dot(normed_own, w_query).astype(bf16) * 0.125).astype(bf16).reshape(seqs, piece_len, width)
    k_win = dot(normed, w_key).astype(bf16).reshape(-1, TILE, width)
    v_win = dot(normed, w_value).astype(bf16).reshape(-1, TILE, width)
    contexts, lses, context_rows = [None] * seqs, [], [None] * seqs
    for first in (2, 0):
        others = [contexts[2], cot_slots[1]] if first == 0 else [cot_slots[2]]
        *c, l = attend((first, first + 1), z, lo[first : first + 2], q[first : first + 2], k_win, v_win, bias, others)
        lses.insert(0, l)
        for k in (first, first + 1):
            contexts[k] = c[k - first]
            context_rows[k] = z_swap(contexts[k], k)
    router_wide = jnp.pad(w_router, ((0, 0), (0, TILE - experts)))
    gain_two = norm2_gain.astype(f32)[None]
    hidden, moe_in, *sent = call(
        functools.partial(hidden_kernel, [2, 0], slot),
        [z, targets, tokens, w_out, gain_two] + context_rows,
        [((rows, width), f32), ((rows, width), bf16), slot_shape, slot_shape], 9, "hidden_rows", [cot_slots[3]],
    )
    inputs = [sent[1], None, z_swap(sent[0], 2), None]
    held, returned, turns = None, [None] * experts, [0, 2, 1, 3]
    for ks, index in (([0], 0), ([2], 1), ([1], 2), ([3], 3)):
        found = expert(
            index, experts, held, z, [inputs[k] for k in ks], [cot_slots[k] for k in ks], w_gate, w_up, w_down, router_wide, experts
        )
        back, held = found[: len(ks)], found[len(ks) :]
        for k, rows_k in zip(ks, back):
            returned[k] = z_swap(rows_k, k)
        if index == 0:
            sent = call(functools.partial(rows_kernel, [3, 1], slot), [targets, moe_in], [slot_shape] * 2, 3, "moe_rows", back)
            inputs[3], inputs[1] = z_swap(sent[0], 3), z_swap(sent[1], 1)
    all_inputs, act_low, grad_gate_pre, grad_up_pre, grad_out_slots, gate, grad_logits = held
    chips = ctx_count // 2
    side_ref = jnp.reshape(side, (1,))
    produced = expert_out(act_low, w_down, gate, experts, [returned[2]])
    down_other, down_mine = down_grads(side_ref, chips, act_low, grad_out_slots, produced[:1])

    part_count = 2
    part_width = width // part_count
    grad_hidden, grad_attn, grad_gain_two, *sent_back = call(
        middle_kernel, [z, targets_t, hidden, cotangent, w_out, gain_two] + returned,
        [((rows, width), f32), ((rows, width), bf16), ((1, width), f32)] + [((piece_len, width), bf16)] * seqs,
        9, "middle_rows", [down_other],
    )
    arrived = [z_swap(sent_back[k], k) for k in range(seqs)]
    other, mine, router_part = gate_up_grads(
        side_ref, chips, all_inputs, grad_gate_pre, grad_up_pre, grad_logits, sent_back[-1:]
    )
    grad_router_part = router_part[:, :experts]
    pair = pair_sum(mine, core_swap(other))
    both = over_chips(pair)
    down_other = core_swap(down_other)
    given = [z_swap(produced[turns.index(k)], k) for k in range(experts)]

    weights = (w_query, w_key, w_value)
    flat = lambda grads: [grad.reshape(-1, part_width) for grad in grads]
    back = lambda n, others: attend_back(n, part_count, z, lo, lses, q, k_win, v_win, bias, contexts, arrived, others)
    *grads, diagonal = back(0, [pair])
    other, mine = projection_grads(
        side_ref, normed_t, *flat(grads), context=context_rows, attn=[grad_attn], others=[given[2], given[1]]
    )
    first_pair = add_pair(mine, other)
    first_parts = over_chips(first_pair)
    acc = input_grads(0, *grads, *weights, others=[other])[0]
    *grads, more = back(1, [acc, first_pair, both])
    diagonals = jnp.concatenate([diagonal, more])
    places = np.arange((TILES_SEEN) * 2 * TILE).reshape(TILES_SEEN, 2 * TILE)
    block, lane = places // (2 * TILE), places % (2 * TILE)
    where_dist = lane - TILE + (TILES_SEEN - 1 - block) * TILE
    ok = (where_dist >= 0) & (where_dist < WINDOW)
    to_bucket = (bucket_of(np.clip(where_dist, 0, None))[..., None] == np.arange(bucket_total)) & ok[..., None]
    table_part = exact_dot(diagonals.reshape(heads, -1), jnp.asarray(to_bucket.reshape(-1, bucket_total), f32))
    small = [
        grad_gain_two.reshape(device_count, -1),
        table_part.reshape(device_count, -1),
        grad_router_part.reshape(device_count, -1),
    ]
    cuts = np.cumsum([0] + [item.shape[1] for item in small])
    packed = jnp.concatenate(small, axis=1)
    share = width // device_count
    packed = jnp.pad(packed, ((0, 0), (0, -packed.shape[1] % share))).reshape(width, -1)
    packed = jnp.pad(packed.astype(bf16), ((0, 0), (0, 2 * TILE - packed.shape[1])))
    packed = packed.reshape(ctx_count // 2, 2, -1, 2 * TILE)
    other, mine = projection_grads(side_ref, normed_t, *flat(grads), small=[packed], others=[first_parts, given[3]])
    pair = add_pair(mine, other)
    last = over_chips(pair)
    part_two, part_one, own_sum = input_grads(1, *grads, *weights, acc, [pair])
    leave, swapped, *first = call(
        leave_kernel, [side_ref, z, part_two, core_swap(part_one), first_parts],
        [((block_len, width), bf16)] * 2 + [((share, first_parts.shape[-1]), bf16)] * seqs, 5, "leaving_rows", [last],
        [pltpu.VMEM((exp_count, share, first_parts.shape[-1]), bf16)],
    )
    first = [z_swap(piece, k) for k, piece in enumerate(first)]
    came = shift(leave, -2)
    down = over_chips(pair_sum(down_mine, down_other, [leave]))
    mixed = call(
        mix_kernel, [z, targets_t, hidden] + given, [((seqs, piece_len, width), bf16)], 8, "mixed_rows", [leave]
    )[0]
    share = width // device_count
    long = pair.shape[-1]
    pieces = call(
        tail_kernel, [z, x_own, own_sum, swapped, gain_one[None], came, last],
        [((piece_len + 2 * share, width), bf16)] * seqs, 8, "tail_rows", [mixed] + first[1:],
        [pltpu.VMEM((exp_count, share, long), bf16)],
    )
    pieces = [z_swap(piece, k) for k, piece in enumerate(pieces)]
    own_rows = lambda array: lax.dynamic_slice_in_dim(array, (ctx * exp_count + exp) * share, share, 0)
    grad_tokens, grad_query, grad_key, grad_value, packed, norm1_out, grad_out = call(
        end_kernel,
        [z, grad_hidden] + [own_rows(array) for array in weights] + [own_rows(gain_one[:, None])] + pieces + first,
        [((seqs, piece_len, width), bf16)] + [((share, width), f32)] * 3 + [((share, 2 * TILE), f32), ((share, 1), f32)]
        + [((share, width), f32)],
        6, "end_rows", [down],
    )
    grad_gate, grad_up, grad_down = summed(both[:, 0]), summed(both[:, 1]), summed(down)
    packed = packed[:, : -(-cuts[-1] // share)].reshape(-1)
    norm1_out = norm1_out[:, 0]
    norm2_out, table_out, router_out = [packed[cuts[i] : cuts[i + 1]] for i in range(3)]
    return (
        mixed, grad_tokens, norm1_out, grad_query, grad_key, grad_value, grad_out, table_out, norm2_out,
        router_out.reshape(-1, experts), grad_gate[None], grad_up[None], grad_down[None],
    )


def solution(mesh):
    rows = P(None, ("ctx", "exp"), None)
    flat = P(("ctx", "exp"))
    in_specs = (
        rows, P(), rows, P(None, ("ctx", "exp")), P(), P(), P(), P(), P(), P(), P(), P(),
        P("exp", None, None), P("exp", None, None), P("exp", None, None), rows,
    )
    out_specs = (
        rows, rows, flat, P(("ctx", "exp"), None), P(("ctx", "exp"), None), P(("ctx", "exp"), None),
        P(("ctx", "exp"), None), flat, flat, P(("ctx", "exp"), None),
        P("exp", "ctx", None), P("exp", "ctx", None), P("exp", "ctx", None),
    )
    return jax.shard_map(on_device, mesh=mesh, in_specs=in_specs, out_specs=out_specs, check_vma=False)
```

```python
import functools

import jax
import jax.numpy as jnp
import numpy as np
from jax import lax
from jax.experimental import pallas as pl
from jax.experimental.pallas import tpu as pltpu
from jax.sharding import PartitionSpec as P

WINDOW = 1024
TILE = 128
TILES_SEEN = WINDOW // TILE + 1
epsilon = 1e-06
bucket_total = 32
NEG = -1e30
f32 = jnp.float32
bf16 = jnp.bfloat16
VMEM = 56 * 1024 * 1024


def cost(us):
    return pl.CostEstimate(flops=int(us * 1.15e9), bytes_accessed=0, transcendentals=0)


def behind(kernel, inputs, others):
    return lambda *refs: kernel(*refs[:inputs], *refs[inputs + len(others) :])


def anywhere(others):
    return [pl.BlockSpec(memory_space=pl.ANY)] * len(others)


def dot(left, right):
    return jnp.dot(left, right, preferred_element_type=f32)


def dot_nt(left, right):
    return lax.dot_general(left, right, (((1,), (1,)), ((), ())), preferred_element_type=f32)


def dot_tn(left, right):
    return lax.dot_general(left, right, (((0,), (0,)), ((), ())), preferred_element_type=f32)


def exact_dot(left, right):
    return jnp.dot(left, right, precision=lax.Precision.HIGHEST, preferred_element_type=f32)


def bucket_of(distance):
    limits = np.ceil(16.0 * 8.0 ** (np.arange(1, 16) / 16.0)).astype(np.int32)
    above = np.sum(distance[..., None] >= limits, axis=-1)
    return np.where(distance < 16, distance, 16 + above)


def bias_kernel(vec_ref, out_ref):
    for a in range(TILES_SEEN):
        first = (TILES_SEEN - 1 - a) * TILE
        for h in range(2):
            row = vec_ref[0, h : h + 1, first : first + 2 * TILE]
            wide = jnp.broadcast_to(row, (TILE, 2 * TILE))
            rolled = pltpu.roll(wide, TILE, 1, stride=1, stride_axis=0)
            out_ref[0, a, :, h * TILE : (h + 1) * TILE] = rolled[:, :TILE].astype(bf16)


def split_heads(x):
    lane = lax.broadcasted_iota(jnp.int32, x.shape, 1)
    zero = jnp.zeros_like(x)
    return jnp.concatenate([jnp.where(lane < 64, x, zero), jnp.where(lane < 64, zero, x)], axis=0)


def merge_heads(xt):
    return jnp.concatenate([xt[:64, :TILE], xt[64:, TILE:]], axis=0).T


def key_block(kb, z):
    return (kb // 4) * 4 + ((kb % 4) ^ z)


def attend_kernel(ks, z_ref, lo_ref, q_ref, k_ref, v_ref, b_ref, *refs):
    outs, (lse_ref, s_ref, p_ref, v_s) = refs[: len(ks)], refs[len(ks) :]
    z = z_ref[0]
    row = lax.broadcasted_iota(jnp.int32, (TILE, 2 * TILE), 0)
    for n, k in enumerate(ks):
        t = z ^ k
        q2 = split_heads(q_ref[n])
        lo = lo_ref[n] - t * TILE
        top = jnp.full((8, 2 * TILE), NEG, f32)
        for a in range(TILES_SEEN):
            at = key_block(t + a, z)
            v_s[a * TILE : (a + 1) * TILE, :] = v_ref[at]
            s = dot_nt(k_ref[at], q2) + b_ref[0, a].astype(f32)
            s = jnp.where(row >= lo - a * TILE, s, NEG)
            s_ref[a] = s
            top = jnp.maximum(top, jnp.max(s.reshape(TILE // 8, 8, 2 * TILE), axis=0))
        top = jnp.max(top, axis=0, keepdims=True)
        total = jnp.zeros((8, 2 * TILE), f32)
        for a in range(TILES_SEEN):
            p = jnp.exp(s_ref[a] - top)
            total = total + jnp.sum(p.reshape(TILE // 8, 8, 2 * TILE), axis=0)
            p_ref[a * TILE : (a + 1) * TILE, :] = p.astype(bf16)
        total = jnp.sum(total, axis=0, keepdims=True)
        ct = dot(v_s[...].T, p_ref[...]) / total
        outs[n][...] = merge_heads(ct).astype(bf16)
        lse_ref[0, n] = top + jnp.log(total)


def attend_back_kernel(pieces, z_ref, lo_ref, lse_a, lse_b, q_ref, k_ref, v_ref, b_ref, *refs):
    o_refs, do_refs = refs[:pieces], refs[pieces : 2 * pieces]
    dq_ref, dk_ref, dv_ref, tab_ref, q2_ref, do2_ref, ds_ref, p_ref, acc_ref, row_ref, k_s = refs[2 * pieces :]
    z = z_ref[0]
    row = lax.broadcasted_iota(jnp.int32, (TILE, 2 * TILE), 0)
    for k in range(pieces):
        both = pl.ds(pl.multiple_of((z ^ k) * 2 * TILE, 2 * TILE), 2 * TILE)
        out, grad = o_refs[k][...], do_refs[k][...]
        q2_ref[both, :] = split_heads(q_ref[k])
        do2_ref[both, :] = split_heads(grad)
        prod = (grad.astype(f32) * out.astype(f32)).T
        lse_ref = lse_a if k < pieces // 2 else lse_b
        row_ref[0:1, both] = lse_ref[0, k % (pieces // 2)]
        row_ref[1:2, both] = jnp.concatenate(
            [jnp.sum(prod[:64], axis=0, keepdims=True), jnp.sum(prod[64:], axis=0, keepdims=True)], axis=1
        )
    acc_ref[...] = jnp.zeros_like(acc_ref)
    keys = pieces + TILES_SEEN - 1
    for kb in range(keys):
        first, last = max(0, kb - TILES_SEEN + 1), min(pieces - 1, kb)
        krows = slice(kb * TILE, (kb + 1) * TILE)
        cols = slice(first * 2 * TILE, (last + 1) * 2 * TILE)
        at = key_block(kb, z)
        key, value = k_ref[at], v_ref[at]
        k_s[krows, :] = key
        for t in range(first, last + 1):
            both = slice(t * 2 * TILE, (t + 1) * 2 * TILE)
            a = kb - t
            s = dot_nt(key, q2_ref[both, :]) + b_ref[0, a].astype(f32)
            s = jnp.where(row >= lo_ref[z ^ t] - kb * TILE, s, NEG)
            p = jnp.exp(s - row_ref[0:1, both])
            dp = dot_nt(value, do2_ref[both, :])
            ds = p * (dp - row_ref[1:2, both])
            acc_ref[a] += ds
            p_ref[:, both] = p.astype(bf16)
            ds_ref[krows, both] = ds.astype(bf16)
        dk_ref[at] = dot(ds_ref[krows, cols], q2_ref[cols, :]).astype(bf16)
        dv_ref[at] = dot(p_ref[:, cols], do2_ref[cols, :]).astype(bf16)
    kt = k_s[...].T
    for t in range(pieces):
        both = slice(t * 2 * TILE, (t + 1) * 2 * TILE)
        span = slice(t * TILE, (t + TILES_SEEN) * TILE)
        dqt = dot(kt[:, span], ds_ref[span, both]) * 0.125
        dq_ref[z ^ t] = merge_heads(dqt).astype(bf16)
    for a in range(TILES_SEEN):
        for h in range(2):
            part = acc_ref[a, :, h * TILE : (h + 1) * TILE]
            part = jnp.concatenate([part, jnp.zeros_like(part)], axis=1)
            half = TILE // 2
            while half >= 1:
                part = part[:half] + pltpu.roll(part[half:], 2 * TILE - half, 1)
                half //= 2
            tab_ref[0, h, a : a + 1, :] = pltpu.roll(part, TILE, 1)


def bias_tiles(vec, others=()):
    pairs = vec.shape[0]
    return pl.pallas_call(
        behind(bias_kernel, 1, others),
        grid=(pairs,),
        in_specs=[pl.BlockSpec((1, 2, vec.shape[2]), lambda g: (g, 0, 0))] + anywhere(others),
        out_specs=pl.BlockSpec((1, TILES_SEEN, TILE, 2 * TILE), lambda g: (g, 0, 0, 0)),
        out_shape=jax.ShapeDtypeStruct((pairs, TILES_SEEN, TILE, 2 * TILE), bf16),
        compiler_params=pltpu.CompilerParams(vmem_limit_bytes=VMEM),
        cost_estimate=cost(6),
        name="bias_tiles",
    )(vec, *others)


SMEM = pl.BlockSpec(memory_space=pltpu.SMEM)


def attend(ks, z, lo, q, k, v, bias, others=()):
    count, _, width = q.shape
    blocks, pairs = k.shape[0], width // TILE
    part = lambda n: pl.BlockSpec((n, TILE, TILE), lambda g: (0, 0, g))
    return pl.pallas_call(
        behind(functools.partial(attend_kernel, ks), 6, others),
        grid=(pairs,),
        in_specs=[
            SMEM,
            pl.BlockSpec((count, 1, 2 * TILE), lambda g: (0, 0, 0)),
            part(count), part(blocks), part(blocks),
            pl.BlockSpec((1, TILES_SEEN, TILE, 2 * TILE), lambda g: (g, 0, 0, 0)),
        ] + anywhere(others),
        out_specs=[pl.BlockSpec((TILE, TILE), lambda g: (0, g))] * count
        + [pl.BlockSpec((1, count, 1, 2 * TILE), lambda g: (g, 0, 0, 0))],
        out_shape=[jax.ShapeDtypeStruct((TILE, width), bf16)] * count
        + [
            jax.ShapeDtypeStruct((pairs, count, 1, 2 * TILE), f32),
        ],
        scratch_shapes=[
            pltpu.VMEM((TILES_SEEN, TILE, 2 * TILE), f32),
            pltpu.VMEM((TILES_SEEN * TILE, 2 * TILE), bf16),
            pltpu.VMEM((TILES_SEEN * TILE, TILE), bf16),
        ],
        compiler_params=pltpu.CompilerParams(vmem_limit_bytes=VMEM),
        cost_estimate=cost(7.4 * count),
        name="attend",
    )(z, lo, q, k, v, bias, *others)


def attend_back(part_index, part_count, z, lo, lses, q, k, v, bias, o, do, others=()):
    pieces, _, width = q.shape
    blocks, pairs = k.shape[0], width // TILE // part_count
    base = part_index * pairs
    part = lambda n: pl.BlockSpec((n, TILE, TILE), lambda g: (0, 0, base + g))
    alone = lambda n: pl.BlockSpec((n, TILE, TILE), lambda g: (0, 0, g))
    columns = pieces * 2 * TILE
    return pl.pallas_call(
        behind(functools.partial(attend_back_kernel, pieces), 8 + 2 * pieces, others),
        grid=(pairs,),
        in_specs=[
            SMEM,
            pl.BlockSpec((pieces, 1, 2 * TILE), lambda g: (0, 0, 0)),
            pl.BlockSpec((1, pieces // 2, 1, 2 * TILE), lambda g: (base + g, 0, 0, 0)),
            pl.BlockSpec((1, pieces // 2, 1, 2 * TILE), lambda g: (base + g, 0, 0, 0)),
            part(pieces), part(blocks), part(blocks),
            pl.BlockSpec((1, TILES_SEEN, TILE, 2 * TILE), lambda g: (base + g, 0, 0, 0)),
        ]
        + [pl.BlockSpec((TILE, TILE), lambda g: (0, base + g))] * pieces
        + [pl.BlockSpec((TILE, TILE), lambda g: (0, base + g))] * pieces
        + anywhere(others),
        out_specs=[
            alone(pieces), alone(blocks), alone(blocks),
            pl.BlockSpec((1, 2, TILES_SEEN, 2 * TILE), lambda g: (g, 0, 0, 0)),
        ],
        out_shape=[
            jax.ShapeDtypeStruct((pieces, TILE, width // part_count), bf16),
            jax.ShapeDtypeStruct((blocks, TILE, width // part_count), bf16),
            jax.ShapeDtypeStruct((blocks, TILE, width // part_count), bf16),
            jax.ShapeDtypeStruct((pairs, 2, TILES_SEEN, 2 * TILE), f32),
        ],
        scratch_shapes=[
            pltpu.VMEM((columns, TILE), bf16),
            pltpu.VMEM((columns, TILE), bf16),
            pltpu.VMEM((blocks * TILE, columns), bf16),
            pltpu.VMEM((TILE, columns), bf16),
            pltpu.VMEM((TILES_SEEN, TILE, 2 * TILE), f32),
            pltpu.VMEM((8, columns), f32),
            pltpu.VMEM((blocks * TILE, TILE), bf16),
        ],
        compiler_params=pltpu.CompilerParams(vmem_limit_bytes=VMEM),
        cost_estimate=cost(42 / part_count),
        name="attend_back",
    )(z, lo, *lses, q, k, v, bias, *o, *do, *others)


def gelu_parts(v):
    c = np.float32(np.sqrt(2.0 / np.pi))
    t = jnp.tanh(c * (v + 0.044715 * v * v * v))
    half = 0.5 * (1.0 + t)
    return v * half, half + 0.5 * v * (1.0 - t * t) * (c * (1.0 + 3.0 * 0.044715 * v * v))


def expert_kernel(experts, count, held, z_ref, *refs):
    x_refs, c_refs, (wg_ref, wu_ref, wd_ref, wr_ref) = refs[:count], refs[count : 2 * count], refs[2 * count : 2 * count + 4]
    refs = refs[2 * count + 4 + held :]
    gin_refs, refs = refs[:count], refs[count:]
    kept_ref, act_ref, dgp_ref, dup_ref, gcot_ref, gate_out, glog_ref, acc_ref, gg_ref, rp_ref, gate_ref, xs_ref, cs_ref = refs
    step = pl.program_id(0)
    rows = xs_ref.shape[0]
    lane = lax.broadcasted_iota(jnp.int32, (rows, TILE), 1)

    @pl.when(step == 0)
    def _():
        for n in range(count):
            part = slice(n * rows // count, (n + 1) * rows // count)
            xs_ref[part, :] = x_refs[n][...]
            cs_ref[part, :] = c_refs[n][...]
        x = xs_ref[...]
        logits = jnp.where(lane < experts, dot(x, wr_ref[...]), NEG)
        e = jnp.exp(logits - jnp.max(logits, axis=1, keepdims=True))
        probs = e / jnp.sum(e, axis=1, keepdims=True)
        rp_ref[...] = probs
        gate = jnp.sum(jnp.where(lane == z_ref[0], probs, 0.0), axis=1, keepdims=True)
        gate_ref[...] = jnp.broadcast_to(gate, gate_ref.shape)
        gate_out[...] = gate_ref[...]
        kept_ref[...] = x
        gcot_ref[...] = (gate * cs_ref[...].astype(f32)).astype(bf16)
        acc_ref[...] = jnp.zeros_like(acc_ref)
        gg_ref[...] = jnp.zeros_like(gg_ref)

    x, c = xs_ref[...], cs_ref[...]
    raw = dot_nt(c, wd_ref[0])
    gate_pre = dot(x, wg_ref[0])
    up_pre = dot(x, wu_ref[0])
    gelu, slope = gelu_parts(gate_pre)
    act = gelu * up_pre
    act_ref[...] = act.astype(bf16)
    prod = act * raw
    gg_ref[...] += prod[:, :TILE] + prod[:, TILE:]
    scaled = raw * gate_ref[:, :1]
    dgp = (scaled * up_pre * slope).astype(bf16)
    dup = (scaled * gelu).astype(bf16)
    dgp_ref[...] = dgp
    dup_ref[...] = dup
    acc_ref[...] += dot_nt(dgp, wg_ref[0]) + dot_nt(dup, wu_ref[0])

    @pl.when(step == pl.num_programs(0) - 1)
    def _():
        gg = jnp.sum(gg_ref[...], axis=1, keepdims=True)
        own = jnp.where(lane == z_ref[0], 1.0, 0.0)
        glog = gg * rp_ref[...] * (own - gate_ref[...])
        glog_ref[...] = glog
        high = glog.astype(bf16)
        low = (glog - high.astype(f32)).astype(bf16)
        gin = (acc_ref[...] + dot_nt(high, wr_ref[...]) + dot_nt(low, wr_ref[...])).astype(bf16)
        for n in range(count):
            gin_refs[n][...] = gin[n * rows // count : (n + 1) * rows // count]


def expert(index, total, held, z, xs, cs, wg, wu, wd, wr, experts, others=()):
    count, (slot, width) = len(xs), xs[0].shape
    rows = count * slot
    hidden = wg.shape[2]
    wide = 2 * TILE
    whole = pl.BlockSpec((slot, width), lambda f: (0, 0))
    kept = pl.BlockSpec((rows, width), lambda f: (index, 0))
    thin = pl.BlockSpec((rows, TILE), lambda f: (index, 0))
    tile = pl.BlockSpec((rows, wide), lambda f: (index, f))
    full = lambda n, t: jax.ShapeDtypeStruct((total * slot, n), t)
    held = [] if held is None else list(held)
    return pl.pallas_call(
        functools.partial(expert_kernel, experts, count, len(held) + len(others)),
        grid=(hidden // wide,),
        in_specs=[SMEM] + [whole] * (2 * count) + [
            pl.BlockSpec((1, width, wide), lambda f: (0, 0, f)),
            pl.BlockSpec((1, width, wide), lambda f: (0, 0, f)),
            pl.BlockSpec((1, wide, width), lambda f: (0, f, 0)),
            pl.BlockSpec((width, TILE), lambda f: (0, 0)),
        ] + anywhere(held) + anywhere(others),
        out_specs=[whole] * count + [kept, tile, tile, tile, kept, thin, thin],
        out_shape=[jax.ShapeDtypeStruct((slot, width), bf16)] * count + [
            full(width, bf16), full(hidden, bf16), full(hidden, bf16), full(hidden, bf16), full(width, bf16),
            full(TILE, f32), full(TILE, f32),
        ],
        input_output_aliases={2 * count + 5 + i: count + i for i in range(len(held))},
        scratch_shapes=[
            pltpu.VMEM((rows, width), f32), pltpu.VMEM((rows, TILE), f32), pltpu.VMEM((rows, TILE), f32),
            pltpu.VMEM((rows, TILE), f32), pltpu.VMEM((rows, width), bf16), pltpu.VMEM((rows, width), bf16),
        ],
        compiler_params=pltpu.CompilerParams(vmem_limit_bytes=VMEM),
        cost_estimate=cost(10 + 13 * count),
        name="expert",
    )(z, *xs, *cs, wg, wu, wd, wr, *held, *others)


def gate_up_kernel(s_ref, x_ref, dgp_ref, dup_ref, glog_ref, other_ref, mine_ref, router_ref, xt_ref):
    @pl.when(pl.program_id(0) == 0)
    def _():
        xt_ref[...] = x_ref[...].T
        high = glog_ref[...].astype(bf16)
        low = (glog_ref[...] - high.astype(f32)).astype(bf16)
        router_ref[...] = dot(xt_ref[...], high) + dot(xt_ref[...], low)

    first = s_ref[0] == 0
    for n, ref in enumerate((dgp_ref, dup_ref)):
        result = dot(xt_ref[...], ref[...]).astype(bf16).reshape((other_ref.shape[0], 2) + other_ref.shape[2:])
        other_ref[:, n] = jnp.where(first, result[:, 1], result[:, 0])
        mine_ref[:, n] = jnp.where(first, result[:, 0], result[:, 1])


def gate_up_grads(side, chips, x, dgp, dup, glog, others=()):
    rows, width = x.shape
    hidden, wide = dgp.shape[1], 2 * TILE
    part = width // chips // 2
    tile = pl.BlockSpec((rows, wide), lambda f: (0, f))
    out = pl.BlockSpec((chips, 2, part, wide), lambda f: (0, 0, 0, f))
    shape = jax.ShapeDtypeStruct((chips, 2, part, hidden), bf16)
    return pl.pallas_call(
        behind(gate_up_kernel, 5, others),
        grid=(hidden // wide,),
        in_specs=[
            SMEM,
            pl.BlockSpec((rows, width), lambda f: (0, 0)),
            tile,
            tile,
            pl.BlockSpec((rows, TILE), lambda f: (0, 0)),
        ]
        + anywhere(others),
        out_specs=[out, out, pl.BlockSpec((width, TILE), lambda f: (0, 0))],
        out_shape=[shape, shape, jax.ShapeDtypeStruct((width, TILE), f32)],
        scratch_shapes=[pltpu.VMEM((width, rows), bf16)],
        compiler_params=pltpu.CompilerParams(vmem_limit_bytes=VMEM),
        cost_estimate=cost(24),
        name="gate_up_grads",
    )(side, x, dgp, dup, glog, *others)


def down_kernel(s_ref, act_ref, gcot_ref, other_ref, mine_ref, res_ref):
    res_ref[...] = dot(act_ref[...].T, gcot_ref[...]).astype(bf16).reshape(res_ref.shape)
    other_ref[...] = res_ref[:, 1 - s_ref[0]]
    mine_ref[...] = res_ref[:, s_ref[0]]


def down_grads(side, chips, act, gcot, others=()):
    rows, hidden = act.shape
    width, wide = gcot.shape[1], hidden // 2
    part = hidden // chips // 2
    out = pl.BlockSpec((chips // 2, part, width), lambda f: (f, 0, 0))
    shape = jax.ShapeDtypeStruct((chips, part, width), bf16)
    return pl.pallas_call(
        behind(down_kernel, 3, others),
        grid=(2,),
        in_specs=[SMEM, pl.BlockSpec((rows, wide), lambda f: (0, f)), pl.BlockSpec((rows, width), lambda f: (0, 0))]
        + anywhere(others),
        out_specs=[out, out],
        out_shape=[shape, shape],
        scratch_shapes=[pltpu.VMEM((chips // 2, 2, part, width), bf16)],
        compiler_params=pltpu.CompilerParams(vmem_limit_bytes=VMEM),
        cost_estimate=cost(14),
        name="down_grads",
    )(side, act, gcot, *others)


def out_kernel(act_ref, wd_ref, gate_ref, *refs):
    outs, acc_ref = refs[:-1], refs[-1]
    step = pl.program_id(0)
    more = dot(act_ref[...], wd_ref[0])

    @pl.when(step == 0)
    def _():
        acc_ref[...] = more

    @pl.when(step > 0)
    def _():
        acc_ref[...] += more

    @pl.when(step == pl.num_programs(0) - 1)
    def _():
        rows = outs[0].shape[0]
        for n, out in enumerate(outs):
            part = slice(n * rows, (n + 1) * rows)
            out[...] = (acc_ref[part, :] * gate_ref[part, :1]).astype(bf16)


def expert_out(act, wd, gate, chunks, others=()):
    rows, hidden = act.shape
    width, wide = wd.shape[2], hidden // 2
    fixed = lambda r, c: pl.BlockSpec((r, c), lambda f: (0, 0))
    return pl.pallas_call(
        behind(out_kernel, 3, others),
        grid=(hidden // wide,),
        in_specs=[
            pl.BlockSpec((rows, wide), lambda f: (0, f)),
            pl.BlockSpec((1, wide, width), lambda f: (0, f, 0)), fixed(rows, TILE),
        ] + anywhere(others),
        out_specs=[fixed(rows // chunks, width)] * chunks,
        out_shape=[jax.ShapeDtypeStruct((rows // chunks, width), bf16)] * chunks,
        scratch_shapes=[pltpu.VMEM((rows, width), f32)],
        compiler_params=pltpu.CompilerParams(vmem_limit_bytes=VMEM),
        cost_estimate=cost(14),
        name="expert_out",
    )(act, wd, gate, *others)


def norm_kernel(two_ref, one_ref, own_ref, gain_ref, out_ref):
    step = pl.program_id(0)

    def put(ref):
        x = ref[...].astype(f32)
        r = lax.rsqrt(jnp.mean(x * x, axis=-1, keepdims=True) + epsilon)
        out_ref[...] = (x * r * gain_ref[...][None]).astype(bf16)

    for n, ref in enumerate((two_ref, one_ref, own_ref)):
        pl.when(step // 2 == n)(functools.partial(put, ref))


def norm_window(two, one, own, gain):
    pieces, rows, width = own.shape
    some = pieces // 2
    at = lambda n: pl.BlockSpec((some, rows, width), lambda f: (jnp.clip(f - 2 * n, 0, 1), 0, 0))
    return pl.pallas_call(
        norm_kernel,
        grid=(6,),
        in_specs=[at(0), at(1), at(2), pl.BlockSpec((1, width), lambda f: (0, 0))],
        out_specs=pl.BlockSpec((some, rows, width), lambda f: (f, 0, 0)),
        out_shape=jax.ShapeDtypeStruct((3 * pieces, rows, width), bf16),
        compiler_params=pltpu.CompilerParams(vmem_limit_bytes=VMEM),
        cost_estimate=cost(5),
        name="norm_window",
    )(two, one, own, gain)


def turn_kernel(rows_ref, out_ref):
    out_ref[...] = rows_ref[0].T.reshape(out_ref.shape)


def turn_rows(normed, chips, others=()):
    pieces, rows, width = normed.shape
    part = width // chips // 2
    return pl.pallas_call(
        behind(turn_kernel, 1, others),
        grid=(pieces,),
        in_specs=[pl.BlockSpec((1, rows, width), lambda f: (f, 0, 0))] + anywhere(others),
        out_specs=pl.BlockSpec((chips, 2, part, rows), lambda f: (0, 0, 0, f)),
        out_shape=jax.ShapeDtypeStruct((chips, 2, part, pieces * rows), bf16),
        compiler_params=pltpu.CompilerParams(vmem_limit_bytes=VMEM),
        cost_estimate=cost(8),
        name="turn_rows",
    )(normed, *others)


def slot_rows(t_ref, k, slot):
    index = lax.broadcasted_iota(jnp.int32, (slot, t_ref.shape[1]), 0) + k * slot
    return ((index == t_ref[0:1, :]) | (index == t_ref[1:2, :])).astype(bf16)


def row_slots(t_ref, k, slot):
    index = lax.broadcasted_iota(jnp.int32, (t_ref.shape[0], slot), 1) + k * slot
    return ((index == t_ref[:, 0:1]) | (index == t_ref[:, 1:2])).astype(bf16)


def collect(t_ref, refs):
    total = None
    for k, ref in enumerate(refs):
        part = dot(row_slots(t_ref, k, ref.shape[0]), ref[...])
        total = part if total is None else total + part
    return total


def turned(ref, z):
    return jnp.concatenate([ref[z ^ k] for k in range(ref.shape[0])], axis=0)


def call(kernel, ins, outs, us, name, others=(), scratch=()):
    specs = [SMEM if a.ndim == 1 else pl.BlockSpec(memory_space=pltpu.VMEM) for a in ins]
    return pl.pallas_call(
        behind(kernel, len(ins), others),
        in_specs=specs + anywhere(others),
        out_specs=[pl.BlockSpec(memory_space=pltpu.VMEM)] * len(outs),
        out_shape=[jax.ShapeDtypeStruct(shape, dtype) for shape, dtype in outs],
        scratch_shapes=list(scratch),
        compiler_params=pltpu.CompilerParams(vmem_limit_bytes=VMEM),
        cost_estimate=cost(us),
        name=name,
    )(*ins, *others)


def pair_kernel(mine_ref, other_ref, out_ref):
    out_ref[...] = (mine_ref[...].astype(f32) + other_ref[...].astype(f32)).astype(bf16)


def pair_sum(mine, other, others=()):
    block = pl.BlockSpec((1,) + mine.shape[1:], lambda f: (f,) + (0,) * (mine.ndim - 1))
    return pl.pallas_call(
        behind(pair_kernel, 2, others),
        grid=mine.shape[:1],
        in_specs=[block, block] + anywhere(others),
        out_specs=block,
        out_shape=jax.ShapeDtypeStruct(mine.shape, bf16),
        compiler_params=pltpu.CompilerParams(vmem_limit_bytes=VMEM),
        cost_estimate=cost(6),
        name="pair_sum",
    )(mine, other, *others)


def cot_kernel(ks, slot, z_ref, t_ref, cot_ref, *outs):
    values = turned(cot_ref, z_ref[0])
    for k, out in zip(ks, outs):
        out[...] = dot(slot_rows(t_ref, k, slot), values).astype(bf16)


def rows_kernel(ks, slot, t_ref, value_ref, *outs):
    for k, out in zip(ks, outs):
        out[...] = dot(slot_rows(t_ref, k, slot), value_ref[...]).astype(bf16)


def hidden_kernel(ks, slot, z_ref, t_ref, tok_ref, w_ref, gain_ref, *refs):
    pieces = tok_ref.shape[0]
    context, hidden_ref, moe_ref, outs = refs[:pieces], refs[pieces], refs[pieces + 1], refs[pieces + 2 :]
    left = jnp.concatenate([ref[...] for ref in context], axis=0)
    hidden = turned(tok_ref, z_ref[0]).astype(f32) + dot(left, w_ref[...])
    hidden_ref[...] = hidden
    moe_in = norm_rows(hidden, gain_ref[...]).astype(bf16)
    moe_ref[...] = moe_in
    for k, out in zip(ks, outs):
        out[...] = dot(slot_rows(t_ref, k, slot), moe_in).astype(bf16)


def middle_kernel(z_ref, t_ref, hidden_ref, cot_ref, w_ref, gain_ref, *refs):
    pieces = cot_ref.shape[0]
    grad_ref, attn_ref, gain_grad_ref, outs = refs[pieces], refs[pieces + 1], refs[pieces + 2], refs[pieces + 3 :]
    grad_moe = collect(t_ref, refs[:pieces])
    grad_norm, gain_grad = norm_back(hidden_ref[...], gain_ref[...], grad_moe)
    gain_grad_ref[...] = gain_grad[None]
    grad = turned(cot_ref, z_ref[0]).astype(f32) + grad_norm
    grad_ref[...] = grad
    low = grad.astype(bf16)
    attn_ref[...] = low
    context = dot_nt(low, w_ref[...]).astype(bf16)
    rows = context.shape[0] // pieces
    for k in range(pieces):
        outs[k][...] = context[k * rows : (k + 1) * rows]


def mix_kernel(z_ref, t_ref, hidden_ref, *refs):
    out_ref = refs[-1]
    rows = out_ref.shape[1]
    mixed = (hidden_ref[...] + collect(t_ref, refs[:-1])).astype(bf16)
    for k in range(out_ref.shape[0]):
        out_ref[z_ref[0] ^ k] = mixed[k * rows : (k + 1) * rows]


def inputs_kernel(last, dq_ref, dk_ref, dv_ref, wq_ref, wk_ref, wv_ref, *refs):
    step = pl.program_id(0)
    flat = lambda ref: ref[...].reshape(-1, ref.shape[-1])
    grad = dot_nt(flat(dk_ref), wk_ref[...]) + dot_nt(flat(dv_ref), wv_ref[...])
    if not last:
        refs[0][...] = grad

        @pl.when(step == 2)
        def _():
            refs[0][...] = grad + dot_nt(flat(dq_ref), wq_ref[...])

        return
    acc_ref, two_ref, one_ref, own_ref = refs
    grad = grad + acc_ref[...]

    @pl.when(step == 0)
    def _():
        two_ref[...] = grad.astype(bf16)

    @pl.when(step == 1)
    def _():
        one_ref[...] = grad.astype(bf16)

    @pl.when(step == 2)
    def _():
        own_ref[...] = grad + dot_nt(flat(dq_ref), wq_ref[...])


def input_grads(part, dq, dk, dv, wq, wk, wv, acc=None, others=()):
    pieces, rows, some = dq.shape
    width = wq.shape[0]
    block = pieces * rows
    window = pl.BlockSpec((pieces, rows, some), lambda f: (f, 0, 0))
    weight = pl.BlockSpec((width, some), lambda f: (0, part))
    once = pl.BlockSpec((block, width), lambda f: (0, 0))
    step = pl.BlockSpec((block, width), lambda f: (f, 0))
    specs = [pl.BlockSpec((pieces, rows, some), lambda f: (0, 0, 0)), window, window, weight, weight, weight]
    ins, outs = [dq, dk, dv, wq, wk, wv], [(step, (3 * block, width), f32)]
    if acc is not None:
        specs += [step]
        ins += [acc]
        outs = [(once, (block, width), bf16)] * 2 + [(once, (block, width), f32)]
    return pl.pallas_call(
        behind(functools.partial(inputs_kernel, acc is not None), len(ins), others),
        grid=(3,),
        in_specs=specs + anywhere(others),
        out_specs=[o[0] for o in outs],
        out_shape=[jax.ShapeDtypeStruct(o[1], o[2]) for o in outs],
        compiler_params=pltpu.CompilerParams(vmem_limit_bytes=VMEM),
        cost_estimate=cost(7),
        name="input_grads",
    )(*ins, *others)


def leave_kernel(s_ref, z_ref, two_ref, swapped_ref, parts_ref, leave_ref, keep_ref, *refs):
    outs, total_ref = refs[:-1], refs[-1]
    zero = jnp.zeros_like(swapped_ref)
    swapped = swapped_ref[...]
    add = jnp.where(s_ref[0] == 0, zero, swapped)
    leave_ref[...] = (two_ref[...].astype(f32) + add.astype(f32)).astype(bf16)
    keep_ref[...] = jnp.where(s_ref[0] == 0, swapped, zero)
    total = parts_ref[0].astype(f32)
    for i in range(1, parts_ref.shape[0]):
        total = total + parts_ref[i].astype(f32)
    total_ref[...] = total.astype(bf16).reshape(total_ref.shape)
    for k, out in enumerate(outs):
        out[...] = total_ref[z_ref[0] ^ k]


def tail_kernel(z_ref, x_ref, sum_ref, swapped_ref, gain_ref, came_ref, *refs):
    pieces, rows, width = x_ref.shape
    blocks, outs, total_ref = refs[0], refs[1:-1], refs[-1]
    total = blocks[0].astype(f32)
    for i in range(1, blocks.shape[0]):
        total = total + blocks[i].astype(f32)
    total_ref[...] = total.astype(bf16).reshape(total_ref.shape)
    share, long = total_ref.shape[1:]
    for k in range(pieces):
        part = slice(k * rows, (k + 1) * rows)
        grad = sum_ref[part, :] + swapped_ref[part, :].astype(f32) + came_ref[part, :].astype(f32)
        outs[k][:rows, :] = norm_back(x_ref[k].astype(f32), gain_ref[...], grad)[0].astype(bf16)
        theirs = total_ref[z_ref[0] ^ k]
        outs[k][rows : rows + share, :] = theirs[:, :width]
        outs[k][rows + share :, : long - width] = theirs[:, width:]
        outs[k][rows + share :, long - width :] = jnp.zeros((share, 2 * width - long), bf16)


def end_kernel(z_ref, grad_ref, wq_ref, wk_ref, wv_ref, gain_ref, *refs):
    outs = refs[-7:]
    pieces, rows, width = outs[0].shape
    share, long = refs[pieces].shape
    half = (long - width) // 3
    first = refs[pieces][...].astype(f32)
    for k in range(1, pieces):
        first = first + refs[pieces + k][...].astype(f32)
    outs[6][...] = first[:, 3 * half :]
    total = None
    for k in range(pieces):
        outs[0][z_ref[0] ^ k] = (grad_ref[k * rows : (k + 1) * rows, :] + refs[k][:rows, :].astype(f32)).astype(bf16)
        part = jnp.concatenate([refs[k][rows : rows + share, :], refs[k][rows + share :, :]], axis=1).astype(f32)
        total = part if total is None else total + part
    gain = jnp.zeros((share, 1), f32)
    for i, weight in enumerate((wq_ref, wk_ref, wv_ref)):
        parts = (first[:, i * half : (i + 1) * half], total[:, i * half : (i + 1) * half])
        for n, part in enumerate(parts):
            columns = slice(n * half, (n + 1) * half)
            outs[1 + i][:, columns] = part
            gain = gain + jnp.sum(part * weight[:, columns].astype(f32), axis=1, keepdims=True)
    outs[4][...] = total[:, 3 * half : 3 * half + outs[4].shape[1]]
    outs[5][...] = gain / gain_ref[...]


def projection_kernel(third, small, pieces, s_ref, nt_ref, dq_ref, dk_ref, dv_ref, *refs):
    other_ref, mine_ref = refs[small + pieces + (pieces > 0) :][:2]
    step = pl.program_id(0)
    keys = nt_ref.shape[3]
    own = dq_ref.shape[0]

    def put(grad_ref, first):
        for where, ref in ((1 - s_ref[0], other_ref), (s_ref[0], mine_ref)):
            left = nt_ref[:, where, :, first:].reshape(-1, keys - first)
            ref[...] = dot(left, grad_ref[...]).astype(bf16).reshape(ref.shape)

    @pl.when(step < third)
    def _():
        put(dq_ref, keys - own)

    @pl.when((step >= third) & (step < 2 * third))
    def _():
        put(dk_ref, 0)

    @pl.when((step >= 2 * third) & (step < 3 * third))
    def _():
        put(dv_ref, 0)

    if pieces:
        turned_ref, context, attn_ref = refs[-1], refs[:pieces], refs[pieces]
        count = context[0].shape[0]

        @pl.when(step == 3 * third)
        def _():
            for k in range(pieces):
                turned_ref[:, :, :, k * count : (k + 1) * count] = context[k][...].T.reshape(turned_ref.shape[:3] + (count,))

        @pl.when(step >= 3 * third)
        def _():
            for where, ref in ((1 - s_ref[0], other_ref), (s_ref[0], mine_ref)):
                left = turned_ref[:, where].reshape(-1, pieces * count)
                ref[...] = dot(left, attn_ref[...]).astype(bf16).reshape(ref.shape)

    if small:

        @pl.when(step == 3 * third)
        def _():
            other_ref[...] = refs[0][:, 1 - s_ref[0]]
            mine_ref[...] = refs[0][:, s_ref[0]]


def projection_grads(side, normed_t, dq, dk, dv, small=(), context=(), attn=(), others=()):
    chips, _, rows, keys = normed_t.shape
    own, width = dq.shape
    wide = 2 * TILE
    third = width // wide
    at = lambda j: (lambda f: (0, jnp.clip(f - j * third, 0, third - 1)))
    fixed = lambda array: pl.BlockSpec(array.shape, lambda f: (0,) * array.ndim)
    more = len(small) + sum(array.shape[1] // wide for array in attn)
    out = pl.BlockSpec((chips, rows, wide), lambda f: (0, 0, f))
    shape = jax.ShapeDtypeStruct((chips, rows, 3 * width + wide * more), bf16)
    ins = [side, normed_t, dq, dk, dv, *small, *context, *attn]
    scratch = [pltpu.VMEM((chips, 2, rows, len(context) * array.shape[0]), bf16) for array in context[:1]]
    return pl.pallas_call(
        behind(functools.partial(projection_kernel, third, len(small), len(context)), len(ins), others),
        grid=(3 * third + more,),
        in_specs=[
            SMEM,
            fixed(normed_t),
            pl.BlockSpec((own, wide), at(0)),
            pl.BlockSpec((keys, wide), at(1)),
            pl.BlockSpec((keys, wide), at(2)),
        ]
        + [fixed(array) for array in [*small, *context]]
        + [pl.BlockSpec((array.shape[0], wide), lambda f: (0, jnp.maximum(f - 3 * third, 0))) for array in attn]
        + anywhere(others),
        out_specs=[out, out],
        out_shape=[shape, shape],
        scratch_shapes=scratch,
        compiler_params=pltpu.CompilerParams(vmem_limit_bytes=VMEM),
        cost_estimate=cost(9.3 + more),
        name="projection_grads",
    )(*ins, *others)


def shift(x, by):
    count = lax.axis_size("ctx")
    return lax.ppermute(x, "ctx", [(i, i + by) for i in range(count) if 0 <= i + by < count])


def core_swap(x):
    return lax.ppermute(x, "ctx", [(i, i ^ 1) for i in range(lax.axis_size("ctx"))])


def z_swap(x, k):
    if k == 0:
        return x
    return lax.ppermute(x, "exp", [(i, i ^ k) for i in range(lax.axis_size("exp"))])


def over_chips(pair):
    count = lax.axis_size("ctx")
    groups = [list(range(core, count, 2)) for core in range(2)]
    return lax.all_to_all(pair, "ctx", split_axis=0, concat_axis=0, tiled=True, axis_index_groups=groups)


def summed(parts):
    return jnp.sum(parts.astype(f32), axis=0)


def add_pair(mine, other):
    return (mine.astype(f32) + core_swap(other).astype(f32)).astype(bf16)


def norm_rows(values, gain):
    return values * lax.rsqrt(jnp.mean(values * values, axis=-1, keepdims=True) + epsilon) * gain


def norm_back(values, gain, grad):
    r = lax.rsqrt(jnp.mean(values * values, axis=-1, keepdims=True) + epsilon)
    u = grad * gain
    inner = jnp.mean(values * u, axis=-1, keepdims=True)
    return r * u - values * (r * r * r) * inner, jnp.sum(grad * values * r, axis=0)


def on_device(
    tokens, doc_lengths, routes, priority, norm1_gain, w_query, w_key, w_value, w_out, bias_table,
    norm2_gain, w_router, w_gate, w_up, w_down, cotangent,
):
    seqs, piece_len, width = tokens.shape
    exp_count = lax.axis_size("exp")
    ctx_count = lax.axis_size("ctx")
    device_count = exp_count * ctx_count
    block_len = piece_len * exp_count
    rows = seqs * piece_len
    heads = bias_table.shape[0] // bucket_total
    experts = w_router.shape[1]
    slot = 5 * rows // (2 * experts)
    slots = experts * slot
    ctx = lax.axis_index("ctx")
    exp = lax.axis_index("exp")
    side = ctx % 2

    z = jnp.reshape(exp, (1,))
    far_first = [2, 3, 1]

    turn = jnp.arange(seqs, dtype=jnp.int32) ^ exp
    pick = lambda array, k: lax.dynamic_index_in_dim(array, exp ^ k, 0, keepdims=False)

    x_own = [None] * seqs
    for k in [0, 2, 3, 1]:
        x_own[k] = z_swap(pick(tokens, k), k)
    x_pieces = x_own
    x_two = [shift(piece, 2) for piece in x_own]
    x_own, x_two = jnp.stack(x_own), jnp.stack(x_two)
    x_one = core_swap(jnp.where(side == 0, x_own, x_two))

    route_rows = jnp.take(routes, turn, axis=0).reshape(rows, 2)
    order = jnp.take(priority, turn, axis=0).reshape(rows)
    earlier = order[None, :] < order[:, None]
    r0, r1 = route_rows[:, 0], route_rows[:, 1]
    place0 = jnp.sum((earlier & (r0[None, :] == r0[:, None])).astype(jnp.int32), axis=1)
    place1 = jnp.sum((earlier & (r1[None, :] == r1[:, None])).astype(jnp.int32), axis=1) + jnp.sum(
        (r0[None, :] == r1[:, None]).astype(jnp.int32), axis=1
    )
    target0 = jnp.where(place0 < slot, (r0 ^ exp) * slot + place0, -1)
    target1 = jnp.where(place1 < slot, (r1 ^ exp) * slot + place1, -1)
    targets = jnp.stack([target0, target1])
    targets_t = targets.T
    slot_shape = ((slot, width), bf16)
    sent = call(
        functools.partial(cot_kernel, far_first + [0], slot), [z, targets, cotangent], [slot_shape] * experts, 4, "cot_rows", x_pieces[1:]
    )
    cot_slots = [None] * experts
    for k, rows_k in zip(far_first + [0], sent):
        cot_slots[k] = z_swap(rows_k, k)

    distance = np.arange(-TILE, WINDOW + TILE)
    seen = (distance >= 0) & (distance < WINDOW)
    hot = (bucket_of(np.clip(distance, 0, None))[None, :] == np.arange(bucket_total)[:, None]) & seen[None, :]
    vec = exact_dot(bias_table.astype(f32).reshape(heads, bucket_total), jnp.asarray(hot, f32))
    vec = jnp.where(jnp.asarray(seen)[None, :], vec, NEG).reshape(heads // 2, 2, -1)
    bias = bias_tiles(vec, sent[:1])

    ends = jnp.cumsum(lax.dynamic_index_in_dim(doc_lengths, exp, 0, keepdims=False))
    piece_start = ctx * block_len + turn[:, None] * piece_len
    q_pos = piece_start + jnp.arange(piece_len, dtype=jnp.int32)[None, :]
    start = jnp.max(jnp.where(ends <= q_pos[..., None], ends, 0), axis=2)
    lo = start - (ctx - 2) * block_len
    lo = jnp.broadcast_to(lo[:, None, None, :], (seqs, 1, 2, TILE)).reshape(seqs, 1, 2 * TILE)

    gain_one = norm1_gain.astype(f32)
    normed_pieces = norm_window(x_two, x_one, x_own, gain_one[None])
    normed = normed_pieces.reshape(-1, width)
    normed_own = normed[2 * block_len :]
    q = (dot(normed_own, w_query).astype(bf16) * 0.125).astype(bf16).reshape(seqs, piece_len, width)
    k_win = dot(normed, w_key).astype(bf16).reshape(-1, TILE, width)
    v_win = dot(normed, w_value).astype(bf16).reshape(-1, TILE, width)
    contexts, lses, context_rows = [None] * seqs, [], [None] * seqs
    for first in (2, 0):
        others = [contexts[2], cot_slots[2]] if first == 0 else []
        *c, l = attend((first, first + 1), z, lo[first : first + 2], q[first : first + 2], k_win, v_win, bias, others)
        lses.insert(0, l)
        for k in (first, first + 1):
            contexts[k] = c[k - first]
            context_rows[k] = z_swap(contexts[k], k)
    normed_t = turn_rows(normed_pieces, ctx_count // 2, contexts[:1])
    router_wide = jnp.pad(w_router, ((0, 0), (0, TILE - experts)))
    gain_two = norm2_gain.astype(f32)[None]
    hidden, moe_in, *sent = call(
        functools.partial(hidden_kernel, [2, 0], slot),
        [z, targets, tokens, w_out, gain_two] + context_rows,
        [((rows, width), f32), ((rows, width), bf16), slot_shape, slot_shape], 9, "hidden_rows", [cot_slots[1], cot_slots[3], normed_t],
    )
    inputs = [sent[1], None, z_swap(sent[0], 2), None]
    held, returned, turns = None, [None] * experts, [0, 2, 1, 3]
    for ks, index in (([0], 0), ([2], 1), ([1], 2), ([3], 3)):
        found = expert(
            index, experts, held, z, [inputs[k] for k in ks], [cot_slots[k] for k in ks], w_gate, w_up, w_down, router_wide, experts
        )
        back, held = found[: len(ks)], found[len(ks) :]
        for k, rows_k in zip(ks, back):
            returned[k] = z_swap(rows_k, k)
        if index == 0:
            sent = call(functools.partial(rows_kernel, [3, 1], slot), [targets, moe_in], [slot_shape] * 2, 3, "moe_rows", back)
            inputs[3], inputs[1] = z_swap(sent[0], 3), z_swap(sent[1], 1)
    all_inputs, act_low, grad_gate_pre, grad_up_pre, grad_out_slots, gate, grad_logits = held
    chips = ctx_count // 2
    side_ref = jnp.reshape(side, (1,))
    produced = expert_out(act_low, w_down, gate, experts, [returned[2]])
    down_other, down_mine = down_grads(side_ref, chips, act_low, grad_out_slots, produced[:1])

    part_count = 2
    part_width = width // part_count
    grad_hidden, grad_attn, grad_gain_two, *sent_back = call(
        middle_kernel, [z, targets_t, hidden, cotangent, w_out, gain_two] + returned,
        [((rows, width), f32), ((rows, width), bf16), ((1, width), f32)] + [((piece_len, width), bf16)] * seqs,
        9, "middle_rows", [down_other],
    )
    arrived = [z_swap(sent_back[k], k) for k in range(seqs)]
    other, mine, router_part = gate_up_grads(
        side_ref, chips, all_inputs, grad_gate_pre, grad_up_pre, grad_logits, sent_back[-1:]
    )
    grad_router_part = router_part[:, :experts]
    pair = pair_sum(mine, core_swap(other))
    both = over_chips(pair)
    down_other = core_swap(down_other)
    given = [z_swap(produced[turns.index(k)], k) for k in range(experts)]

    weights = (w_query, w_key, w_value)
    flat = lambda grads: [grad.reshape(-1, part_width) for grad in grads]
    back = lambda n, others: attend_back(n, part_count, z, lo, lses, q, k_win, v_win, bias, contexts, arrived, others)
    *grads, diagonal = back(0, [pair])
    other, mine = projection_grads(
        side_ref, normed_t, *flat(grads), context=context_rows, attn=[grad_attn], others=[given[2], given[1]]
    )
    first_pair = add_pair(mine, other)
    first_parts = over_chips(first_pair)
    acc = input_grads(0, *grads, *weights, others=[other])[0]
    *grads, more = back(1, [acc, first_pair, both])
    diagonals = jnp.concatenate([diagonal, more])
    places = np.arange((TILES_SEEN) * 2 * TILE).reshape(TILES_SEEN, 2 * TILE)
    block, lane = places // (2 * TILE), places % (2 * TILE)
    where_dist = lane - TILE + (TILES_SEEN - 1 - block) * TILE
    ok = (where_dist >= 0) & (where_dist < WINDOW)
    to_bucket = (bucket_of(np.clip(where_dist, 0, None))[..., None] == np.arange(bucket_total)) & ok[..., None]
    table_part = exact_dot(diagonals.reshape(heads, -1), jnp.asarray(to_bucket.reshape(-1, bucket_total), f32))
    small = [
        grad_gain_two.reshape(device_count, -1),
        table_part.reshape(device_count, -1),
        grad_router_part.reshape(device_count, -1),
    ]
    cuts = np.cumsum([0] + [item.shape[1] for item in small])
    packed = jnp.concatenate(small, axis=1)
    share = width // device_count
    packed = jnp.pad(packed, ((0, 0), (0, -packed.shape[1] % share))).reshape(width, -1)
    packed = jnp.pad(packed.astype(bf16), ((0, 0), (0, 2 * TILE - packed.shape[1])))
    packed = packed.reshape(ctx_count // 2, 2, -1, 2 * TILE)
    other, mine = projection_grads(side_ref, normed_t, *flat(grads), small=[packed], others=[first_parts, given[3]])
    pair = add_pair(mine, other)
    last = over_chips(pair)
    part_two, part_one, own_sum = input_grads(1, *grads, *weights, acc, [pair])
    leave, swapped, *first = call(
        leave_kernel, [side_ref, z, part_two, core_swap(part_one), first_parts],
        [((block_len, width), bf16)] * 2 + [((share, first_parts.shape[-1]), bf16)] * seqs, 5, "leaving_rows", [last],
        [pltpu.VMEM((exp_count, share, first_parts.shape[-1]), bf16)],
    )
    first = [z_swap(piece, k) for k, piece in enumerate(first)]
    came = shift(leave, -2)
    down = over_chips(pair_sum(down_mine, down_other, [leave]))
    mixed = call(
        mix_kernel, [z, targets_t, hidden] + given, [((seqs, piece_len, width), bf16)], 8, "mixed_rows", [leave]
    )[0]
    share = width // device_count
    long = pair.shape[-1]
    pieces = call(
        tail_kernel, [z, x_own, own_sum, swapped, gain_one[None], came, last],
        [((piece_len + 2 * share, width), bf16)] * seqs, 8, "tail_rows", [mixed] + first[1:],
        [pltpu.VMEM((exp_count, share, long), bf16)],
    )
    pieces = [z_swap(piece, k) for k, piece in enumerate(pieces)]
    grad_gate, grad_up, grad_down = summed(both[:, 0]), summed(both[:, 1]), summed(down)
    own_rows = lambda array: lax.dynamic_slice_in_dim(array, (ctx * exp_count + exp) * share, share, 0)
    grad_tokens, grad_query, grad_key, grad_value, packed, norm1_out, grad_out = call(
        end_kernel,
        [z, grad_hidden] + [own_rows(array) for array in weights] + [own_rows(gain_one[:, None])] + pieces + first,
        [((seqs, piece_len, width), bf16)] + [((share, width), f32)] * 3 + [((share, 2 * TILE), f32), ((share, 1), f32)]
        + [((share, width), f32)],
        6, "end_rows", [grad_down],
    )
    packed = packed[:, : -(-cuts[-1] // share)].reshape(-1)
    norm1_out = norm1_out[:, 0]
    norm2_out, table_out, router_out = [packed[cuts[i] : cuts[i + 1]] for i in range(3)]
    return (
        mixed, grad_tokens, norm1_out, grad_query, grad_key, grad_value, grad_out, table_out, norm2_out,
        router_out.reshape(-1, experts), grad_gate[None], grad_up[None], grad_down[None],
    )


def solution(mesh):
    rows = P(None, ("ctx", "exp"), None)
    flat = P(("ctx", "exp"))
    in_specs = (
        rows, P(), rows, P(None, ("ctx", "exp")), P(), P(), P(), P(), P(), P(), P(), P(),
        P("exp", None, None), P("exp", None, None), P("exp", None, None), rows,
    )
    out_specs = (
        rows, rows, flat, P(("ctx", "exp"), None), P(("ctx", "exp"), None), P(("ctx", "exp"), None),
        P(("ctx", "exp"), None), flat, flat, P(("ctx", "exp"), None),
        P("exp", "ctx", None), P("exp", "ctx", None), P("exp", "ctx", None),
    )
    return jax.shard_map(on_device, mesh=mesh, in_specs=in_specs, out_specs=out_specs, check_vma=False)
```

```python
import functools

import jax
import jax.numpy as jnp
import numpy as np
from jax import lax
from jax.experimental import pallas as pl
from jax.experimental.pallas import tpu as pltpu
from jax.sharding import PartitionSpec as P

WINDOW = 1024
TILE = 128
TILES_SEEN = WINDOW // TILE + 1
epsilon = 1e-06
bucket_total = 32
NEG = -1e30
f32 = jnp.float32
bf16 = jnp.bfloat16
VMEM = 56 * 1024 * 1024


def cost(us):
    return pl.CostEstimate(flops=int(us * 1.15e9), bytes_accessed=0, transcendentals=0)


def behind(kernel, inputs, others):
    return lambda *refs: kernel(*refs[:inputs], *refs[inputs + len(others) :])


def anywhere(others):
    return [pl.BlockSpec(memory_space=pl.ANY)] * len(others)


def dot(left, right):
    return jnp.dot(left, right, preferred_element_type=f32)


def dot_nt(left, right):
    return lax.dot_general(left, right, (((1,), (1,)), ((), ())), preferred_element_type=f32)


def dot_tn(left, right):
    return lax.dot_general(left, right, (((0,), (0,)), ((), ())), preferred_element_type=f32)


def exact_dot(left, right):
    return jnp.dot(left, right, precision=lax.Precision.HIGHEST, preferred_element_type=f32)


def bucket_of(distance):
    limits = np.ceil(16.0 * 8.0 ** (np.arange(1, 16) / 16.0)).astype(np.int32)
    above = np.sum(distance[..., None] >= limits, axis=-1)
    return np.where(distance < 16, distance, 16 + above)


def bias_kernel(vec_ref, out_ref):
    for a in range(TILES_SEEN):
        first = (TILES_SEEN - 1 - a) * TILE
        for h in range(2):
            row = vec_ref[0, h : h + 1, first : first + 2 * TILE]
            wide = jnp.broadcast_to(row, (TILE, 2 * TILE))
            rolled = pltpu.roll(wide, TILE, 1, stride=1, stride_axis=0)
            out_ref[0, a, :, h * TILE : (h + 1) * TILE] = rolled[:, :TILE].astype(bf16)


def split_heads(x):
    lane = lax.broadcasted_iota(jnp.int32, x.shape, 1)
    zero = jnp.zeros_like(x)
    return jnp.concatenate([jnp.where(lane < 64, x, zero), jnp.where(lane < 64, zero, x)], axis=0)


def merge_heads(xt):
    return jnp.concatenate([xt[:64, :TILE], xt[64:, TILE:]], axis=0).T


def key_block(kb, z):
    return (kb // 4) * 4 + ((kb % 4) ^ z)


def attend_kernel(ks, z_ref, lo_ref, q_ref, k_ref, v_ref, b_ref, *refs):
    outs, (lse_ref, s_ref, p_ref, v_s) = refs[: len(ks)], refs[len(ks) :]
    z = z_ref[0]
    row = lax.broadcasted_iota(jnp.int32, (TILE, 2 * TILE), 0)
    for i, (p, n) in enumerate((p, n) for p in range(2) for n in range(len(ks))):
        pair = slice(p * TILE, (p + 1) * TILE)
        t = z ^ ks[n]
        q2 = split_heads(q_ref[n, :, pair])
        lo = lo_ref[n] - t * TILE
        top = jnp.full((8, 2 * TILE), NEG, f32)
        for a in range(TILES_SEEN):
            at = key_block(t + a, z)
            v_s[i, a * TILE : (a + 1) * TILE, :] = v_ref[at, :, pair]
            s = dot_nt(k_ref[at, :, pair], q2) + b_ref[p, a].astype(f32)
            s = jnp.where(row >= lo - a * TILE, s, NEG)
            s_ref[i, a] = s
            top = jnp.maximum(top, jnp.max(s.reshape(TILE // 8, 8, 2 * TILE), axis=0))
        top = jnp.max(top, axis=0, keepdims=True)
        total = jnp.zeros((8, 2 * TILE), f32)
        for a in range(TILES_SEEN):
            e = jnp.exp(s_ref[i, a] - top)
            total = total + jnp.sum(e.reshape(TILE // 8, 8, 2 * TILE), axis=0)
            p_ref[i, a * TILE : (a + 1) * TILE, :] = e.astype(bf16)
        total = jnp.sum(total, axis=0, keepdims=True)
        ct = dot(v_s[i].T, p_ref[i]) / total
        outs[n][:, pair] = merge_heads(ct).astype(bf16)
        lse_ref[p, n] = top + jnp.log(total)


def attend_back_kernel(pieces, z_ref, lo_ref, lse_a, lse_b, q_ref, k_ref, v_ref, b_ref, *refs):
    o_refs, do_refs = refs[:pieces], refs[pieces : 2 * pieces]
    dq_ref, dk_ref, dv_ref, tab_ref, q2_ref, do2_ref, ds_ref, p_ref, acc_ref, row_ref, k_s = refs[2 * pieces :]
    z = z_ref[0]
    row = lax.broadcasted_iota(jnp.int32, (TILE, 2 * TILE), 0)
    for k in range(pieces):
        both = pl.ds(pl.multiple_of((z ^ k) * 2 * TILE, 2 * TILE), 2 * TILE)
        out, grad = o_refs[k][...], do_refs[k][...]
        q2_ref[both, :] = split_heads(q_ref[k])
        do2_ref[both, :] = split_heads(grad)
        prod = (grad.astype(f32) * out.astype(f32)).T
        lse_ref = lse_a if k < pieces // 2 else lse_b
        row_ref[0:1, both] = lse_ref[0, k % (pieces // 2)]
        row_ref[1:2, both] = jnp.concatenate(
            [jnp.sum(prod[:64], axis=0, keepdims=True), jnp.sum(prod[64:], axis=0, keepdims=True)], axis=1
        )
    acc_ref[...] = jnp.zeros_like(acc_ref)
    keys = pieces + TILES_SEEN - 1
    for kb in range(keys):
        first, last = max(0, kb - TILES_SEEN + 1), min(pieces - 1, kb)
        krows = slice(kb * TILE, (kb + 1) * TILE)
        cols = slice(first * 2 * TILE, (last + 1) * 2 * TILE)
        at = key_block(kb, z)
        key, value = k_ref[at], v_ref[at]
        k_s[krows, :] = key
        for t in range(first, last + 1):
            both = slice(t * 2 * TILE, (t + 1) * 2 * TILE)
            a = kb - t
            s = dot_nt(key, q2_ref[both, :]) + b_ref[0, a].astype(f32)
            s = jnp.where(row >= lo_ref[z ^ t] - kb * TILE, s, NEG)
            p = jnp.exp(s - row_ref[0:1, both])
            dp = dot_nt(value, do2_ref[both, :])
            ds = p * (dp - row_ref[1:2, both])
            acc_ref[a] += ds
            p_ref[:, both] = p.astype(bf16)
            ds_ref[krows, both] = ds.astype(bf16)
        dk_ref[at] = dot(ds_ref[krows, cols], q2_ref[cols, :]).astype(bf16)
        dv_ref[at] = dot(p_ref[:, cols], do2_ref[cols, :]).astype(bf16)
    kt = k_s[...].T
    for t in range(pieces):
        both = slice(t * 2 * TILE, (t + 1) * 2 * TILE)
        span = slice(t * TILE, (t + TILES_SEEN) * TILE)
        dqt = dot(kt[:, span], ds_ref[span, both]) * 0.125
        dq_ref[z ^ t] = merge_heads(dqt).astype(bf16)
    for a in range(TILES_SEEN):
        for h in range(2):
            part = acc_ref[a, :, h * TILE : (h + 1) * TILE]
            part = jnp.concatenate([part, jnp.zeros_like(part)], axis=1)
            half = TILE // 2
            while half >= 1:
                part = part[:half] + pltpu.roll(part[half:], 2 * TILE - half, 1)
                half //= 2
            tab_ref[0, h, a : a + 1, :] = pltpu.roll(part, TILE, 1)


def bias_tiles(vec, others=()):
    pairs = vec.shape[0]
    return pl.pallas_call(
        behind(bias_kernel, 1, others),
        grid=(pairs,),
        in_specs=[pl.BlockSpec((1, 2, vec.shape[2]), lambda g: (g, 0, 0))] + anywhere(others),
        out_specs=pl.BlockSpec((1, TILES_SEEN, TILE, 2 * TILE), lambda g: (g, 0, 0, 0)),
        out_shape=jax.ShapeDtypeStruct((pairs, TILES_SEEN, TILE, 2 * TILE), bf16),
        compiler_params=pltpu.CompilerParams(vmem_limit_bytes=VMEM),
        cost_estimate=cost(6),
        name="bias_tiles",
    )(vec, *others)


SMEM = pl.BlockSpec(memory_space=pltpu.SMEM)


def attend(ks, z, lo, q, k, v, bias, others=()):
    count, _, width = q.shape
    blocks, pairs = k.shape[0], width // TILE
    part = lambda n: pl.BlockSpec((n, TILE, 2 * TILE), lambda g: (0, 0, g))
    return pl.pallas_call(
        behind(functools.partial(attend_kernel, ks), 6, others),
        grid=(pairs // 2,),
        in_specs=[
            SMEM,
            pl.BlockSpec((count, 1, 2 * TILE), lambda g: (0, 0, 0)),
            part(count), part(blocks), part(blocks),
            pl.BlockSpec((2, TILES_SEEN, TILE, 2 * TILE), lambda g: (g, 0, 0, 0)),
        ] + anywhere(others),
        out_specs=[pl.BlockSpec((TILE, 2 * TILE), lambda g: (0, g))] * count
        + [pl.BlockSpec((2, count, 1, 2 * TILE), lambda g: (g, 0, 0, 0))],
        out_shape=[jax.ShapeDtypeStruct((TILE, width), bf16)] * count
        + [
            jax.ShapeDtypeStruct((pairs, count, 1, 2 * TILE), f32),
        ],
        scratch_shapes=[
            pltpu.VMEM((2 * count, TILES_SEEN, TILE, 2 * TILE), f32),
            pltpu.VMEM((2 * count, TILES_SEEN * TILE, 2 * TILE), bf16),
            pltpu.VMEM((2 * count, TILES_SEEN * TILE, TILE), bf16),
        ],
        compiler_params=pltpu.CompilerParams(vmem_limit_bytes=VMEM),
        cost_estimate=cost(6 * count),
        name="attend",
    )(z, lo, q, k, v, bias, *others)


def attend_back(part_index, part_count, z, lo, lses, q, k, v, bias, o, do, others=()):
    pieces, _, width = q.shape
    blocks, pairs = k.shape[0], width // TILE // part_count
    base = part_index * pairs
    part = lambda n: pl.BlockSpec((n, TILE, TILE), lambda g: (0, 0, base + g))
    alone = lambda n: pl.BlockSpec((n, TILE, TILE), lambda g: (0, 0, g))
    columns = pieces * 2 * TILE
    return pl.pallas_call(
        behind(functools.partial(attend_back_kernel, pieces), 8 + 2 * pieces, others),
        grid=(pairs,),
        in_specs=[
            SMEM,
            pl.BlockSpec((pieces, 1, 2 * TILE), lambda g: (0, 0, 0)),
            pl.BlockSpec((1, pieces // 2, 1, 2 * TILE), lambda g: (base + g, 0, 0, 0)),
            pl.BlockSpec((1, pieces // 2, 1, 2 * TILE), lambda g: (base + g, 0, 0, 0)),
            part(pieces), part(blocks), part(blocks),
            pl.BlockSpec((1, TILES_SEEN, TILE, 2 * TILE), lambda g: (base + g, 0, 0, 0)),
        ]
        + [pl.BlockSpec((TILE, TILE), lambda g: (0, base + g))] * pieces
        + [pl.BlockSpec((TILE, TILE), lambda g: (0, base + g))] * pieces
        + anywhere(others),
        out_specs=[
            alone(pieces), alone(blocks), alone(blocks),
            pl.BlockSpec((1, 2, TILES_SEEN, 2 * TILE), lambda g: (g, 0, 0, 0)),
        ],
        out_shape=[
            jax.ShapeDtypeStruct((pieces, TILE, width // part_count), bf16),
            jax.ShapeDtypeStruct((blocks, TILE, width // part_count), bf16),
            jax.ShapeDtypeStruct((blocks, TILE, width // part_count), bf16),
            jax.ShapeDtypeStruct((pairs, 2, TILES_SEEN, 2 * TILE), f32),
        ],
        scratch_shapes=[
            pltpu.VMEM((columns, TILE), bf16),
            pltpu.VMEM((columns, TILE), bf16),
            pltpu.VMEM((blocks * TILE, columns), bf16),
            pltpu.VMEM((TILE, columns), bf16),
            pltpu.VMEM((TILES_SEEN, TILE, 2 * TILE), f32),
            pltpu.VMEM((8, columns), f32),
            pltpu.VMEM((blocks * TILE, TILE), bf16),
        ],
        compiler_params=pltpu.CompilerParams(vmem_limit_bytes=VMEM),
        cost_estimate=cost(42 / part_count),
        name="attend_back",
    )(z, lo, *lses, q, k, v, bias, *o, *do, *others)


def gelu_parts(v):
    c = np.float32(np.sqrt(2.0 / np.pi))
    t = jnp.tanh(c * (v + 0.044715 * v * v * v))
    half = 0.5 * (1.0 + t)
    return v * half, half + 0.5 * v * (1.0 - t * t) * (c * (1.0 + 3.0 * 0.044715 * v * v))


def expert_kernel(experts, count, held, z_ref, *refs):
    x_refs, c_refs, (wg_ref, wu_ref, wd_ref, wr_ref) = refs[:count], refs[count : 2 * count], refs[2 * count : 2 * count + 4]
    refs = refs[2 * count + 4 + held :]
    gin_refs, refs = refs[:count], refs[count:]
    kept_ref, act_ref, dgp_ref, dup_ref, gcot_ref, gate_out, glog_ref, acc_ref, gg_ref, rp_ref, gate_ref, xs_ref, cs_ref = refs
    step = pl.program_id(0)
    rows = xs_ref.shape[0]
    lane = lax.broadcasted_iota(jnp.int32, (rows, TILE), 1)

    @pl.when(step == 0)
    def _():
        for n in range(count):
            part = slice(n * rows // count, (n + 1) * rows // count)
            xs_ref[part, :] = x_refs[n][...]
            cs_ref[part, :] = c_refs[n][...]
        x = xs_ref[...]
        logits = jnp.where(lane < experts, dot(x, wr_ref[...]), NEG)
        e = jnp.exp(logits - jnp.max(logits, axis=1, keepdims=True))
        probs = e / jnp.sum(e, axis=1, keepdims=True)
        rp_ref[...] = probs
        gate = jnp.sum(jnp.where(lane == z_ref[0], probs, 0.0), axis=1, keepdims=True)
        gate_ref[...] = jnp.broadcast_to(gate, gate_ref.shape)
        gate_out[...] = gate_ref[...]
        kept_ref[...] = x
        gcot_ref[...] = (gate * cs_ref[...].astype(f32)).astype(bf16)
        acc_ref[...] = jnp.zeros_like(acc_ref)
        gg_ref[...] = jnp.zeros_like(gg_ref)

    x, c = xs_ref[...], cs_ref[...]
    raw = dot_nt(c, wd_ref[0])
    gate_pre = dot(x, wg_ref[0])
    up_pre = dot(x, wu_ref[0])
    gelu, slope = gelu_parts(gate_pre)
    act = gelu * up_pre
    act_ref[...] = act.astype(bf16)
    prod = act * raw
    gg_ref[...] += prod[:, :TILE] + prod[:, TILE:]
    scaled = raw * gate_ref[:, :1]
    dgp = (scaled * up_pre * slope).astype(bf16)
    dup = (scaled * gelu).astype(bf16)
    dgp_ref[...] = dgp
    dup_ref[...] = dup
    acc_ref[...] += dot_nt(dgp, wg_ref[0]) + dot_nt(dup, wu_ref[0])

    @pl.when(step == pl.num_programs(0) - 1)
    def _():
        gg = jnp.sum(gg_ref[...], axis=1, keepdims=True)
        own = jnp.where(lane == z_ref[0], 1.0, 0.0)
        glog = gg * rp_ref[...] * (own - gate_ref[...])
        glog_ref[...] = glog
        high = glog.astype(bf16)
        low = (glog - high.astype(f32)).astype(bf16)
        gin = (acc_ref[...] + dot_nt(high, wr_ref[...]) + dot_nt(low, wr_ref[...])).astype(bf16)
        for n in range(count):
            gin_refs[n][...] = gin[n * rows // count : (n + 1) * rows // count]


def expert(index, total, held, z, xs, cs, wg, wu, wd, wr, experts, others=()):
    count, (slot, width) = len(xs), xs[0].shape
    rows = count * slot
    hidden = wg.shape[2]
    wide = 2 * TILE
    whole = pl.BlockSpec((slot, width), lambda f: (0, 0))
    kept = pl.BlockSpec((rows, width), lambda f: (index, 0))
    thin = pl.BlockSpec((rows, TILE), lambda f: (index, 0))
    tile = pl.BlockSpec((rows, wide), lambda f: (index, f))
    full = lambda n, t: jax.ShapeDtypeStruct((total * slot, n), t)
    held = [] if held is None else list(held)
    return pl.pallas_call(
        functools.partial(expert_kernel, experts, count, len(held) + len(others)),
        grid=(hidden // wide,),
        in_specs=[SMEM] + [whole] * (2 * count) + [
            pl.BlockSpec((1, width, wide), lambda f: (0, 0, f)),
            pl.BlockSpec((1, width, wide), lambda f: (0, 0, f)),
            pl.BlockSpec((1, wide, width), lambda f: (0, f, 0)),
            pl.BlockSpec((width, TILE), lambda f: (0, 0)),
        ] + anywhere(held) + anywhere(others),
        out_specs=[whole] * count + [kept, tile, tile, tile, kept, thin, thin],
        out_shape=[jax.ShapeDtypeStruct((slot, width), bf16)] * count + [
            full(width, bf16), full(hidden, bf16), full(hidden, bf16), full(hidden, bf16), full(width, bf16),
            full(TILE, f32), full(TILE, f32),
        ],
        input_output_aliases={2 * count + 5 + i: count + i for i in range(len(held))},
        scratch_shapes=[
            pltpu.VMEM((rows, width), f32), pltpu.VMEM((rows, TILE), f32), pltpu.VMEM((rows, TILE), f32),
            pltpu.VMEM((rows, TILE), f32), pltpu.VMEM((rows, width), bf16), pltpu.VMEM((rows, width), bf16),
        ],
        compiler_params=pltpu.CompilerParams(vmem_limit_bytes=VMEM),
        cost_estimate=cost(10 + 13 * count),
        name="expert",
    )(z, *xs, *cs, wg, wu, wd, wr, *held, *others)


def gate_up_kernel(s_ref, x_ref, dgp_ref, dup_ref, glog_ref, other_ref, mine_ref, router_ref, xt_ref):
    @pl.when(pl.program_id(0) == 0)
    def _():
        xt_ref[...] = x_ref[...].T
        high = glog_ref[...].astype(bf16)
        low = (glog_ref[...] - high.astype(f32)).astype(bf16)
        router_ref[...] = dot(xt_ref[...], high) + dot(xt_ref[...], low)

    first = s_ref[0] == 0
    for n, ref in enumerate((dgp_ref, dup_ref)):
        result = dot(xt_ref[...], ref[...]).astype(bf16).reshape((other_ref.shape[0], 2) + other_ref.shape[2:])
        other_ref[:, n] = jnp.where(first, result[:, 1], result[:, 0])
        mine_ref[:, n] = jnp.where(first, result[:, 0], result[:, 1])


def gate_up_grads(side, chips, x, dgp, dup, glog, others=()):
    rows, width = x.shape
    hidden, wide = dgp.shape[1], 2 * TILE
    part = width // chips // 2
    tile = pl.BlockSpec((rows, wide), lambda f: (0, f))
    out = pl.BlockSpec((chips, 2, part, wide), lambda f: (0, 0, 0, f))
    shape = jax.ShapeDtypeStruct((chips, 2, part, hidden), bf16)
    return pl.pallas_call(
        behind(gate_up_kernel, 5, others),
        grid=(hidden // wide,),
        in_specs=[
            SMEM,
            pl.BlockSpec((rows, width), lambda f: (0, 0)),
            tile,
            tile,
            pl.BlockSpec((rows, TILE), lambda f: (0, 0)),
        ]
        + anywhere(others),
        out_specs=[out, out, pl.BlockSpec((width, TILE), lambda f: (0, 0))],
        out_shape=[shape, shape, jax.ShapeDtypeStruct((width, TILE), f32)],
        scratch_shapes=[pltpu.VMEM((width, rows), bf16)],
        compiler_params=pltpu.CompilerParams(vmem_limit_bytes=VMEM),
        cost_estimate=cost(24),
        name="gate_up_grads",
    )(side, x, dgp, dup, glog, *others)


def down_kernel(s_ref, act_ref, gcot_ref, other_ref, mine_ref, res_ref):
    res_ref[...] = dot(act_ref[...].T, gcot_ref[...]).astype(bf16).reshape(res_ref.shape)
    other_ref[...] = res_ref[:, 1 - s_ref[0]]
    mine_ref[...] = res_ref[:, s_ref[0]]


def down_grads(side, chips, act, gcot, others=()):
    rows, hidden = act.shape
    width, wide = gcot.shape[1], hidden // 2
    part = hidden // chips // 2
    out = pl.BlockSpec((chips // 2, part, width), lambda f: (f, 0, 0))
    shape = jax.ShapeDtypeStruct((chips, part, width), bf16)
    return pl.pallas_call(
        behind(down_kernel, 3, others),
        grid=(2,),
        in_specs=[SMEM, pl.BlockSpec((rows, wide), lambda f: (0, f)), pl.BlockSpec((rows, width), lambda f: (0, 0))]
        + anywhere(others),
        out_specs=[out, out],
        out_shape=[shape, shape],
        scratch_shapes=[pltpu.VMEM((chips // 2, 2, part, width), bf16)],
        compiler_params=pltpu.CompilerParams(vmem_limit_bytes=VMEM),
        cost_estimate=cost(14),
        name="down_grads",
    )(side, act, gcot, *others)


def out_kernel(act_ref, wd_ref, gate_ref, *refs):
    outs, acc_ref = refs[:-1], refs[-1]
    step = pl.program_id(0)
    more = dot(act_ref[...], wd_ref[0])

    @pl.when(step == 0)
    def _():
        acc_ref[...] = more

    @pl.when(step > 0)
    def _():
        acc_ref[...] += more

    @pl.when(step == pl.num_programs(0) - 1)
    def _():
        rows = outs[0].shape[0]
        for n, out in enumerate(outs):
            part = slice(n * rows, (n + 1) * rows)
            out[...] = (acc_ref[part, :] * gate_ref[part, :1]).astype(bf16)


def expert_out(act, wd, gate, chunks, others=()):
    rows, hidden = act.shape
    width, wide = wd.shape[2], hidden // 2
    fixed = lambda r, c: pl.BlockSpec((r, c), lambda f: (0, 0))
    return pl.pallas_call(
        behind(out_kernel, 3, others),
        grid=(hidden // wide,),
        in_specs=[
            pl.BlockSpec((rows, wide), lambda f: (0, f)),
            pl.BlockSpec((1, wide, width), lambda f: (0, f, 0)), fixed(rows, TILE),
        ] + anywhere(others),
        out_specs=[fixed(rows // chunks, width)] * chunks,
        out_shape=[jax.ShapeDtypeStruct((rows // chunks, width), bf16)] * chunks,
        scratch_shapes=[pltpu.VMEM((rows, width), f32)],
        compiler_params=pltpu.CompilerParams(vmem_limit_bytes=VMEM),
        cost_estimate=cost(14),
        name="expert_out",
    )(act, wd, gate, *others)


def norm_kernel(two_ref, one_ref, own_ref, gain_ref, out_ref):
    step = pl.program_id(0)

    def put(ref):
        x = ref[...].astype(f32)
        r = lax.rsqrt(jnp.mean(x * x, axis=-1, keepdims=True) + epsilon)
        out_ref[...] = (x * r * gain_ref[...][None]).astype(bf16)

    for n, ref in enumerate((two_ref, one_ref, own_ref)):
        pl.when(step // 2 == n)(functools.partial(put, ref))


def norm_window(two, one, own, gain):
    pieces, rows, width = own.shape
    some = pieces // 2
    at = lambda n: pl.BlockSpec((some, rows, width), lambda f: (jnp.clip(f - 2 * n, 0, 1), 0, 0))
    return pl.pallas_call(
        norm_kernel,
        grid=(6,),
        in_specs=[at(0), at(1), at(2), pl.BlockSpec((1, width), lambda f: (0, 0))],
        out_specs=pl.BlockSpec((some, rows, width), lambda f: (f, 0, 0)),
        out_shape=jax.ShapeDtypeStruct((3 * pieces, rows, width), bf16),
        compiler_params=pltpu.CompilerParams(vmem_limit_bytes=VMEM),
        cost_estimate=cost(5),
        name="norm_window",
    )(two, one, own, gain)


def turn_kernel(rows_ref, out_ref):
    out_ref[...] = rows_ref[0].T.reshape(out_ref.shape)


def turn_rows(normed, chips, others=()):
    pieces, rows, width = normed.shape
    part = width // chips // 2
    return pl.pallas_call(
        behind(turn_kernel, 1, others),
        grid=(pieces,),
        in_specs=[pl.BlockSpec((1, rows, width), lambda f: (f, 0, 0))] + anywhere(others),
        out_specs=pl.BlockSpec((chips, 2, part, rows), lambda f: (0, 0, 0, f)),
        out_shape=jax.ShapeDtypeStruct((chips, 2, part, pieces * rows), bf16),
        compiler_params=pltpu.CompilerParams(vmem_limit_bytes=VMEM),
        cost_estimate=cost(8),
        name="turn_rows",
    )(normed, *others)


def slot_rows(t_ref, k, slot):
    index = lax.broadcasted_iota(jnp.int32, (slot, t_ref.shape[1]), 0) + k * slot
    return ((index == t_ref[0:1, :]) | (index == t_ref[1:2, :])).astype(bf16)


def row_slots(t_ref, k, slot):
    index = lax.broadcasted_iota(jnp.int32, (t_ref.shape[0], slot), 1) + k * slot
    return ((index == t_ref[:, 0:1]) | (index == t_ref[:, 1:2])).astype(bf16)


def collect(t_ref, refs):
    total = None
    for k, ref in enumerate(refs):
        part = dot(row_slots(t_ref, k, ref.shape[0]), ref[...])
        total = part if total is None else total + part
    return total


def turned(ref, z):
    return jnp.concatenate([ref[z ^ k] for k in range(ref.shape[0])], axis=0)


def call(kernel, ins, outs, us, name, others=(), scratch=(), passed=()):
    specs = [SMEM if a.ndim == 1 else pl.BlockSpec(memory_space=pltpu.VMEM) for a in ins]
    first, last = len(ins), len(ins) + len(passed) + len(others)

    def body(*refs):
        kernel(*refs[:first], *refs[last : last + len(outs)], *refs[last + len(outs) + len(passed) :])

    return pl.pallas_call(
        body,
        in_specs=specs + anywhere(passed) + anywhere(others),
        out_specs=[pl.BlockSpec(memory_space=pltpu.VMEM)] * len(outs) + anywhere(passed),
        out_shape=[jax.ShapeDtypeStruct(shape, dtype) for shape, dtype in outs]
        + [jax.ShapeDtypeStruct(array.shape, array.dtype) for array in passed],
        input_output_aliases={first + i: len(outs) + i for i in range(len(passed))},
        scratch_shapes=list(scratch),
        compiler_params=pltpu.CompilerParams(vmem_limit_bytes=VMEM),
        cost_estimate=cost(us),
        name=name,
    )(*ins, *passed, *others)


def pair_kernel(mine_ref, other_ref, out_ref):
    out_ref[...] = (mine_ref[...].astype(f32) + other_ref[...].astype(f32)).astype(bf16)


def pair_sum(mine, other, others=()):
    block = pl.BlockSpec((1,) + mine.shape[1:], lambda f: (f,) + (0,) * (mine.ndim - 1))
    return pl.pallas_call(
        behind(pair_kernel, 2, others),
        grid=mine.shape[:1],
        in_specs=[block, block] + anywhere(others),
        out_specs=block,
        out_shape=jax.ShapeDtypeStruct(mine.shape, bf16),
        compiler_params=pltpu.CompilerParams(vmem_limit_bytes=VMEM),
        cost_estimate=cost(6),
        name="pair_sum",
    )(mine, other, *others)


def cot_kernel(ks, slot, z_ref, t_ref, cot_ref, *outs):
    values = turned(cot_ref, z_ref[0])
    for k, out in zip(ks, outs):
        out[...] = dot(slot_rows(t_ref, k, slot), values).astype(bf16)


def rows_kernel(ks, slot, t_ref, value_ref, *outs):
    for k, out in zip(ks, outs):
        out[...] = dot(slot_rows(t_ref, k, slot), value_ref[...]).astype(bf16)


def hidden_kernel(ks, slot, z_ref, t_ref, tok_ref, w_ref, gain_ref, *refs):
    pieces = tok_ref.shape[0]
    context, hidden_ref, moe_ref, outs = refs[:pieces], refs[pieces], refs[pieces + 1], refs[pieces + 2 :]
    left = jnp.concatenate([ref[...] for ref in context], axis=0)
    hidden = turned(tok_ref, z_ref[0]).astype(f32) + dot(left, w_ref[...])
    hidden_ref[...] = hidden
    moe_in = norm_rows(hidden, gain_ref[...]).astype(bf16)
    moe_ref[...] = moe_in
    for k, out in zip(ks, outs):
        out[...] = dot(slot_rows(t_ref, k, slot), moe_in).astype(bf16)


def middle_kernel(z_ref, t_ref, hidden_ref, cot_ref, w_ref, gain_ref, *refs):
    pieces = cot_ref.shape[0]
    grad_ref, attn_ref, gain_grad_ref, outs = refs[pieces], refs[pieces + 1], refs[pieces + 2], refs[pieces + 3 :]
    grad_moe = collect(t_ref, refs[:pieces])
    grad_norm, gain_grad = norm_back(hidden_ref[...], gain_ref[...], grad_moe)
    gain_grad_ref[...] = gain_grad[None]
    grad = turned(cot_ref, z_ref[0]).astype(f32) + grad_norm
    grad_ref[...] = grad
    low = grad.astype(bf16)
    attn_ref[...] = low
    context = dot_nt(low, w_ref[...]).astype(bf16)
    rows = context.shape[0] // pieces
    for k in range(pieces):
        outs[k][...] = context[k * rows : (k + 1) * rows]


def mix_kernel(z_ref, t_ref, hidden_ref, *refs):
    out_ref = refs[-1]
    rows = out_ref.shape[1]
    mixed = (hidden_ref[...] + collect(t_ref, refs[:-1])).astype(bf16)
    for k in range(out_ref.shape[0]):
        out_ref[z_ref[0] ^ k] = mixed[k * rows : (k + 1) * rows]


def inputs_kernel(last, dq_ref, dk_ref, dv_ref, wq_ref, wk_ref, wv_ref, *refs):
    step = pl.program_id(0)
    flat = lambda ref: ref[...].reshape(-1, ref.shape[-1])
    grad = dot_nt(flat(dk_ref), wk_ref[...]) + dot_nt(flat(dv_ref), wv_ref[...])
    if not last:
        refs[0][...] = grad

        @pl.when(step == 2)
        def _():
            refs[0][...] = grad + dot_nt(flat(dq_ref), wq_ref[...])

        return
    acc_ref, two_ref, one_ref, own_ref = refs
    grad = grad + acc_ref[...]

    @pl.when(step == 0)
    def _():
        two_ref[...] = grad.astype(bf16)

    @pl.when(step == 1)
    def _():
        one_ref[...] = grad.astype(bf16)

    @pl.when(step == 2)
    def _():
        own_ref[...] = grad + dot_nt(flat(dq_ref), wq_ref[...])


def input_grads(part, dq, dk, dv, wq, wk, wv, acc=None, others=()):
    pieces, rows, some = dq.shape
    width = wq.shape[0]
    block = pieces * rows
    window = pl.BlockSpec((pieces, rows, some), lambda f: (f, 0, 0))
    weight = pl.BlockSpec((width, some), lambda f: (0, part))
    once = pl.BlockSpec((block, width), lambda f: (0, 0))
    step = pl.BlockSpec((block, width), lambda f: (f, 0))
    specs = [pl.BlockSpec((pieces, rows, some), lambda f: (0, 0, 0)), window, window, weight, weight, weight]
    ins, outs = [dq, dk, dv, wq, wk, wv], [(step, (3 * block, width), f32)]
    if acc is not None:
        specs += [step]
        ins += [acc]
        outs = [(once, (block, width), bf16)] * 2 + [(once, (block, width), f32)]
    return pl.pallas_call(
        behind(functools.partial(inputs_kernel, acc is not None), len(ins), others),
        grid=(3,),
        in_specs=specs + anywhere(others),
        out_specs=[o[0] for o in outs],
        out_shape=[jax.ShapeDtypeStruct(o[1], o[2]) for o in outs],
        compiler_params=pltpu.CompilerParams(vmem_limit_bytes=VMEM),
        cost_estimate=cost(7),
        name="input_grads",
    )(*ins, *others)


def leave_kernel(s_ref, z_ref, two_ref, swapped_ref, parts_ref, leave_ref, keep_ref, *refs):
    outs, total_ref = refs[:-1], refs[-1]
    zero = jnp.zeros_like(swapped_ref)
    swapped = swapped_ref[...]
    add = jnp.where(s_ref[0] == 0, zero, swapped)
    leave_ref[...] = (two_ref[...].astype(f32) + add.astype(f32)).astype(bf16)
    keep_ref[...] = jnp.where(s_ref[0] == 0, swapped, zero)
    total = parts_ref[0].astype(f32)
    for i in range(1, parts_ref.shape[0]):
        total = total + parts_ref[i].astype(f32)
    total_ref[...] = total.astype(bf16).reshape(total_ref.shape)
    for k, out in enumerate(outs):
        out[...] = total_ref[z_ref[0] ^ k]


def tail_kernel(z_ref, x_ref, sum_ref, swapped_ref, gain_ref, came_ref, *refs):
    pieces, rows, width = x_ref.shape
    blocks, outs, total_ref = refs[0], refs[1:-1], refs[-1]
    total = blocks[0].astype(f32)
    for i in range(1, blocks.shape[0]):
        total = total + blocks[i].astype(f32)
    total_ref[...] = total.astype(bf16).reshape(total_ref.shape)
    share, long = total_ref.shape[1:]
    for k in range(pieces):
        part = slice(k * rows, (k + 1) * rows)
        grad = sum_ref[part, :] + swapped_ref[part, :].astype(f32) + came_ref[part, :].astype(f32)
        outs[k][:rows, :] = norm_back(x_ref[k].astype(f32), gain_ref[...], grad)[0].astype(bf16)
        theirs = total_ref[z_ref[0] ^ k]
        outs[k][rows : rows + share, :] = theirs[:, :width]
        outs[k][rows + share :, : long - width] = theirs[:, width:]
        outs[k][rows + share :, long - width :] = jnp.zeros((share, 2 * width - long), bf16)


def end_kernel(z_ref, grad_ref, wq_ref, wk_ref, wv_ref, gain_ref, *refs):
    outs = refs[-7:]
    pieces, rows, width = outs[0].shape
    share, long = refs[pieces].shape
    half = (long - width) // 3
    first = refs[pieces][...].astype(f32)
    for k in range(1, pieces):
        first = first + refs[pieces + k][...].astype(f32)
    outs[6][...] = first[:, 3 * half :]
    total = None
    for k in range(pieces):
        outs[0][z_ref[0] ^ k] = (grad_ref[k * rows : (k + 1) * rows, :] + refs[k][:rows, :].astype(f32)).astype(bf16)
        part = jnp.concatenate([refs[k][rows : rows + share, :], refs[k][rows + share :, :]], axis=1).astype(f32)
        total = part if total is None else total + part
    gain = jnp.zeros((share, 1), f32)
    for i, weight in enumerate((wq_ref, wk_ref, wv_ref)):
        parts = (first[:, i * half : (i + 1) * half], total[:, i * half : (i + 1) * half])
        for n, part in enumerate(parts):
            columns = slice(n * half, (n + 1) * half)
            outs[1 + i][:, columns] = part
            gain = gain + jnp.sum(part * weight[:, columns].astype(f32), axis=1, keepdims=True)
    outs[4][...] = total[:, 3 * half : 3 * half + outs[4].shape[1]]
    outs[5][...] = gain / gain_ref[...]


def projection_kernel(third, small, pieces, s_ref, nt_ref, dq_ref, dk_ref, dv_ref, *refs):
    other_ref, mine_ref = refs[small + pieces + (pieces > 0) :][:2]
    step = pl.program_id(0)
    keys = nt_ref.shape[3]
    own = dq_ref.shape[0]

    def put(grad_ref, first):
        for where, ref in ((1 - s_ref[0], other_ref), (s_ref[0], mine_ref)):
            left = nt_ref[:, where, :, first:].reshape(-1, keys - first)
            ref[...] = dot(left, grad_ref[...]).astype(bf16).reshape(ref.shape)

    @pl.when(step < third)
    def _():
        put(dq_ref, keys - own)

    @pl.when((step >= third) & (step < 2 * third))
    def _():
        put(dk_ref, 0)

    @pl.when((step >= 2 * third) & (step < 3 * third))
    def _():
        put(dv_ref, 0)

    if pieces:
        turned_ref, context, attn_ref = refs[-1], refs[:pieces], refs[pieces]
        count = context[0].shape[0]

        @pl.when(step == 3 * third)
        def _():
            for k in range(pieces):
                turned_ref[:, :, :, k * count : (k + 1) * count] = context[k][...].T.reshape(turned_ref.shape[:3] + (count,))

        @pl.when(step >= 3 * third)
        def _():
            for where, ref in ((1 - s_ref[0], other_ref), (s_ref[0], mine_ref)):
                left = turned_ref[:, where].reshape(-1, pieces * count)
                ref[...] = dot(left, attn_ref[...]).astype(bf16).reshape(ref.shape)

    if small:

        @pl.when(step == 3 * third)
        def _():
            other_ref[...] = refs[0][:, 1 - s_ref[0]]
            mine_ref[...] = refs[0][:, s_ref[0]]


def projection_grads(side, normed_t, dq, dk, dv, small=(), context=(), attn=(), others=()):
    chips, _, rows, keys = normed_t.shape
    own, width = dq.shape
    wide = 2 * TILE
    third = width // wide
    at = lambda j: (lambda f: (0, jnp.clip(f - j * third, 0, third - 1)))
    fixed = lambda array: pl.BlockSpec(array.shape, lambda f: (0,) * array.ndim)
    more = len(small) + sum(array.shape[1] // wide for array in attn)
    out = pl.BlockSpec((chips, rows, wide), lambda f: (0, 0, f))
    shape = jax.ShapeDtypeStruct((chips, rows, 3 * width + wide * more), bf16)
    ins = [side, normed_t, dq, dk, dv, *small, *context, *attn]
    scratch = [pltpu.VMEM((chips, 2, rows, len(context) * array.shape[0]), bf16) for array in context[:1]]
    return pl.pallas_call(
        behind(functools.partial(projection_kernel, third, len(small), len(context)), len(ins), others),
        grid=(3 * third + more,),
        in_specs=[
            SMEM,
            fixed(normed_t),
            pl.BlockSpec((own, wide), at(0)),
            pl.BlockSpec((keys, wide), at(1)),
            pl.BlockSpec((keys, wide), at(2)),
        ]
        + [fixed(array) for array in [*small, *context]]
        + [pl.BlockSpec((array.shape[0], wide), lambda f: (0, jnp.maximum(f - 3 * third, 0))) for array in attn]
        + anywhere(others),
        out_specs=[out, out],
        out_shape=[shape, shape],
        scratch_shapes=scratch,
        compiler_params=pltpu.CompilerParams(vmem_limit_bytes=VMEM),
        cost_estimate=cost(9.3 + more),
        name="projection_grads",
    )(*ins, *others)


def shift(x, by):
    count = lax.axis_size("ctx")
    return lax.ppermute(x, "ctx", [(i, i + by) for i in range(count) if 0 <= i + by < count])


def core_swap(x):
    return lax.ppermute(x, "ctx", [(i, i ^ 1) for i in range(lax.axis_size("ctx"))])


def z_swap(x, k):
    if k == 0:
        return x
    return lax.ppermute(x, "exp", [(i, i ^ k) for i in range(lax.axis_size("exp"))])


def over_chips(pair):
    count = lax.axis_size("ctx")
    groups = [list(range(core, count, 2)) for core in range(2)]
    return lax.all_to_all(pair, "ctx", split_axis=0, concat_axis=0, tiled=True, axis_index_groups=groups)


def summed(parts):
    return jnp.sum(parts.astype(f32), axis=0)


def add_pair(mine, other):
    return (mine.astype(f32) + core_swap(other).astype(f32)).astype(bf16)


def norm_rows(values, gain):
    return values * lax.rsqrt(jnp.mean(values * values, axis=-1, keepdims=True) + epsilon) * gain


def norm_back(values, gain, grad):
    r = lax.rsqrt(jnp.mean(values * values, axis=-1, keepdims=True) + epsilon)
    u = grad * gain
    inner = jnp.mean(values * u, axis=-1, keepdims=True)
    return r * u - values * (r * r * r) * inner, jnp.sum(grad * values * r, axis=0)


def on_device(
    tokens, doc_lengths, routes, priority, norm1_gain, w_query, w_key, w_value, w_out, bias_table,
    norm2_gain, w_router, w_gate, w_up, w_down, cotangent,
):
    seqs, piece_len, width = tokens.shape
    exp_count = lax.axis_size("exp")
    ctx_count = lax.axis_size("ctx")
    device_count = exp_count * ctx_count
    block_len = piece_len * exp_count
    rows = seqs * piece_len
    heads = bias_table.shape[0] // bucket_total
    experts = w_router.shape[1]
    slot = 5 * rows // (2 * experts)
    slots = experts * slot
    ctx = lax.axis_index("ctx")
    exp = lax.axis_index("exp")
    side = ctx % 2

    z = jnp.reshape(exp, (1,))
    far_first = [2, 3, 1]

    turn = jnp.arange(seqs, dtype=jnp.int32) ^ exp
    pick = lambda array, k: lax.dynamic_index_in_dim(array, exp ^ k, 0, keepdims=False)

    x_own = [None] * seqs
    for k in [0, 2, 3, 1]:
        x_own[k] = z_swap(pick(tokens, k), k)
    x_pieces = x_own
    x_two = [shift(piece, 2) for piece in x_own]
    x_own, x_two = jnp.stack(x_own), jnp.stack(x_two)
    x_one = core_swap(jnp.where(side == 0, x_own, x_two))

    route_rows = jnp.take(routes, turn, axis=0).reshape(rows, 2)
    order = jnp.take(priority, turn, axis=0).reshape(rows)
    earlier = order[None, :] < order[:, None]
    r0, r1 = route_rows[:, 0], route_rows[:, 1]
    place0 = jnp.sum((earlier & (r0[None, :] == r0[:, None])).astype(jnp.int32), axis=1)
    place1 = jnp.sum((earlier & (r1[None, :] == r1[:, None])).astype(jnp.int32), axis=1) + jnp.sum(
        (r0[None, :] == r1[:, None]).astype(jnp.int32), axis=1
    )
    target0 = jnp.where(place0 < slot, (r0 ^ exp) * slot + place0, -1)
    target1 = jnp.where(place1 < slot, (r1 ^ exp) * slot + place1, -1)
    targets = jnp.stack([target0, target1])
    targets_t = targets.T
    slot_shape = ((slot, width), bf16)
    sent = call(
        functools.partial(cot_kernel, far_first + [0], slot), [z, targets, cotangent], [slot_shape] * experts, 4, "cot_rows", x_pieces[1:]
    )
    cot_slots = [None] * experts
    for k, rows_k in zip(far_first + [0], sent):
        cot_slots[k] = z_swap(rows_k, k)

    distance = np.arange(-TILE, WINDOW + TILE)
    seen = (distance >= 0) & (distance < WINDOW)
    hot = (bucket_of(np.clip(distance, 0, None))[None, :] == np.arange(bucket_total)[:, None]) & seen[None, :]
    vec = exact_dot(bias_table.astype(f32).reshape(heads, bucket_total), jnp.asarray(hot, f32))
    vec = jnp.where(jnp.asarray(seen)[None, :], vec, NEG).reshape(heads // 2, 2, -1)
    bias = bias_tiles(vec, sent[:1])

    ends = jnp.cumsum(lax.dynamic_index_in_dim(doc_lengths, exp, 0, keepdims=False))
    piece_start = ctx * block_len + turn[:, None] * piece_len
    q_pos = piece_start + jnp.arange(piece_len, dtype=jnp.int32)[None, :]
    start = jnp.max(jnp.where(ends <= q_pos[..., None], ends, 0), axis=2)
    lo = start - (ctx - 2) * block_len
    lo = jnp.broadcast_to(lo[:, None, None, :], (seqs, 1, 2, TILE)).reshape(seqs, 1, 2 * TILE)

    gain_one = norm1_gain.astype(f32)
    normed_pieces = norm_window(x_two, x_one, x_own, gain_one[None])
    normed = normed_pieces.reshape(-1, width)
    normed_own = normed[2 * block_len :]
    q = (dot(normed_own, w_query).astype(bf16) * 0.125).astype(bf16).reshape(seqs, piece_len, width)
    k_win = dot(normed, w_key).astype(bf16).reshape(-1, TILE, width)
    v_win = dot(normed, w_value).astype(bf16).reshape(-1, TILE, width)
    contexts, lses, context_rows = [None] * seqs, [], [None] * seqs
    for first in (2, 0):
        others = [contexts[2], cot_slots[2]] if first == 0 else []
        *c, l = attend((first, first + 1), z, lo[first : first + 2], q[first : first + 2], k_win, v_win, bias, others)
        lses.insert(0, l)
        for k in (first, first + 1):
            contexts[k] = c[k - first]
            context_rows[k] = z_swap(contexts[k], k)
    normed_t = turn_rows(normed_pieces, ctx_count // 2, contexts[:1])
    router_wide = jnp.pad(w_router, ((0, 0), (0, TILE - experts)))
    gain_two = norm2_gain.astype(f32)[None]
    hidden, moe_in, *sent = call(
        functools.partial(hidden_kernel, [2, 0], slot),
        [z, targets, tokens, w_out, gain_two] + context_rows,
        [((rows, width), f32), ((rows, width), bf16), slot_shape, slot_shape], 9, "hidden_rows", [cot_slots[1], cot_slots[3], normed_t],
    )
    inputs = [sent[1], None, z_swap(sent[0], 2), None]
    held, returned, turns = None, [None] * experts, [0, 2, 1, 3]
    for ks, index in (([0], 0), ([2], 1), ([1], 2), ([3], 3)):
        found = expert(
            index, experts, held, z, [inputs[k] for k in ks], [cot_slots[k] for k in ks], w_gate, w_up, w_down, router_wide, experts
        )
        back, held = found[: len(ks)], found[len(ks) :]
        for k, rows_k in zip(ks, back):
            returned[k] = z_swap(rows_k, k)
        if index == 0:
            sent = call(functools.partial(rows_kernel, [3, 1], slot), [targets, moe_in], [slot_shape] * 2, 3, "moe_rows", back)
            inputs[3], inputs[1] = z_swap(sent[0], 3), z_swap(sent[1], 1)
    all_inputs, act_low, grad_gate_pre, grad_up_pre, grad_out_slots, gate, grad_logits = held
    chips = ctx_count // 2
    side_ref = jnp.reshape(side, (1,))
    produced = expert_out(act_low, w_down, gate, experts, [returned[2]])
    down_other, down_mine = down_grads(side_ref, chips, act_low, grad_out_slots, produced[:1])

    part_count = 2
    part_width = width // part_count
    grad_hidden, grad_attn, grad_gain_two, *sent_back = call(
        middle_kernel, [z, targets_t, hidden, cotangent, w_out, gain_two] + returned,
        [((rows, width), f32), ((rows, width), bf16), ((1, width), f32)] + [((piece_len, width), bf16)] * seqs,
        9, "middle_rows", [down_other],
    )
    arrived = [z_swap(sent_back[k], k) for k in range(seqs)]
    other, mine, router_part = gate_up_grads(
        side_ref, chips, all_inputs, grad_gate_pre, grad_up_pre, grad_logits, sent_back[-1:]
    )
    grad_router_part = router_part[:, :experts]
    pair = pair_sum(mine, core_swap(other))
    both = over_chips(pair)
    down_other = core_swap(down_other)
    given = [z_swap(produced[turns.index(k)], k) for k in range(experts)]

    weights = (w_query, w_key, w_value)
    flat = lambda grads: [grad.reshape(-1, part_width) for grad in grads]
    back = lambda n, others: attend_back(n, part_count, z, lo, lses, q, k_win, v_win, bias, contexts, arrived, others)
    *grads, diagonal = back(0, [pair])
    other, mine = projection_grads(
        side_ref, normed_t, *flat(grads), context=context_rows, attn=[grad_attn], others=[given[2], given[1]]
    )
    first_pair = add_pair(mine, other)
    first_parts = over_chips(first_pair)
    acc = input_grads(0, *grads, *weights, others=[other])[0]
    down_pair = pair_sum(down_mine, down_other)
    *grads, more = back(1, [acc, first_pair, both, down_pair])
    diagonals = jnp.concatenate([diagonal, more])
    places = np.arange((TILES_SEEN) * 2 * TILE).reshape(TILES_SEEN, 2 * TILE)
    block, lane = places // (2 * TILE), places % (2 * TILE)
    where_dist = lane - TILE + (TILES_SEEN - 1 - block) * TILE
    ok = (where_dist >= 0) & (where_dist < WINDOW)
    to_bucket = (bucket_of(np.clip(where_dist, 0, None))[..., None] == np.arange(bucket_total)) & ok[..., None]
    table_part = exact_dot(diagonals.reshape(heads, -1), jnp.asarray(to_bucket.reshape(-1, bucket_total), f32))
    small = [
        grad_gain_two.reshape(device_count, -1),
        table_part.reshape(device_count, -1),
        grad_router_part.reshape(device_count, -1),
    ]
    cuts = np.cumsum([0] + [item.shape[1] for item in small])
    packed = jnp.concatenate(small, axis=1)
    share = width // device_count
    packed = jnp.pad(packed, ((0, 0), (0, -packed.shape[1] % share))).reshape(width, -1)
    packed = jnp.pad(packed.astype(bf16), ((0, 0), (0, 2 * TILE - packed.shape[1])))
    packed = packed.reshape(ctx_count // 2, 2, -1, 2 * TILE)
    other, mine = projection_grads(side_ref, normed_t, *flat(grads), small=[packed], others=[first_parts, given[3]])
    pair = add_pair(mine, other)
    last = over_chips(pair)
    part_two, part_one, own_sum = input_grads(1, *grads, *weights, acc, [pair])
    leave, swapped, *first, down_pair = call(
        leave_kernel, [side_ref, z, part_two, core_swap(part_one), first_parts],
        [((block_len, width), bf16)] * 2 + [((share, first_parts.shape[-1]), bf16)] * seqs, 5, "leaving_rows", [last],
        [pltpu.VMEM((exp_count, share, first_parts.shape[-1]), bf16)], [down_pair],
    )
    first = [z_swap(piece, k) for k, piece in enumerate(first)]
    came = shift(leave, -2)
    down = over_chips(down_pair)
    mixed = call(
        mix_kernel, [z, targets_t, hidden] + given, [((seqs, piece_len, width), bf16)], 8, "mixed_rows", [leave]
    )[0]
    share = width // device_count
    long = pair.shape[-1]
    pieces = call(
        tail_kernel, [z, x_own, own_sum, swapped, gain_one[None], came, last],
        [((piece_len + 2 * share, width), bf16)] * seqs, 8, "tail_rows", [mixed] + first[1:],
        [pltpu.VMEM((exp_count, share, long), bf16)],
    )
    pieces = [z_swap(piece, k) for k, piece in enumerate(pieces)]
    grad_gate, grad_up, grad_down = summed(both[:, 0]), summed(both[:, 1]), summed(down)
    own_rows = lambda array: lax.dynamic_slice_in_dim(array, (ctx * exp_count + exp) * share, share, 0)
    grad_tokens, grad_query, grad_key, grad_value, packed, norm1_out, grad_out = call(
        end_kernel,
        [z, grad_hidden] + [own_rows(array) for array in weights] + [own_rows(gain_one[:, None])] + pieces + first,
        [((seqs, piece_len, width), bf16)] + [((share, width), f32)] * 3 + [((share, 2 * TILE), f32), ((share, 1), f32)]
        + [((share, width), f32)],
        6, "end_rows", [grad_down],
    )
    packed = packed[:, : -(-cuts[-1] // share)].reshape(-1)
    norm1_out = norm1_out[:, 0]
    norm2_out, table_out, router_out = [packed[cuts[i] : cuts[i + 1]] for i in range(3)]
    return (
        mixed, grad_tokens, norm1_out, grad_query, grad_key, grad_value, grad_out, table_out, norm2_out,
        router_out.reshape(-1, experts), grad_gate[None], grad_up[None], grad_down[None],
    )


def solution(mesh):
    rows = P(None, ("ctx", "exp"), None)
    flat = P(("ctx", "exp"))
    in_specs = (
        rows, P(), rows, P(None, ("ctx", "exp")), P(), P(), P(), P(), P(), P(), P(), P(),
        P("exp", None, None), P("exp", None, None), P("exp", None, None), rows,
    )
    out_specs = (
        rows, rows, flat, P(("ctx", "exp"), None), P(("ctx", "exp"), None), P(("ctx", "exp"), None),
        P(("ctx", "exp"), None), flat, flat, P(("ctx", "exp"), None),
        P("exp", "ctx", None), P("exp", "ctx", None), P("exp", "ctx", None),
    )
    return jax.shard_map(on_device, mesh=mesh, in_specs=in_specs, out_specs=out_specs, check_vma=False)
```

```python
import functools

import jax
import jax.numpy as jnp
import numpy as np
from jax import lax
from jax.experimental import pallas as pl
from jax.experimental.pallas import tpu as pltpu
from jax.sharding import PartitionSpec as P

WINDOW = 1024
TILE = 128
TILES_SEEN = WINDOW // TILE + 1
epsilon = 1e-06
bucket_total = 32
NEG = -1e30
f32 = jnp.float32
bf16 = jnp.bfloat16
VMEM = 56 * 1024 * 1024


def cost(us):
    return pl.CostEstimate(flops=int(us * 1.15e9), bytes_accessed=0, transcendentals=0)


def behind(kernel, inputs, others):
    return lambda *refs: kernel(*refs[:inputs], *refs[inputs + len(others) :])


def anywhere(others):
    return [pl.BlockSpec(memory_space=pl.ANY)] * len(others)


def dot(left, right):
    return jnp.dot(left, right, preferred_element_type=f32)


def dot_nt(left, right):
    return lax.dot_general(left, right, (((1,), (1,)), ((), ())), preferred_element_type=f32)


def dot_tn(left, right):
    return lax.dot_general(left, right, (((0,), (0,)), ((), ())), preferred_element_type=f32)


def exact_dot(left, right):
    return jnp.dot(left, right, precision=lax.Precision.HIGHEST, preferred_element_type=f32)


def bucket_of(distance):
    limits = np.ceil(16.0 * 8.0 ** (np.arange(1, 16) / 16.0)).astype(np.int32)
    above = np.sum(distance[..., None] >= limits, axis=-1)
    return np.where(distance < 16, distance, 16 + above)


def bias_kernel(vec_ref, out_ref):
    for a in range(TILES_SEEN):
        first = (TILES_SEEN - 1 - a) * TILE
        for h in range(2):
            row = vec_ref[0, h : h + 1, first : first + 2 * TILE]
            wide = jnp.broadcast_to(row, (TILE, 2 * TILE))
            rolled = pltpu.roll(wide, TILE, 1, stride=1, stride_axis=0)
            out_ref[0, a, :, h * TILE : (h + 1) * TILE] = rolled[:, :TILE].astype(bf16)


def split_heads(x):
    lane = lax.broadcasted_iota(jnp.int32, x.shape, 1)
    zero = jnp.zeros_like(x)
    return jnp.concatenate([jnp.where(lane < 64, x, zero), jnp.where(lane < 64, zero, x)], axis=0)


def merge_heads(xt):
    return jnp.concatenate([xt[:64, :TILE], xt[64:, TILE:]], axis=0).T


def key_block(kb, z):
    return (kb // 4) * 4 + ((kb % 4) ^ z)


def attend_kernel(ks, z_ref, lo_ref, q_ref, k_ref, v_ref, b_ref, *refs):
    outs, (lse_ref, s_ref, p_ref, v_s) = refs[: len(ks)], refs[len(ks) :]
    z = z_ref[0]
    row = lax.broadcasted_iota(jnp.int32, (TILE, 2 * TILE), 0)
    for i, (p, n) in enumerate((p, n) for p in range(2) for n in range(len(ks))):
        pair = slice(p * TILE, (p + 1) * TILE)
        t = z ^ ks[n]
        q2 = split_heads(q_ref[n, :, pair])
        lo = lo_ref[n] - t * TILE
        top = jnp.full((8, 2 * TILE), NEG, f32)
        for a in range(TILES_SEEN):
            at = key_block(t + a, z)
            v_s[i, a * TILE : (a + 1) * TILE, :] = v_ref[at, :, pair]
            s = dot_nt(k_ref[at, :, pair], q2) + b_ref[p, a].astype(f32)
            s = jnp.where(row >= lo - a * TILE, s, NEG)
            s_ref[i, a] = s
            top = jnp.maximum(top, jnp.max(s.reshape(TILE // 8, 8, 2 * TILE), axis=0))
        top = jnp.max(top, axis=0, keepdims=True)
        total = jnp.zeros((8, 2 * TILE), f32)
        for a in range(TILES_SEEN):
            e = jnp.exp(s_ref[i, a] - top)
            total = total + jnp.sum(e.reshape(TILE // 8, 8, 2 * TILE), axis=0)
            p_ref[i, a * TILE : (a + 1) * TILE, :] = e.astype(bf16)
        total = jnp.sum(total, axis=0, keepdims=True)
        ct = dot(v_s[i].T, p_ref[i]) / total
        outs[n][:, pair] = merge_heads(ct).astype(bf16)
        lse_ref[p, n] = top + jnp.log(total)


def attend_back_kernel(pieces, z_ref, lo_ref, lse_a, lse_b, q_ref, k_ref, v_ref, b_ref, *refs):
    o_refs, do_refs = refs[:pieces], refs[pieces : 2 * pieces]
    dq_ref, dk_ref, dv_ref, tab_ref, q2_ref, do2_ref, ds_ref, p_ref, acc_ref, row_ref, k_s = refs[2 * pieces :]
    z = z_ref[0]
    row = lax.broadcasted_iota(jnp.int32, (TILE, 2 * TILE), 0)
    for k in range(pieces):
        both = pl.ds(pl.multiple_of((z ^ k) * 2 * TILE, 2 * TILE), 2 * TILE)
        out, grad = o_refs[k][...], do_refs[k][...]
        q2_ref[both, :] = split_heads(q_ref[k])
        do2_ref[both, :] = split_heads(grad)
        prod = (grad.astype(f32) * out.astype(f32)).T
        lse_ref = lse_a if k < pieces // 2 else lse_b
        row_ref[0:1, both] = lse_ref[0, k % (pieces // 2)]
        row_ref[1:2, both] = jnp.concatenate(
            [jnp.sum(prod[:64], axis=0, keepdims=True), jnp.sum(prod[64:], axis=0, keepdims=True)], axis=1
        )
    acc_ref[...] = jnp.zeros_like(acc_ref)
    keys = pieces + TILES_SEEN - 1
    for kb in range(keys):
        first, last = max(0, kb - TILES_SEEN + 1), min(pieces - 1, kb)
        krows = slice(kb * TILE, (kb + 1) * TILE)
        cols = slice(first * 2 * TILE, (last + 1) * 2 * TILE)
        at = key_block(kb, z)
        key, value = k_ref[at], v_ref[at]
        k_s[krows, :] = key
        for t in range(first, last + 1):
            both = slice(t * 2 * TILE, (t + 1) * 2 * TILE)
            a = kb - t
            s = dot_nt(key, q2_ref[both, :]) + b_ref[0, a].astype(f32)
            s = jnp.where(row >= lo_ref[z ^ t] - kb * TILE, s, NEG)
            p = jnp.exp(s - row_ref[0:1, both])
            dp = dot_nt(value, do2_ref[both, :])
            ds = p * (dp - row_ref[1:2, both])
            acc_ref[a] += ds
            p_ref[:, both] = p.astype(bf16)
            ds_ref[krows, both] = ds.astype(bf16)
        dk_ref[at] = dot(ds_ref[krows, cols], q2_ref[cols, :]).astype(bf16)
        dv_ref[at] = dot(p_ref[:, cols], do2_ref[cols, :]).astype(bf16)
    kt = k_s[...].T
    for t in range(pieces):
        both = slice(t * 2 * TILE, (t + 1) * 2 * TILE)
        span = slice(t * TILE, (t + TILES_SEEN) * TILE)
        dqt = dot(kt[:, span], ds_ref[span, both]) * 0.125
        dq_ref[z ^ t] = merge_heads(dqt).astype(bf16)
    for a in range(TILES_SEEN):
        for h in range(2):
            part = acc_ref[a, :, h * TILE : (h + 1) * TILE]
            part = jnp.concatenate([part, jnp.zeros_like(part)], axis=1)
            half = TILE // 2
            while half >= 1:
                part = part[:half] + pltpu.roll(part[half:], 2 * TILE - half, 1)
                half //= 2
            tab_ref[0, h, a : a + 1, :] = pltpu.roll(part, TILE, 1)


def bias_tiles(vec, others=()):
    pairs = vec.shape[0]
    return pl.pallas_call(
        behind(bias_kernel, 1, others),
        grid=(pairs,),
        in_specs=[pl.BlockSpec((1, 2, vec.shape[2]), lambda g: (g, 0, 0))] + anywhere(others),
        out_specs=pl.BlockSpec((1, TILES_SEEN, TILE, 2 * TILE), lambda g: (g, 0, 0, 0)),
        out_shape=jax.ShapeDtypeStruct((pairs, TILES_SEEN, TILE, 2 * TILE), bf16),
        compiler_params=pltpu.CompilerParams(vmem_limit_bytes=VMEM),
        cost_estimate=cost(6),
        name="bias_tiles",
    )(vec, *others)


SMEM = pl.BlockSpec(memory_space=pltpu.SMEM)


def attend(ks, z, lo, q, k, v, bias, others=()):
    count, _, width = q.shape
    blocks, pairs = k.shape[0], width // TILE
    part = lambda n: pl.BlockSpec((n, TILE, 2 * TILE), lambda g: (0, 0, g))
    return pl.pallas_call(
        behind(functools.partial(attend_kernel, ks), 6, others),
        grid=(pairs // 2,),
        in_specs=[
            SMEM,
            pl.BlockSpec((count, 1, 2 * TILE), lambda g: (0, 0, 0)),
            part(count), part(blocks), part(blocks),
            pl.BlockSpec((2, TILES_SEEN, TILE, 2 * TILE), lambda g: (g, 0, 0, 0)),
        ] + anywhere(others),
        out_specs=[pl.BlockSpec((TILE, 2 * TILE), lambda g: (0, g))] * count
        + [pl.BlockSpec((2, count, 1, 2 * TILE), lambda g: (g, 0, 0, 0))],
        out_shape=[jax.ShapeDtypeStruct((TILE, width), bf16)] * count
        + [
            jax.ShapeDtypeStruct((pairs, count, 1, 2 * TILE), f32),
        ],
        scratch_shapes=[
            pltpu.VMEM((2 * count, TILES_SEEN, TILE, 2 * TILE), f32),
            pltpu.VMEM((2 * count, TILES_SEEN * TILE, 2 * TILE), bf16),
            pltpu.VMEM((2 * count, TILES_SEEN * TILE, TILE), bf16),
        ],
        compiler_params=pltpu.CompilerParams(vmem_limit_bytes=VMEM),
        cost_estimate=cost(6 * count),
        name="attend",
    )(z, lo, q, k, v, bias, *others)


def attend_back(part_index, part_count, z, lo, lses, q, k, v, bias, o, do, others=()):
    pieces, _, width = q.shape
    blocks, pairs = k.shape[0], width // TILE // part_count
    base = part_index * pairs
    part = lambda n: pl.BlockSpec((n, TILE, TILE), lambda g: (0, 0, base + g))
    alone = lambda n: pl.BlockSpec((n, TILE, TILE), lambda g: (0, 0, g))
    columns = pieces * 2 * TILE
    return pl.pallas_call(
        behind(functools.partial(attend_back_kernel, pieces), 8 + 2 * pieces, others),
        grid=(pairs,),
        in_specs=[
            SMEM,
            pl.BlockSpec((pieces, 1, 2 * TILE), lambda g: (0, 0, 0)),
            pl.BlockSpec((1, pieces // 2, 1, 2 * TILE), lambda g: (base + g, 0, 0, 0)),
            pl.BlockSpec((1, pieces // 2, 1, 2 * TILE), lambda g: (base + g, 0, 0, 0)),
            part(pieces), part(blocks), part(blocks),
            pl.BlockSpec((1, TILES_SEEN, TILE, 2 * TILE), lambda g: (base + g, 0, 0, 0)),
        ]
        + [pl.BlockSpec((TILE, TILE), lambda g: (0, base + g))] * pieces
        + [pl.BlockSpec((TILE, TILE), lambda g: (0, base + g))] * pieces
        + anywhere(others),
        out_specs=[
            alone(pieces), alone(blocks), alone(blocks),
            pl.BlockSpec((1, 2, TILES_SEEN, 2 * TILE), lambda g: (g, 0, 0, 0)),
        ],
        out_shape=[
            jax.ShapeDtypeStruct((pieces, TILE, width // part_count), bf16),
            jax.ShapeDtypeStruct((blocks, TILE, width // part_count), bf16),
            jax.ShapeDtypeStruct((blocks, TILE, width // part_count), bf16),
            jax.ShapeDtypeStruct((pairs, 2, TILES_SEEN, 2 * TILE), f32),
        ],
        scratch_shapes=[
            pltpu.VMEM((columns, TILE), bf16),
            pltpu.VMEM((columns, TILE), bf16),
            pltpu.VMEM((blocks * TILE, columns), bf16),
            pltpu.VMEM((TILE, columns), bf16),
            pltpu.VMEM((TILES_SEEN, TILE, 2 * TILE), f32),
            pltpu.VMEM((8, columns), f32),
            pltpu.VMEM((blocks * TILE, TILE), bf16),
        ],
        compiler_params=pltpu.CompilerParams(vmem_limit_bytes=VMEM),
        cost_estimate=cost(42 / part_count),
        name="attend_back",
    )(z, lo, *lses, q, k, v, bias, *o, *do, *others)


def gelu_parts(v):
    c = np.float32(np.sqrt(2.0 / np.pi))
    t = jnp.tanh(c * (v + 0.044715 * v * v * v))
    half = 0.5 * (1.0 + t)
    return v * half, half + 0.5 * v * (1.0 - t * t) * (c * (1.0 + 3.0 * 0.044715 * v * v))


def expert_kernel(experts, count, held, z_ref, *refs):
    x_refs, c_refs, (wg_ref, wu_ref, wd_ref, wr_ref) = refs[:count], refs[count : 2 * count], refs[2 * count : 2 * count + 4]
    refs = refs[2 * count + 4 + held :]
    gin_refs, refs = refs[:count], refs[count:]
    kept_ref, act_ref, dgp_ref, dup_ref, gcot_ref, gate_out, glog_ref, acc_ref, gg_ref, rp_ref, gate_ref, xs_ref, cs_ref = refs
    step = pl.program_id(0)
    rows = xs_ref.shape[0]
    lane = lax.broadcasted_iota(jnp.int32, (rows, TILE), 1)

    @pl.when(step == 0)
    def _():
        for n in range(count):
            part = slice(n * rows // count, (n + 1) * rows // count)
            xs_ref[part, :] = x_refs[n][...]
            cs_ref[part, :] = c_refs[n][...]
        x = xs_ref[...]
        logits = jnp.where(lane < experts, dot(x, wr_ref[...]), NEG)
        e = jnp.exp(logits - jnp.max(logits, axis=1, keepdims=True))
        probs = e / jnp.sum(e, axis=1, keepdims=True)
        rp_ref[...] = probs
        gate = jnp.sum(jnp.where(lane == z_ref[0], probs, 0.0), axis=1, keepdims=True)
        gate_ref[...] = jnp.broadcast_to(gate, gate_ref.shape)
        gate_out[...] = gate_ref[...]
        kept_ref[...] = x
        gcot_ref[...] = (gate * cs_ref[...].astype(f32)).astype(bf16)
        acc_ref[...] = jnp.zeros_like(acc_ref)
        gg_ref[...] = jnp.zeros_like(gg_ref)

    x, c = xs_ref[...], cs_ref[...]
    raw = dot_nt(c, wd_ref[0])
    gate_pre = dot(x, wg_ref[0])
    up_pre = dot(x, wu_ref[0])
    gelu, slope = gelu_parts(gate_pre)
    act = gelu * up_pre
    act_ref[...] = act.astype(bf16)
    prod = act * raw
    gg_ref[...] += prod[:, :TILE] + prod[:, TILE:]
    scaled = raw * gate_ref[:, :1]
    dgp = (scaled * up_pre * slope).astype(bf16)
    dup = (scaled * gelu).astype(bf16)
    dgp_ref[...] = dgp
    dup_ref[...] = dup
    acc_ref[...] += dot_nt(dgp, wg_ref[0]) + dot_nt(dup, wu_ref[0])

    @pl.when(step == pl.num_programs(0) - 1)
    def _():
        gg = jnp.sum(gg_ref[...], axis=1, keepdims=True)
        own = jnp.where(lane == z_ref[0], 1.0, 0.0)
        glog = gg * rp_ref[...] * (own - gate_ref[...])
        glog_ref[...] = glog
        high = glog.astype(bf16)
        low = (glog - high.astype(f32)).astype(bf16)
        gin = (acc_ref[...] + dot_nt(high, wr_ref[...]) + dot_nt(low, wr_ref[...])).astype(bf16)
        for n in range(count):
            gin_refs[n][...] = gin[n * rows // count : (n + 1) * rows // count]


def expert(index, total, held, z, xs, cs, wg, wu, wd, wr, experts, others=()):
    count, (slot, width) = len(xs), xs[0].shape
    rows = count * slot
    hidden = wg.shape[2]
    wide = 2 * TILE
    whole = pl.BlockSpec((slot, width), lambda f: (0, 0))
    kept = pl.BlockSpec((rows, width), lambda f: (index, 0))
    thin = pl.BlockSpec((rows, TILE), lambda f: (index, 0))
    tile = pl.BlockSpec((rows, wide), lambda f: (index, f))
    full = lambda n, t: jax.ShapeDtypeStruct((total * slot, n), t)
    held = [] if held is None else list(held)
    return pl.pallas_call(
        functools.partial(expert_kernel, experts, count, len(held) + len(others)),
        grid=(hidden // wide,),
        in_specs=[SMEM] + [whole] * (2 * count) + [
            pl.BlockSpec((1, width, wide), lambda f: (0, 0, f)),
            pl.BlockSpec((1, width, wide), lambda f: (0, 0, f)),
            pl.BlockSpec((1, wide, width), lambda f: (0, f, 0)),
            pl.BlockSpec((width, TILE), lambda f: (0, 0)),
        ] + anywhere(held) + anywhere(others),
        out_specs=[whole] * count + [kept, tile, tile, tile, kept, thin, thin],
        out_shape=[jax.ShapeDtypeStruct((slot, width), bf16)] * count + [
            full(width, bf16), full(hidden, bf16), full(hidden, bf16), full(hidden, bf16), full(width, bf16),
            full(TILE, f32), full(TILE, f32),
        ],
        input_output_aliases={2 * count + 5 + i: count + i for i in range(len(held))},
        scratch_shapes=[
            pltpu.VMEM((rows, width), f32), pltpu.VMEM((rows, TILE), f32), pltpu.VMEM((rows, TILE), f32),
            pltpu.VMEM((rows, TILE), f32), pltpu.VMEM((rows, width), bf16), pltpu.VMEM((rows, width), bf16),
        ],
        compiler_params=pltpu.CompilerParams(vmem_limit_bytes=VMEM),
        cost_estimate=cost(10 + 13 * count),
        name="expert",
    )(z, *xs, *cs, wg, wu, wd, wr, *held, *others)


def gate_up_kernel(s_ref, x_ref, dgp_ref, dup_ref, glog_ref, other_ref, mine_ref, router_ref, xt_ref):
    @pl.when(pl.program_id(0) == 0)
    def _():
        xt_ref[...] = x_ref[...].T
        high = glog_ref[...].astype(bf16)
        low = (glog_ref[...] - high.astype(f32)).astype(bf16)
        router_ref[...] = dot(xt_ref[...], high) + dot(xt_ref[...], low)

    first = s_ref[0] == 0
    for n, ref in enumerate((dgp_ref, dup_ref)):
        result = dot(xt_ref[...], ref[...]).astype(bf16).reshape((other_ref.shape[0], 2) + other_ref.shape[2:])
        other_ref[:, n] = jnp.where(first, result[:, 1], result[:, 0])
        mine_ref[:, n] = jnp.where(first, result[:, 0], result[:, 1])


def gate_up_grads(side, chips, x, dgp, dup, glog, others=()):
    rows, width = x.shape
    hidden, wide = dgp.shape[1], 2 * TILE
    part = width // chips // 2
    tile = pl.BlockSpec((rows, wide), lambda f: (0, f))
    out = pl.BlockSpec((chips, 2, part, wide), lambda f: (0, 0, 0, f))
    shape = jax.ShapeDtypeStruct((chips, 2, part, hidden), bf16)
    return pl.pallas_call(
        behind(gate_up_kernel, 5, others),
        grid=(hidden // wide,),
        in_specs=[
            SMEM,
            pl.BlockSpec((rows, width), lambda f: (0, 0)),
            tile,
            tile,
            pl.BlockSpec((rows, TILE), lambda f: (0, 0)),
        ]
        + anywhere(others),
        out_specs=[out, out, pl.BlockSpec((width, TILE), lambda f: (0, 0))],
        out_shape=[shape, shape, jax.ShapeDtypeStruct((width, TILE), f32)],
        scratch_shapes=[pltpu.VMEM((width, rows), bf16)],
        compiler_params=pltpu.CompilerParams(vmem_limit_bytes=VMEM),
        cost_estimate=cost(24),
        name="gate_up_grads",
    )(side, x, dgp, dup, glog, *others)


def down_kernel(s_ref, act_ref, gcot_ref, other_ref, mine_ref, res_ref):
    res_ref[...] = dot(act_ref[...].T, gcot_ref[...]).astype(bf16).reshape(res_ref.shape)
    other_ref[...] = res_ref[:, 1 - s_ref[0]]
    mine_ref[...] = res_ref[:, s_ref[0]]


def down_grads(side, chips, act, gcot, others=()):
    rows, hidden = act.shape
    width, wide = gcot.shape[1], hidden // 2
    part = hidden // chips // 2
    out = pl.BlockSpec((chips // 2, part, width), lambda f: (f, 0, 0))
    shape = jax.ShapeDtypeStruct((chips, part, width), bf16)
    return pl.pallas_call(
        behind(down_kernel, 3, others),
        grid=(2,),
        in_specs=[SMEM, pl.BlockSpec((rows, wide), lambda f: (0, f)), pl.BlockSpec((rows, width), lambda f: (0, 0))]
        + anywhere(others),
        out_specs=[out, out],
        out_shape=[shape, shape],
        scratch_shapes=[pltpu.VMEM((chips // 2, 2, part, width), bf16)],
        compiler_params=pltpu.CompilerParams(vmem_limit_bytes=VMEM),
        cost_estimate=cost(14),
        name="down_grads",
    )(side, act, gcot, *others)


def out_kernel(act_ref, wd_ref, gate_ref, *refs):
    outs, acc_ref = refs[:-1], refs[-1]
    step = pl.program_id(0)
    more = dot(act_ref[...], wd_ref[0])

    @pl.when(step == 0)
    def _():
        acc_ref[...] = more

    @pl.when(step > 0)
    def _():
        acc_ref[...] += more

    @pl.when(step == pl.num_programs(0) - 1)
    def _():
        rows = outs[0].shape[0]
        for n, out in enumerate(outs):
            part = slice(n * rows, (n + 1) * rows)
            out[...] = (acc_ref[part, :] * gate_ref[part, :1]).astype(bf16)


def expert_out(act, wd, gate, chunks, others=()):
    rows, hidden = act.shape
    width, wide = wd.shape[2], hidden // 2
    fixed = lambda r, c: pl.BlockSpec((r, c), lambda f: (0, 0))
    return pl.pallas_call(
        behind(out_kernel, 3, others),
        grid=(hidden // wide,),
        in_specs=[
            pl.BlockSpec((rows, wide), lambda f: (0, f)),
            pl.BlockSpec((1, wide, width), lambda f: (0, f, 0)), fixed(rows, TILE),
        ] + anywhere(others),
        out_specs=[fixed(rows // chunks, width)] * chunks,
        out_shape=[jax.ShapeDtypeStruct((rows // chunks, width), bf16)] * chunks,
        scratch_shapes=[pltpu.VMEM((rows, width), f32)],
        compiler_params=pltpu.CompilerParams(vmem_limit_bytes=VMEM),
        cost_estimate=cost(14),
        name="expert_out",
    )(act, wd, gate, *others)


def norm_kernel(two_ref, one_ref, own_ref, gain_ref, out_ref):
    step = pl.program_id(0)

    def put(ref):
        x = ref[...].astype(f32)
        r = lax.rsqrt(jnp.mean(x * x, axis=-1, keepdims=True) + epsilon)
        out_ref[...] = (x * r * gain_ref[...][None]).astype(bf16)

    for n, ref in enumerate((two_ref, one_ref, own_ref)):
        pl.when(step // 2 == n)(functools.partial(put, ref))


def norm_window(two, one, own, gain):
    pieces, rows, width = own.shape
    some = pieces // 2
    at = lambda n: pl.BlockSpec((some, rows, width), lambda f: (jnp.clip(f - 2 * n, 0, 1), 0, 0))
    return pl.pallas_call(
        norm_kernel,
        grid=(6,),
        in_specs=[at(0), at(1), at(2), pl.BlockSpec((1, width), lambda f: (0, 0))],
        out_specs=pl.BlockSpec((some, rows, width), lambda f: (f, 0, 0)),
        out_shape=jax.ShapeDtypeStruct((3 * pieces, rows, width), bf16),
        compiler_params=pltpu.CompilerParams(vmem_limit_bytes=VMEM),
        cost_estimate=cost(5),
        name="norm_window",
    )(two, one, own, gain)


def turn_kernel(rows_ref, out_ref):
    out_ref[...] = rows_ref[0].T.reshape(out_ref.shape)


def turn_rows(normed, chips, others=()):
    pieces, rows, width = normed.shape
    part = width // chips // 2
    return pl.pallas_call(
        behind(turn_kernel, 1, others),
        grid=(pieces,),
        in_specs=[pl.BlockSpec((1, rows, width), lambda f: (f, 0, 0))] + anywhere(others),
        out_specs=pl.BlockSpec((chips, 2, part, rows), lambda f: (0, 0, 0, f)),
        out_shape=jax.ShapeDtypeStruct((chips, 2, part, pieces * rows), bf16),
        compiler_params=pltpu.CompilerParams(vmem_limit_bytes=VMEM),
        cost_estimate=cost(8),
        name="turn_rows",
    )(normed, *others)


def slot_rows(t_ref, k, slot):
    index = lax.broadcasted_iota(jnp.int32, (slot, t_ref.shape[1]), 0) + k * slot
    return ((index == t_ref[0:1, :]) | (index == t_ref[1:2, :])).astype(bf16)


def row_slots(t_ref, k, slot):
    index = lax.broadcasted_iota(jnp.int32, (t_ref.shape[0], slot), 1) + k * slot
    return ((index == t_ref[:, 0:1]) | (index == t_ref[:, 1:2])).astype(bf16)


def collect(t_ref, refs):
    total = None
    for k, ref in enumerate(refs):
        part = dot(row_slots(t_ref, k, ref.shape[0]), ref[...])
        total = part if total is None else total + part
    return total


def turned(ref, z):
    return jnp.concatenate([ref[z ^ k] for k in range(ref.shape[0])], axis=0)


def call(kernel, ins, outs, us, name, others=(), scratch=(), passed=()):
    specs = [SMEM if a.ndim == 1 else pl.BlockSpec(memory_space=pltpu.VMEM) for a in ins]
    first, last = len(ins), len(ins) + len(passed) + len(others)

    def body(*refs):
        kernel(*refs[:first], *refs[last : last + len(outs)], *refs[last + len(outs) + len(passed) :])

    return pl.pallas_call(
        body,
        in_specs=specs + anywhere(passed) + anywhere(others),
        out_specs=[pl.BlockSpec(memory_space=pltpu.VMEM)] * len(outs) + anywhere(passed),
        out_shape=[jax.ShapeDtypeStruct(shape, dtype) for shape, dtype in outs]
        + [jax.ShapeDtypeStruct(array.shape, array.dtype) for array in passed],
        input_output_aliases={first + i: len(outs) + i for i in range(len(passed))},
        scratch_shapes=list(scratch),
        compiler_params=pltpu.CompilerParams(vmem_limit_bytes=VMEM),
        cost_estimate=cost(us),
        name=name,
    )(*ins, *passed, *others)


def pair_kernel(mine_ref, other_ref, out_ref):
    out_ref[...] = (mine_ref[...].astype(f32) + other_ref[...].astype(f32)).astype(bf16)


def pair_sum(mine, other, others=()):
    block = pl.BlockSpec((1,) + mine.shape[1:], lambda f: (f,) + (0,) * (mine.ndim - 1))
    return pl.pallas_call(
        behind(pair_kernel, 2, others),
        grid=mine.shape[:1],
        in_specs=[block, block] + anywhere(others),
        out_specs=block,
        out_shape=jax.ShapeDtypeStruct(mine.shape, bf16),
        compiler_params=pltpu.CompilerParams(vmem_limit_bytes=VMEM),
        cost_estimate=cost(6),
        name="pair_sum",
    )(mine, other, *others)


def cot_kernel(ks, slot, z_ref, t_ref, cot_ref, *outs):
    values = turned(cot_ref, z_ref[0])
    for k, out in zip(ks, outs):
        out[...] = dot(slot_rows(t_ref, k, slot), values).astype(bf16)


def rows_kernel(ks, slot, t_ref, value_ref, *outs):
    for k, out in zip(ks, outs):
        out[...] = dot(slot_rows(t_ref, k, slot), value_ref[...]).astype(bf16)


def hidden_kernel(ks, slot, z_ref, t_ref, tok_ref, w_ref, gain_ref, *refs):
    pieces = tok_ref.shape[0]
    context, hidden_ref, moe_ref, outs = refs[:pieces], refs[pieces], refs[pieces + 1], refs[pieces + 2 :]
    left = jnp.concatenate([ref[...] for ref in context], axis=0)
    hidden = turned(tok_ref, z_ref[0]).astype(f32) + dot(left, w_ref[...])
    hidden_ref[...] = hidden
    moe_in = norm_rows(hidden, gain_ref[...]).astype(bf16)
    moe_ref[...] = moe_in
    for k, out in zip(ks, outs):
        out[...] = dot(slot_rows(t_ref, k, slot), moe_in).astype(bf16)


def middle_kernel(z_ref, t_ref, hidden_ref, cot_ref, w_ref, gain_ref, *refs):
    pieces = cot_ref.shape[0]
    grad_ref, attn_ref, gain_grad_ref, outs = refs[pieces], refs[pieces + 1], refs[pieces + 2], refs[pieces + 3 :]
    grad_moe = collect(t_ref, refs[:pieces])
    grad_norm, gain_grad = norm_back(hidden_ref[...], gain_ref[...], grad_moe)
    gain_grad_ref[...] = gain_grad[None]
    grad = turned(cot_ref, z_ref[0]).astype(f32) + grad_norm
    grad_ref[...] = grad
    low = grad.astype(bf16)
    attn_ref[...] = low
    context = dot_nt(low, w_ref[...]).astype(bf16)
    rows = context.shape[0] // pieces
    for k in range(pieces):
        outs[k][...] = context[k * rows : (k + 1) * rows]


def mix_kernel(z_ref, t_ref, hidden_ref, *refs):
    out_ref = refs[-1]
    rows = out_ref.shape[1]
    mixed = (hidden_ref[...] + collect(t_ref, refs[:-1])).astype(bf16)
    for k in range(out_ref.shape[0]):
        out_ref[z_ref[0] ^ k] = mixed[k * rows : (k + 1) * rows]


def inputs_kernel(last, dq_ref, dk_ref, dv_ref, wq_ref, wk_ref, wv_ref, *refs):
    step = pl.program_id(0)
    flat = lambda ref: ref[...].reshape(-1, ref.shape[-1])
    grad = dot_nt(flat(dk_ref), wk_ref[...]) + dot_nt(flat(dv_ref), wv_ref[...])
    if not last:
        refs[0][...] = grad

        @pl.when(step == 2)
        def _():
            refs[0][...] = grad + dot_nt(flat(dq_ref), wq_ref[...])

        return
    acc_ref, two_ref, one_ref, own_ref = refs
    grad = grad + acc_ref[...]

    @pl.when(step == 0)
    def _():
        two_ref[...] = grad.astype(bf16)

    @pl.when(step == 1)
    def _():
        one_ref[...] = grad.astype(bf16)

    @pl.when(step == 2)
    def _():
        own_ref[...] = grad + dot_nt(flat(dq_ref), wq_ref[...])


def input_grads(part, dq, dk, dv, wq, wk, wv, acc=None, others=()):
    pieces, rows, some = dq.shape
    width = wq.shape[0]
    block = pieces * rows
    window = pl.BlockSpec((pieces, rows, some), lambda f: (f, 0, 0))
    weight = pl.BlockSpec((width, some), lambda f: (0, part))
    once = pl.BlockSpec((block, width), lambda f: (0, 0))
    step = pl.BlockSpec((block, width), lambda f: (f, 0))
    specs = [pl.BlockSpec((pieces, rows, some), lambda f: (0, 0, 0)), window, window, weight, weight, weight]
    ins, outs = [dq, dk, dv, wq, wk, wv], [(step, (3 * block, width), f32)]
    if acc is not None:
        specs += [step]
        ins += [acc]
        outs = [(once, (block, width), bf16)] * 2 + [(once, (block, width), f32)]
    return pl.pallas_call(
        behind(functools.partial(inputs_kernel, acc is not None), len(ins), others),
        grid=(3,),
        in_specs=specs + anywhere(others),
        out_specs=[o[0] for o in outs],
        out_shape=[jax.ShapeDtypeStruct(o[1], o[2]) for o in outs],
        compiler_params=pltpu.CompilerParams(vmem_limit_bytes=VMEM),
        cost_estimate=cost(7),
        name="input_grads",
    )(*ins, *others)


def leave_kernel(s_ref, z_ref, two_ref, swapped_ref, parts_ref, leave_ref, keep_ref, *refs):
    outs, total_ref = refs[:-1], refs[-1]
    zero = jnp.zeros_like(swapped_ref)
    swapped = swapped_ref[...]
    add = jnp.where(s_ref[0] == 0, zero, swapped)
    leave_ref[...] = (two_ref[...].astype(f32) + add.astype(f32)).astype(bf16)
    keep_ref[...] = jnp.where(s_ref[0] == 0, swapped, zero)
    total = parts_ref[0].astype(f32)
    for i in range(1, parts_ref.shape[0]):
        total = total + parts_ref[i].astype(f32)
    total_ref[...] = total.astype(bf16).reshape(total_ref.shape)
    for k, out in enumerate(outs):
        out[...] = total_ref[z_ref[0] ^ k]


def tail_kernel(z_ref, x_ref, sum_ref, swapped_ref, gain_ref, came_ref, *refs):
    pieces, rows, width = x_ref.shape
    blocks, outs, total_ref = refs[0], refs[1:-1], refs[-1]
    total = blocks[0].astype(f32)
    for i in range(1, blocks.shape[0]):
        total = total + blocks[i].astype(f32)
    total_ref[...] = total.astype(bf16).reshape(total_ref.shape)
    share, long = total_ref.shape[1:]
    for k in range(pieces):
        part = slice(k * rows, (k + 1) * rows)
        grad = sum_ref[part, :] + swapped_ref[part, :].astype(f32) + came_ref[part, :].astype(f32)
        outs[k][:rows, :] = norm_back(x_ref[k].astype(f32), gain_ref[...], grad)[0].astype(bf16)
        theirs = total_ref[z_ref[0] ^ k]
        outs[k][rows : rows + share, :] = theirs[:, :width]
        outs[k][rows + share :, : long - width] = theirs[:, width:]
        outs[k][rows + share :, long - width :] = jnp.zeros((share, 2 * width - long), bf16)


def end_kernel(z_ref, grad_ref, wq_ref, wk_ref, wv_ref, gain_ref, *refs):
    outs = refs[-7:]
    pieces, rows, width = outs[0].shape
    share, long = refs[pieces].shape
    half = (long - width) // 3
    first = refs[pieces][...].astype(f32)
    for k in range(1, pieces):
        first = first + refs[pieces + k][...].astype(f32)
    outs[6][...] = first[:, 3 * half :]
    total = None
    for k in range(pieces):
        outs[0][z_ref[0] ^ k] = (grad_ref[k * rows : (k + 1) * rows, :] + refs[k][:rows, :].astype(f32)).astype(bf16)
        part = jnp.concatenate([refs[k][rows : rows + share, :], refs[k][rows + share :, :]], axis=1).astype(f32)
        total = part if total is None else total + part
    gain = jnp.zeros((share, 1), f32)
    for i, weight in enumerate((wq_ref, wk_ref, wv_ref)):
        parts = (first[:, i * half : (i + 1) * half], total[:, i * half : (i + 1) * half])
        for n, part in enumerate(parts):
            columns = slice(n * half, (n + 1) * half)
            outs[1 + i][:, columns] = part
            gain = gain + jnp.sum(part * weight[:, columns].astype(f32), axis=1, keepdims=True)
    outs[4][...] = total[:, 3 * half : 3 * half + outs[4].shape[1]]
    outs[5][...] = gain / gain_ref[...]


def projection_kernel(third, small, pieces, s_ref, nt_ref, dq_ref, dk_ref, dv_ref, *refs):
    other_ref, mine_ref = refs[small + pieces + (pieces > 0) :][:2]
    step = pl.program_id(0)
    keys = nt_ref.shape[3]
    own = dq_ref.shape[0]

    def put(grad_ref, first):
        for where, ref in ((1 - s_ref[0], other_ref), (s_ref[0], mine_ref)):
            left = nt_ref[:, where, :, first:].reshape(-1, keys - first)
            ref[...] = dot(left, grad_ref[...]).astype(bf16).reshape(ref.shape)

    @pl.when(step < third)
    def _():
        put(dq_ref, keys - own)

    @pl.when((step >= third) & (step < 2 * third))
    def _():
        put(dk_ref, 0)

    @pl.when((step >= 2 * third) & (step < 3 * third))
    def _():
        put(dv_ref, 0)

    if pieces:
        turned_ref, context, attn_ref = refs[-1], refs[:pieces], refs[pieces]
        count = context[0].shape[0]

        @pl.when(step == 3 * third)
        def _():
            for k in range(pieces):
                turned_ref[:, :, :, k * count : (k + 1) * count] = context[k][...].T.reshape(turned_ref.shape[:3] + (count,))

        @pl.when(step >= 3 * third)
        def _():
            for where, ref in ((1 - s_ref[0], other_ref), (s_ref[0], mine_ref)):
                left = turned_ref[:, where].reshape(-1, pieces * count)
                ref[...] = dot(left, attn_ref[...]).astype(bf16).reshape(ref.shape)

    if small:

        @pl.when(step == 3 * third)
        def _():
            other_ref[...] = refs[0][:, 1 - s_ref[0]]
            mine_ref[...] = refs[0][:, s_ref[0]]


def projection_grads(side, normed_t, dq, dk, dv, small=(), context=(), attn=(), others=()):
    chips, _, rows, keys = normed_t.shape
    own, width = dq.shape
    wide = 2 * TILE
    third = width // wide
    at = lambda j: (lambda f: (0, jnp.clip(f - j * third, 0, third - 1)))
    fixed = lambda array: pl.BlockSpec(array.shape, lambda f: (0,) * array.ndim)
    more = len(small) + sum(array.shape[1] // wide for array in attn)
    out = pl.BlockSpec((chips, rows, wide), lambda f: (0, 0, f))
    shape = jax.ShapeDtypeStruct((chips, rows, 3 * width + wide * more), bf16)
    ins = [side, normed_t, dq, dk, dv, *small, *context, *attn]
    scratch = [pltpu.VMEM((chips, 2, rows, len(context) * array.shape[0]), bf16) for array in context[:1]]
    return pl.pallas_call(
        behind(functools.partial(projection_kernel, third, len(small), len(context)), len(ins), others),
        grid=(3 * third + more,),
        in_specs=[
            SMEM,
            fixed(normed_t),
            pl.BlockSpec((own, wide), at(0)),
            pl.BlockSpec((keys, wide), at(1)),
            pl.BlockSpec((keys, wide), at(2)),
        ]
        + [fixed(array) for array in [*small, *context]]
        + [pl.BlockSpec((array.shape[0], wide), lambda f: (0, jnp.maximum(f - 3 * third, 0))) for array in attn]
        + anywhere(others),
        out_specs=[out, out],
        out_shape=[shape, shape],
        scratch_shapes=scratch,
        compiler_params=pltpu.CompilerParams(vmem_limit_bytes=VMEM),
        cost_estimate=cost(9.3 + more),
        name="projection_grads",
    )(*ins, *others)


def shift(x, by):
    count = lax.axis_size("ctx")
    return lax.ppermute(x, "ctx", [(i, i + by) for i in range(count) if 0 <= i + by < count])


def core_swap(x):
    return lax.ppermute(x, "ctx", [(i, i ^ 1) for i in range(lax.axis_size("ctx"))])


def z_swap(x, k):
    if k == 0:
        return x
    return lax.ppermute(x, "exp", [(i, i ^ k) for i in range(lax.axis_size("exp"))])


def over_chips(pair):
    count = lax.axis_size("ctx")
    groups = [list(range(core, count, 2)) for core in range(2)]
    return lax.all_to_all(pair, "ctx", split_axis=0, concat_axis=0, tiled=True, axis_index_groups=groups)


def summed(parts):
    return jnp.sum(parts.astype(f32), axis=0)


def add_pair(mine, other):
    return (mine.astype(f32) + core_swap(other).astype(f32)).astype(bf16)


def norm_rows(values, gain):
    return values * lax.rsqrt(jnp.mean(values * values, axis=-1, keepdims=True) + epsilon) * gain


def norm_back(values, gain, grad):
    r = lax.rsqrt(jnp.mean(values * values, axis=-1, keepdims=True) + epsilon)
    u = grad * gain
    inner = jnp.mean(values * u, axis=-1, keepdims=True)
    return r * u - values * (r * r * r) * inner, jnp.sum(grad * values * r, axis=0)


def on_device(
    tokens, doc_lengths, routes, priority, norm1_gain, w_query, w_key, w_value, w_out, bias_table,
    norm2_gain, w_router, w_gate, w_up, w_down, cotangent,
):
    seqs, piece_len, width = tokens.shape
    exp_count = lax.axis_size("exp")
    ctx_count = lax.axis_size("ctx")
    device_count = exp_count * ctx_count
    block_len = piece_len * exp_count
    rows = seqs * piece_len
    heads = bias_table.shape[0] // bucket_total
    experts = w_router.shape[1]
    slot = 5 * rows // (2 * experts)
    slots = experts * slot
    ctx = lax.axis_index("ctx")
    exp = lax.axis_index("exp")
    side = ctx % 2

    z = jnp.reshape(exp, (1,))
    far_first = [2, 3, 1]

    turn = jnp.arange(seqs, dtype=jnp.int32) ^ exp
    pick = lambda array, k: lax.dynamic_index_in_dim(array, exp ^ k, 0, keepdims=False)

    x_own = [None] * seqs
    for k in [0, 2, 3, 1]:
        x_own[k] = z_swap(pick(tokens, k), k)
    x_pieces = x_own
    x_two = [shift(piece, 2) for piece in x_own]
    x_own, x_two = jnp.stack(x_own), jnp.stack(x_two)
    x_one = core_swap(jnp.where(side == 0, x_own, x_two))

    route_rows = jnp.take(routes, turn, axis=0).reshape(rows, 2)
    order = jnp.take(priority, turn, axis=0).reshape(rows)
    earlier = order[None, :] < order[:, None]
    r0, r1 = route_rows[:, 0], route_rows[:, 1]
    place0 = jnp.sum((earlier & (r0[None, :] == r0[:, None])).astype(jnp.int32), axis=1)
    place1 = jnp.sum((earlier & (r1[None, :] == r1[:, None])).astype(jnp.int32), axis=1) + jnp.sum(
        (r0[None, :] == r1[:, None]).astype(jnp.int32), axis=1
    )
    target0 = jnp.where(place0 < slot, (r0 ^ exp) * slot + place0, -1)
    target1 = jnp.where(place1 < slot, (r1 ^ exp) * slot + place1, -1)
    targets = jnp.stack([target0, target1])
    targets_t = targets.T
    slot_shape = ((slot, width), bf16)
    sent = call(
        functools.partial(cot_kernel, far_first + [0], slot), [z, targets, cotangent], [slot_shape] * experts, 4, "cot_rows", x_pieces[1:]
    )
    cot_slots = [None] * experts
    for k, rows_k in zip(far_first + [0], sent):
        cot_slots[k] = z_swap(rows_k, k)

    distance = np.arange(-TILE, WINDOW + TILE)
    seen = (distance >= 0) & (distance < WINDOW)
    hot = (bucket_of(np.clip(distance, 0, None))[None, :] == np.arange(bucket_total)[:, None]) & seen[None, :]
    vec = exact_dot(bias_table.astype(f32).reshape(heads, bucket_total), jnp.asarray(hot, f32))
    vec = jnp.where(jnp.asarray(seen)[None, :], vec, NEG).reshape(heads // 2, 2, -1)
    bias = bias_tiles(vec, sent[:1])

    ends = jnp.cumsum(lax.dynamic_index_in_dim(doc_lengths, exp, 0, keepdims=False))
    piece_start = ctx * block_len + turn[:, None] * piece_len
    q_pos = piece_start + jnp.arange(piece_len, dtype=jnp.int32)[None, :]
    start = jnp.max(jnp.where(ends <= q_pos[..., None], ends, 0), axis=2)
    lo = start - (ctx - 2) * block_len
    lo = jnp.broadcast_to(lo[:, None, None, :], (seqs, 1, 2, TILE)).reshape(seqs, 1, 2 * TILE)

    gain_one = norm1_gain.astype(f32)
    normed_pieces = norm_window(x_two, x_one, x_own, gain_one[None])
    normed = normed_pieces.reshape(-1, width)
    normed_own = normed[2 * block_len :]
    q = (dot(normed_own, w_query).astype(bf16) * 0.125).astype(bf16).reshape(seqs, piece_len, width)
    k_win = dot(normed, w_key).astype(bf16).reshape(-1, TILE, width)
    v_win = dot(normed, w_value).astype(bf16).reshape(-1, TILE, width)
    contexts, lses, context_rows = [None] * seqs, [], [None] * seqs
    for first in (2, 0):
        others = [contexts[2], cot_slots[2]] if first == 0 else []
        *c, l = attend((first, first + 1), z, lo[first : first + 2], q[first : first + 2], k_win, v_win, bias, others)
        lses.insert(0, l)
        for k in (first, first + 1):
            contexts[k] = c[k - first]
            context_rows[k] = z_swap(contexts[k], k)
    normed_t = turn_rows(normed_pieces, ctx_count // 2, contexts[:1])
    router_wide = jnp.pad(w_router, ((0, 0), (0, TILE - experts)))
    gain_two = norm2_gain.astype(f32)[None]
    hidden, moe_in, *sent = call(
        functools.partial(hidden_kernel, [2, 0], slot),
        [z, targets, tokens, w_out, gain_two] + context_rows,
        [((rows, width), f32), ((rows, width), bf16), slot_shape, slot_shape], 9, "hidden_rows", [cot_slots[1], cot_slots[3], normed_t],
    )
    inputs = [sent[1], None, z_swap(sent[0], 2), None]
    held, returned, turns = None, [None] * experts, [0, 2, 1, 3]
    for ks, index in (([0], 0), ([2], 1), ([1], 2), ([3], 3)):
        found = expert(
            index, experts, held, z, [inputs[k] for k in ks], [cot_slots[k] for k in ks], w_gate, w_up, w_down, router_wide, experts
        )
        back, held = found[: len(ks)], found[len(ks) :]
        for k, rows_k in zip(ks, back):
            returned[k] = z_swap(rows_k, k)
        if index == 0:
            sent = call(functools.partial(rows_kernel, [3, 1], slot), [targets, moe_in], [slot_shape] * 2, 3, "moe_rows", back)
            inputs[3], inputs[1] = z_swap(sent[0], 3), z_swap(sent[1], 1)
    all_inputs, act_low, grad_gate_pre, grad_up_pre, grad_out_slots, gate, grad_logits = held
    chips = ctx_count // 2
    side_ref = jnp.reshape(side, (1,))
    produced = expert_out(act_low, w_down, gate, experts, [returned[2]])
    down_other, down_mine = down_grads(side_ref, chips, act_low, grad_out_slots, produced[:1])

    part_count = 2
    part_width = width // part_count
    grad_hidden, grad_attn, grad_gain_two, *sent_back = call(
        middle_kernel, [z, targets_t, hidden, cotangent, w_out, gain_two] + returned,
        [((rows, width), f32), ((rows, width), bf16), ((1, width), f32)] + [((piece_len, width), bf16)] * seqs,
        9, "middle_rows", [down_other],
    )
    arrived = [z_swap(sent_back[k], k) for k in range(seqs)]
    other, mine, router_part = gate_up_grads(
        side_ref, chips, all_inputs, grad_gate_pre, grad_up_pre, grad_logits, sent_back[-1:]
    )
    grad_router_part = router_part[:, :experts]
    pair = pair_sum(mine, core_swap(other))
    both = over_chips(pair)
    down_other = core_swap(down_other)
    given = [z_swap(produced[turns.index(k)], k) for k in range(experts)]

    weights = (w_query, w_key, w_value)
    flat = lambda grads: [grad.reshape(-1, part_width) for grad in grads]
    back = lambda n, others: attend_back(n, part_count, z, lo, lses, q, k_win, v_win, bias, contexts, arrived, others)
    *grads, diagonal = back(0, [pair])
    other, mine = projection_grads(
        side_ref, normed_t, *flat(grads), context=context_rows, attn=[grad_attn], others=[given[2], given[1]]
    )
    first_pair = add_pair(mine, other)
    first_parts = over_chips(first_pair)
    acc = input_grads(0, *grads, *weights, others=[other])[0]
    down_pair = pair_sum(down_mine, down_other)
    *grads, more = back(1, [acc, first_pair, both, down_pair])
    diagonals = jnp.concatenate([diagonal, more])
    places = np.arange((TILES_SEEN) * 2 * TILE).reshape(TILES_SEEN, 2 * TILE)
    block, lane = places // (2 * TILE), places % (2 * TILE)
    where_dist = lane - TILE + (TILES_SEEN - 1 - block) * TILE
    ok = (where_dist >= 0) & (where_dist < WINDOW)
    to_bucket = (bucket_of(np.clip(where_dist, 0, None))[..., None] == np.arange(bucket_total)) & ok[..., None]
    table_part = exact_dot(diagonals.reshape(heads, -1), jnp.asarray(to_bucket.reshape(-1, bucket_total), f32))
    share, table_share = width // device_count, heads * bucket_total // device_count
    table_rows = jnp.pad(table_part.reshape(device_count, table_share), ((0, 0), (0, share - table_share)))
    packed = jnp.concatenate([grad_gain_two.reshape(width, 1), grad_router_part, table_rows.reshape(width, 1)], axis=1)
    packed = jnp.pad(packed.astype(bf16), ((0, 0), (0, 2 * TILE - packed.shape[1])))
    packed = packed.reshape(ctx_count // 2, 2, -1, 2 * TILE)
    other, mine = projection_grads(side_ref, normed_t, *flat(grads), small=[packed], others=[first_parts, given[3]])
    pair = add_pair(mine, other)
    last = over_chips(pair)
    part_two, part_one, own_sum = input_grads(1, *grads, *weights, acc, [pair])
    leave, swapped, *first, down_pair = call(
        leave_kernel, [side_ref, z, part_two, core_swap(part_one), first_parts],
        [((block_len, width), bf16)] * 2 + [((share, first_parts.shape[-1]), bf16)] * seqs, 5, "leaving_rows", [last],
        [pltpu.VMEM((exp_count, share, first_parts.shape[-1]), bf16)], [down_pair],
    )
    first = [z_swap(piece, k) for k, piece in enumerate(first)]
    came = shift(leave, -2)
    down = over_chips(down_pair)
    mixed = call(
        mix_kernel, [z, targets_t, hidden] + given, [((seqs, piece_len, width), bf16)], 8, "mixed_rows", [leave]
    )[0]
    share = width // device_count
    long = pair.shape[-1]
    pieces = call(
        tail_kernel, [z, x_own, own_sum, swapped, gain_one[None], came, last],
        [((piece_len + 2 * share, width), bf16)] * seqs, 8, "tail_rows", [mixed] + first[1:],
        [pltpu.VMEM((exp_count, share, long), bf16)],
    )
    pieces = [z_swap(piece, k) for k, piece in enumerate(pieces)]
    grad_gate, grad_up, grad_down = summed(both[:, 0]), summed(both[:, 1]), summed(down)
    own_rows = lambda array: lax.dynamic_slice_in_dim(array, (ctx * exp_count + exp) * share, share, 0)
    grad_tokens, grad_query, grad_key, grad_value, packed, norm1_out, grad_out = call(
        end_kernel,
        [z, grad_hidden] + [own_rows(array) for array in weights] + [own_rows(gain_one[:, None])] + pieces + first,
        [((seqs, piece_len, width), bf16)] + [((share, width), f32)] * 3 + [((share, 2 * TILE), f32), ((share, 1), f32)]
        + [((share, width), f32)],
        6, "end_rows", [grad_down],
    )
    norm1_out, norm2_out = norm1_out[:, 0], packed[:, 0]
    router_out, table_out = packed[:, 1 : 1 + experts], packed[:table_share, 1 + experts]
    return (
        mixed, grad_tokens, norm1_out, grad_query, grad_key, grad_value, grad_out, table_out, norm2_out,
        router_out.reshape(-1, experts), grad_gate[None], grad_up[None], grad_down[None],
    )


def solution(mesh):
    rows = P(None, ("ctx", "exp"), None)
    flat = P(("ctx", "exp"))
    in_specs = (
        rows, P(), rows, P(None, ("ctx", "exp")), P(), P(), P(), P(), P(), P(), P(), P(),
        P("exp", None, None), P("exp", None, None), P("exp", None, None), rows,
    )
    out_specs = (
        rows, rows, flat, P(("ctx", "exp"), None), P(("ctx", "exp"), None), P(("ctx", "exp"), None),
        P(("ctx", "exp"), None), flat, flat, P(("ctx", "exp"), None),
        P("exp", "ctx", None), P("exp", "ctx", None), P("exp", "ctx", None),
    )
    return jax.shard_map(on_device, mesh=mesh, in_specs=in_specs, out_specs=out_specs, check_vma=False)
```
